32 devices in a mesh: req: 2 (over x), mlp: 16 (over z, y, core).
Axes of the slice: x: 2, y: 2, z: 4, core: 2. Of those that a mesh axis runs over, the one named last changes fastest.
Arguments:
- tokens: bfloat16 [2048, 4096], P(('req', 'mlp')), may hold values from -6 to 6
- layer_norm_gain: float32 [4096], replicated, may hold values from 0.1 to 1.9
- layer_norm_bias: float32 [4096], replicated, may hold values from -2 to 2
- query_key_weight: bfloat16 [4096, 16, 768], P(None, 'mlp')
- output_weight: bfloat16 [16, 256, 4096], P('mlp'), may hold values from -0.09375 to 0.09375
- up_weight: bfloat16 [4096, 8192], P(None, 'mlp'), may hold values from -0.09375 to 0.09375
- input_bias: float32 [8192], P('mlp'), may hold values from -3 to 3
- down_weight: bfloat16 [8192, 4096], P('mlp'), may hold values from -0.0625 to 0.0625
- output_bias: float32 [4096], replicated, may hold values from -2 to 2
- input_adapter_left: bfloat16 [4096, 2048], P(None, 'mlp'), may hold values from -0.09375 to 0.09375
- query_key_value_right: bfloat16 [1024, 16, 768], P(None, 'mlp'), may hold values from -1.5 to 1.5
- up_adapter_right: bfloat16 [1024, 8192], P(None, 'mlp'), may hold values from -1.5 to 1.5
- output_adapter_left: bfloat16 [16, 256, 1024], P('mlp'), may hold values from -0.09375 to 0.09375
- down_adapter_left: bfloat16 [8192, 1024], P('mlp'), may hold values from -0.0625 to 0.0625
- output_adapter_right: bfloat16 [2048, 4096], P('mlp'), may hold values from -1 to 1
- lengths: int32 [65], replicated, may hold values from 8 to 1024, as said below
- request_adapter: int32 [65], replicated, may hold values from 0 to 63
- slot_adapter: int32 [64], P('mlp'), may hold values from 0 to 63, each once
Outputs:
- mixed: bfloat16 [2048, 4096], P(('req', 'mlp'))
The draws below stay inside these ranges and needn't reach their ends.
Inputs may be any that keep to these rules, and one draw needn't show every extreme that they name: `lengths`: one request holds exactly 1024 tokens, every other one 8 to 24; together they hold 2048 tokens. `slot_adapter`: every adapter id stands in exactly one slot.
All inputs are finite; a program needn't handle non-finite values.
Results may differ from the reference program's by a relative error of at most 0.017.
Values may be sent and summed in bfloat16 or wider, within the bound.
No kernel may reach another device: no remote copies, remote signals or barrier semaphores. Data moves between devices by JAX's collectives and lax.ppermute only.
A program may use at most 128 MiB of HBM per device.

```python
import math
import jax
import jax.numpy as jnp
import numpy as np
from jax import lax

MODEL_DIM = 4096
ATTENTION_HEADS = 16
HEAD_SIZE = 256
ROT = 64
FEEDFORWARD = 8192
ADAPTER_RANK = 16
TOK_DEV = 64
TOKENS = 2048
LONG = 1024
SHORTS = 64
REQS = 65
ADAPTER_COUNT = 64


def draw_query_key_weight(key, part):
    weights = jax.random.normal(key, (MODEL_DIM, ATTENTION_HEADS, 3 * HEAD_SIZE), jnp.float32) * MODEL_DIM ** (-0.5)
    return weights.astype(jnp.bfloat16)


def draw_lengths(key, part):
    key_first = jax.random.fold_in(key, 11)
    key_second = jax.random.fold_in(key, 12)
    key_third = jax.random.fold_in(key, 13)
    offset = jax.random.randint(key_first, (SHORTS // 2,), -8, 9)
    offset = offset.at[0].set(8)
    shorts = jnp.concatenate([16 + offset, 16 - offset]).astype(jnp.int32)
    shuffle = jax.random.permutation(key_second, SHORTS)
    shorts = shorts[shuffle]
    long_slot = jax.random.randint(key_third, (), 0, REQS)
    slot_index = jnp.arange(REQS, dtype=jnp.int32)
    before = shorts[jnp.clip(slot_index, 0, SHORTS - 1)]
    after_value = shorts[jnp.clip(slot_index - 1, 0, SHORTS - 1)]
    return jnp.where(slot_index < long_slot, before, jnp.where(slot_index == long_slot, LONG, after_value)).astype(jnp.int32)


def touch_ends(entries, own_key, low, top_value):
    longest = entries.shape.index(max(entries.shape))
    spots = []
    for shift in (0, 1):
        where = [jax.random.randint(jax.random.fold_in(own_key, axis), (), 0, length) for axis, length in enumerate(entries.shape)]
        where[longest] = (where[longest] + shift) % entries.shape[longest]
        spots.append(tuple(where))
    return entries.at[spots[0]].set(low).at[spots[1]].set(top_value)


def block_levels(stream_key, extent, cuts, low, top_value):
    def one(dim, blocks):
        draws = jax.random.uniform(jax.random.fold_in(jax.random.fold_in(stream_key, 6), dim), (blocks,), jnp.float32, low / len(cuts), top_value / len(cuts))
        return jnp.repeat(jnp.exp(draws), extent[dim] // blocks).reshape((-1,) + (1,) * (len(extent) - dim - 1))

    factor_of = one(*cuts[0])
    for cut in cuts[1:]:
        factor_of = factor_of * one(*cut)
    return factor_of


def rank_bounds(count, lean):
    weights = [(1 << 20) // math.isqrt(rank ** lean) + 1 for rank in range(1, count + 1)]
    scale = 1 + sum(weights) // (1 << 30)
    return np.cumsum(np.array([max(1, weight // scale) for weight in weights]))


def skewed_ids(key, dims, amount, slope):
    table = rank_bounds(amount, slope)
    lot = jax.random.randint(jax.random.fold_in(key, 1), dims, 0, int(table[amount - 1]))
    standing = jnp.searchsorted(jnp.asarray(table, jnp.int32), lot, side="right")
    return jax.random.permutation(jax.random.fold_in(key, 2), amount)[standing].astype(jnp.int32)


def scatter_about(rng, shape, width, reach, split=(), held_as=jnp.bfloat16):
    loudness = block_levels(rng, shape, split, -0.22, 0.18) if split else 1.0
    values = jax.random.normal(rng, shape, jnp.float32) * width * loudness
    return jnp.minimum(jnp.maximum(values, -reach), reach).astype(held_as)


def setup_inputs(seed: int = 0) -> dict:
    seeds = jax.random.split(jax.random.key(seed), 19)
    return {
        "tokens": scatter_about(seeds[0], (TOKENS, MODEL_DIM), 1.0, 6.0, ((0, 32),)),
        "layer_norm_gain": jnp.clip(1.0 + 0.18 * jax.random.normal(seeds[1], (MODEL_DIM,), jnp.float32), 0.1, 1.9),
        "layer_norm_bias": scatter_about(seeds[2], (MODEL_DIM,), 0.3, 2.0, (), jnp.float32),
        "query_key_weight": draw_query_key_weight(jax.random.fold_in(seeds[18], 71), 0),
        "output_weight": scatter_about(seeds[4], (ATTENTION_HEADS, HEAD_SIZE, MODEL_DIM), MODEL_DIM ** -0.5, 0.09375, ((0, 16),)),
        "up_weight": scatter_about(seeds[5], (MODEL_DIM, FEEDFORWARD), MODEL_DIM ** -0.5, 0.09375, ((1, 16),)),
        "input_bias": scatter_about(seeds[6], (FEEDFORWARD,), 0.5, 3.0, ((0, 16),), jnp.float32),
        "down_weight": scatter_about(seeds[7], (FEEDFORWARD, MODEL_DIM), FEEDFORWARD ** -0.5, 0.0625, ((0, 16),)),
        "output_bias": scatter_about(seeds[8], (MODEL_DIM,), 0.3, 2.0, (), jnp.float32),
        "input_adapter_left": scatter_about(seeds[9], (MODEL_DIM, ADAPTER_COUNT * 2 * ADAPTER_RANK), MODEL_DIM ** -0.5, 0.09375, ((1, 16),)),
        "query_key_value_right": scatter_about(seeds[10], (ADAPTER_COUNT * ADAPTER_RANK, ATTENTION_HEADS, 3 * HEAD_SIZE), ADAPTER_RANK ** -0.5, 1.5, ((1, 16),)),
        "up_adapter_right": scatter_about(seeds[11], (ADAPTER_COUNT * ADAPTER_RANK, FEEDFORWARD), ADAPTER_RANK ** -0.5, 1.5, ((1, 16),)),
        "output_adapter_left": scatter_about(seeds[12], (ATTENTION_HEADS, HEAD_SIZE, ADAPTER_COUNT * ADAPTER_RANK), MODEL_DIM ** -0.5, 0.09375, ((0, 16),)),
        "down_adapter_left": scatter_about(seeds[13], (FEEDFORWARD, ADAPTER_COUNT * ADAPTER_RANK), FEEDFORWARD ** -0.5, 0.0625, ((0, 16),)),
        "output_adapter_right": scatter_about(seeds[14], (ADAPTER_COUNT * 2 * ADAPTER_RANK, MODEL_DIM), (2 * ADAPTER_RANK) ** -0.5, 1.0, ((0, 16),)),
        "lengths": draw_lengths(jax.random.fold_in(seeds[18], 71), 0),
        "request_adapter": touch_ends(skewed_ids(seeds[16], (REQS,), ADAPTER_COUNT, 2), jax.random.fold_in(seeds[16], 3), 0, ADAPTER_COUNT - 1).astype(jnp.int32),
        "slot_adapter": jax.random.permutation(seeds[17], ADAPTER_COUNT).astype(jnp.int32),
    }


EPSILON = 1e-05
NEGATIVE_FILL = -1e+30

def rank_product(left_side, right_side):
    return jnp.dot(left_side, right_side, preferred_element_type=jnp.float32)

def normalize(inputs, layer_norm_gain, layer_norm_bias):
    values = inputs.astype(jnp.float32)
    center = values - lax.optimization_barrier(jnp.mean(values, axis=1, keepdims=True))
    spread = lax.optimization_barrier(jnp.mean(center * center, axis=1, keepdims=True))
    scaled = center * lax.rsqrt(spread + EPSILON)
    return (scaled * layer_norm_gain + layer_norm_bias).astype(jnp.bfloat16)

def token_info(lengths, request_adapter, first_row, row_count):
    endings = jnp.cumsum(lengths).astype(jnp.int32)
    anchors = (endings - lengths).astype(jnp.int32)
    token_index = (first_row + lax.iota(jnp.int32, row_count)).astype(jnp.int32)
    inside = anchors[None, :] <= token_index[:, None]
    request = (lax.optimization_barrier(jnp.sum(inside.astype(jnp.int32), axis=1)) - 1).astype(jnp.int32)
    request_start = lax.optimization_barrier(jnp.max(jnp.where(inside, anchors[None, :], jnp.zeros((), jnp.int32)), axis=1)).astype(jnp.int32)
    adapter_id = jnp.take(request_adapter, jnp.maximum(request, 0)).astype(jnp.int32)
    return (token_index, request, (token_index - request_start).astype(jnp.int32), adapter_id)

def rotate(matrix, position):
    row_count = matrix.shape[0]
    head_count = matrix.shape[1]
    half_rot = ROT // 2
    frequency = jnp.exp(jnp.arange(half_rot, dtype=jnp.float32) * (-2.0 * math.log(10000.0) / ROT))
    angles = position.astype(jnp.float32)[:, None] * frequency[None, :]
    cosine = jnp.cos(angles)[:, None, :]
    sine_value = jnp.sin(angles)[:, None, :]
    paired_part = matrix[:, :, :ROT].reshape(row_count, head_count, half_rot, 2)
    even_part = paired_part[:, :, :, 0]
    odd_part = paired_part[:, :, :, 1]
    turned = jnp.stack([even_part * cosine - odd_part * sine_value, odd_part * cosine + even_part * sine_value], axis=-1)
    return jnp.concatenate([turned.reshape(row_count, head_count, ROT), matrix[:, :, ROT:]], axis=2)

def slot_selector(products, chosen, adapter_id, column_count):
    row_count = products.shape[0]
    selector = (adapter_id[:, None] == chosen[None, :]).astype(jnp.float32)
    reshaped = products.reshape(row_count, chosen.shape[0], column_count)
    return lax.optimization_barrier(jnp.sum(selector[:, :, None] * reshaped, axis=1))

def widen_rows(values, chosen, adapter_id):
    selector = adapter_id[:, None] == chosen[None, :]
    spread = jnp.where(selector[:, :, None], values[:, None, :], jnp.zeros((), values.dtype))
    return spread.reshape(values.shape[0], chosen.shape[0] * values.shape[1])

def reference(tokens, layer_norm_gain, layer_norm_bias, query_key_weight, output_weight, up_weight, input_bias, down_weight, output_bias, input_adapter_left, query_key_value_right, up_adapter_right, output_adapter_left, down_adapter_left, output_adapter_right, lengths, request_adapter, slot_adapter):
    normed_rows = normalize(tokens, layer_norm_gain, layer_norm_bias)
    token_index, request, position, adapter_id = token_info(lengths, request_adapter, 0, TOKENS)
    every_id = jnp.arange(ADAPTER_COUNT, dtype=jnp.int32)
    rank_input = slot_selector(rank_product(normed_rows, input_adapter_left), slot_adapter, adapter_id, 2 * ADAPTER_RANK).astype(jnp.bfloat16)
    query_key_columns = ATTENTION_HEADS * 3 * HEAD_SIZE
    projected_rows = rank_product(normed_rows, query_key_weight.reshape(MODEL_DIM, query_key_columns)) + rank_product(widen_rows(rank_input[:, :ADAPTER_RANK], every_id, adapter_id), query_key_value_right.reshape(ADAPTER_COUNT * ADAPTER_RANK, query_key_columns))
    projected_rows = projected_rows.reshape(TOKENS, ATTENTION_HEADS, 3 * HEAD_SIZE)
    hidden_units = jax.nn.gelu(rank_product(normed_rows, up_weight) + rank_product(widen_rows(rank_input[:, ADAPTER_RANK:], every_id, adapter_id), up_adapter_right) + input_bias, approximate=True).astype(jnp.bfloat16)
    queries = rotate(projected_rows[:, :, :HEAD_SIZE], position).astype(jnp.bfloat16)
    key_rows = rotate(projected_rows[:, :, HEAD_SIZE:2 * HEAD_SIZE], position).astype(jnp.bfloat16)
    value_rows = projected_rows[:, :, 2 * HEAD_SIZE:].astype(jnp.bfloat16)
    keys_wide = key_rows.astype(jnp.float32)
    values_wide = value_rows.astype(jnp.float32)
    window = min(TOKENS, LONG + TOK_DEV)
    score_scale = HEAD_SIZE ** (-0.5)

    def one_block(number):
        first_row = (number * TOK_DEV).astype(jnp.int32)
        window_start = jnp.clip(first_row + TOK_DEV - window, 0, TOKENS - window).astype(jnp.int32)
        block_queries = lax.dynamic_slice_in_dim(queries, first_row, TOK_DEV, 0).astype(jnp.float32)
        block_request = lax.dynamic_slice_in_dim(request, first_row, TOK_DEV, 0)
        block_index = lax.dynamic_slice_in_dim(token_index, first_row, TOK_DEV, 0)
        near_keys = lax.dynamic_slice_in_dim(keys_wide, window_start, window, 0)
        near_values = lax.dynamic_slice_in_dim(values_wide, window_start, window, 0)
        near_request = lax.dynamic_slice_in_dim(request, window_start, window, 0)
        near_index = lax.dynamic_slice_in_dim(token_index, window_start, window, 0)
        scores = jnp.einsum('qhd,khd->qhk', block_queries, near_keys, precision=lax.Precision.HIGHEST) * score_scale
        allowed = jnp.logical_and(near_request[None, :] == block_request[:, None], near_index[None, :] <= block_index[:, None])[:, None, :]
        masked = jnp.where(allowed, scores, NEGATIVE_FILL)
        highest = lax.optimization_barrier(jnp.max(masked, axis=2, keepdims=True))
        weights = jnp.where(allowed, jnp.exp(masked - highest), 0.0)
        totals = lax.optimization_barrier(jnp.sum(weights, axis=2))
        summed = jnp.einsum('qhk,khd->qhd', weights.astype(jnp.bfloat16).astype(jnp.float32), near_values, precision=lax.Precision.HIGHEST)
        return (summed / totals[:, :, None]).astype(jnp.bfloat16)
    attention_output = lax.map(one_block, jnp.arange(TOKENS // TOK_DEV, dtype=jnp.int32)).reshape(TOKENS, MODEL_DIM)
    output_rank_rows = rank_product(attention_output, output_adapter_left.reshape(MODEL_DIM, ADAPTER_COUNT * ADAPTER_RANK))
    down_rank_rows = rank_product(hidden_units, down_adapter_left)
    rank_output = jnp.concatenate([slot_selector(output_rank_rows, every_id, adapter_id, ADAPTER_RANK), slot_selector(down_rank_rows, every_id, adapter_id, ADAPTER_RANK)], axis=1).astype(jnp.bfloat16)
    adapter_delta = rank_product(widen_rows(rank_output, every_id, adapter_id), output_adapter_right)
    total = rank_product(attention_output, output_weight.reshape(MODEL_DIM, MODEL_DIM)) + rank_product(hidden_units, down_weight) + adapter_delta + tokens.astype(jnp.float32) + output_bias
    return total.astype(jnp.bfloat16)
```

```python
import math

import jax
import jax.numpy as jnp
from jax import lax
from jax.sharding import PartitionSpec as P

HEAD_SIZE = 256
ROT = 64
ADAPTER_RANK = 16
EPSILON = 1e-05
NEGATIVE_FILL = -1e30
RING = (0, 2, 4, 6, 7, 5, 3, 1)
PLACE = tuple(RING.index(pair) for pair in range(8))
CORE_PERM = [(i, i ^ 1) for i in range(16)]
RING_PERM = [(RING[i] * 2, RING[(i + 1) % 8] * 2) for i in range(8)] + [
    (RING[i] * 2 + 1, RING[(i - 1) % 8] * 2 + 1) for i in range(8)
]


def to_partner(value):
    return lax.ppermute(value, "mlp", CORE_PERM)


def along_ring(value):
    return lax.ppermute(value, "mlp", RING_PERM)


def rank_product(left_side, right_side):
    return jnp.dot(left_side, right_side, preferred_element_type=jnp.float32)


def normalize(inputs, layer_norm_gain, layer_norm_bias):
    values = inputs.astype(jnp.float32)
    center = values - jnp.mean(values, axis=1, keepdims=True)
    spread = jnp.mean(center * center, axis=1, keepdims=True)
    scaled = center * lax.rsqrt(spread + EPSILON)
    return (scaled * layer_norm_gain + layer_norm_bias).astype(jnp.bfloat16)


def token_info(lengths, request_adapter, token_index):
    count = lengths.shape[0]
    earlier = lax.iota(jnp.int32, count)[:, None] < lax.iota(jnp.int32, count)[None, :]
    anchors = jnp.sum(jnp.where(earlier, lengths[:, None], 0), axis=0)
    endings = anchors + lengths
    inside = jnp.logical_and(
        anchors[None, :] <= token_index[:, None], token_index[:, None] < endings[None, :]
    )

    def pick(values):
        return jnp.sum(jnp.where(inside, values[None, :], 0), axis=1)

    request = pick(lax.iota(jnp.int32, count))
    return request, token_index - pick(anchors), pick(request_adapter)


def rotate(matrix, position):
    half_rot = ROT // 2
    frequency = jnp.exp(jnp.arange(half_rot, dtype=jnp.float32) * (-2.0 * math.log(10000.0) / ROT))
    angles = position.astype(jnp.float32)[:, None] * frequency[None, :]
    cosine = jnp.cos(angles)
    sine = jnp.sin(angles)
    part = matrix[:, :ROT].reshape(matrix.shape[0], half_rot, 2)
    even, odd = part[:, :, 0], part[:, :, 1]
    turned = jnp.stack([even * cosine - odd * sine, odd * cosine + even * sine], axis=-1)
    return jnp.concatenate([turned.reshape(matrix.shape[0], ROT), matrix[:, ROT:]], axis=1)


def slot_selector(products, chosen, adapter_id, column_count):
    row_count = products.shape[0]
    selector = (adapter_id[:, None] == chosen[None, :]).astype(jnp.float32)
    reshaped = products.reshape(row_count, chosen.shape[0], column_count)
    return jnp.sum(selector[:, :, None] * reshaped, axis=1)


def widen_rows(values, chosen, adapter_id):
    selector = adapter_id[:, None] == chosen[None, :]
    spread = jnp.where(selector[:, :, None], values[:, None, :], jnp.zeros((), values.dtype))
    return spread.reshape(values.shape[0], chosen.shape[0] * values.shape[1])


def sum_over_mlp(value):
    for bit in (1, 2, 4, 8):
        value = value + lax.ppermute(value, "mlp", [(i, i ^ bit) for i in range(16)])
    return value


def reorder(value, order, block):
    return jnp.concatenate(
        [lax.dynamic_slice_in_dim(value, order[i] * block, block, 0) for i in range(16)], axis=0
    )


def per_device(
    tokens,
    layer_norm_gain,
    layer_norm_bias,
    query_key_weight,
    output_weight,
    up_weight,
    input_bias,
    down_weight,
    output_bias,
    input_adapter_left,
    query_key_value_right,
    up_adapter_right,
    output_adapter_left,
    down_adapter_left,
    output_adapter_right,
    lengths,
    request_adapter,
    slot_adapter,
):
    block = tokens.shape[0]
    model_width = tokens.shape[1]
    group_rows = block * 16
    req_count = lax.axis_size("req")
    group = lax.axis_index("req")
    me = lax.axis_index("mlp")
    core = me % 2
    place = jnp.array(PLACE, jnp.int32)[me // 2]
    ring = jnp.array(RING, jnp.int32)
    side = 2 * core - 1

    def owner(offset, same):
        pair = ring[(place + offset + 16) % 8]
        return pair * 2 + (core if same else 1 - core)

    order = [me, me ^ 1]
    for s in (1, 2, 3):
        order += [owner(side * s, True), owner(side * s, False)]
        order += [owner(-side * s, False), owner(-side * s, True)]
    order += [owner(4, True), owner(4, False)]
    order = jnp.stack(order)
    inverse = jnp.sum(
        jnp.where(order[:, None] == jnp.arange(16)[None, :], jnp.arange(16)[:, None], 0), axis=0
    )

    adapter_ids = slot_adapter.shape[0] * 16
    every_id = lax.iota(jnp.int32, adapter_ids)
    local_index = (order[:, None] * block + lax.iota(jnp.int32, block)[None, :]).reshape(-1)
    token_index = local_index + group * group_rows
    request, position, adapter_id = token_info(lengths, request_adapter, token_index)

    qkv_rows = query_key_weight.reshape(model_width, 3 * HEAD_SIZE)
    qkv_right = query_key_value_right.reshape(adapter_ids * ADAPTER_RANK, 3 * HEAD_SIZE)
    own = normalize(tokens, layer_norm_gain, layer_norm_bias)
    parts = [jnp.concatenate([own, to_partner(own)], axis=0)]
    a, b = own, parts[0][block:]
    for s in (1, 2, 3):
        a, b = along_ring(a), along_ring(b)
        parts.append(jnp.concatenate([a, b, to_partner(a), to_partner(b)], axis=0))
    a = along_ring(a)
    parts.append(jnp.concatenate([a, to_partner(a)], axis=0))

    base, up_base, left, far_base = [], [], [], [[] for _ in range(req_count - 1)]
    for part in parts:
        product = rank_product(part, qkv_rows)
        base.append(product)
        shared = product[:, HEAD_SIZE:].astype(jnp.bfloat16)
        for d in range(1, req_count):
            far_base[d - 1].append(
                lax.ppermute(shared, "req", [(g, g + d) for g in range(req_count - d)])
            )
        left.append(rank_product(part, input_adapter_left))
        up_base.append(rank_product(part, up_weight))
    base = jnp.concatenate(base, axis=0)
    up_base = jnp.concatenate(up_base, axis=0)
    left = jnp.concatenate(left, axis=0)

    rank_part = slot_selector(left, slot_adapter, adapter_id, 2 * ADAPTER_RANK)
    rank_sum = sum_over_mlp(reorder(rank_part.astype(jnp.bfloat16), inverse, block))
    rank_input = reorder(rank_sum, order, block)
    qkv_extra = rank_product(widen_rows(rank_input[:, :ADAPTER_RANK], every_id, adapter_id), qkv_right)
    up_delta = rank_product(
        widen_rows(rank_input[:, ADAPTER_RANK:], every_id, adapter_id), up_adapter_right
    )
    projected = base + qkv_extra
    hidden_units = jax.nn.gelu(up_base + up_delta + input_bias, approximate=True).astype(jnp.bfloat16)
    queries = rotate(projected[:, :HEAD_SIZE], position).astype(jnp.bfloat16)
    keys = [rotate(projected[:, HEAD_SIZE : 2 * HEAD_SIZE], position).astype(jnp.bfloat16)]
    values = [projected[:, 2 * HEAD_SIZE :].astype(jnp.bfloat16)]
    key_index, key_request = [token_index], [request]
    for d in range(1, req_count):
        far_rank = lax.ppermute(
            rank_input[:, :ADAPTER_RANK], "req", [(g, g + d) for g in range(req_count - d)]
        )
        far_index = token_index - d * group_rows
        far_request, far_position, far_adapter = token_info(lengths, request_adapter, far_index)
        far = jnp.concatenate(far_base[d - 1], axis=0).astype(jnp.float32) + rank_product(
            widen_rows(far_rank, every_id, far_adapter), qkv_right[:, HEAD_SIZE:]
        )
        keys.append(rotate(far[:, :HEAD_SIZE], far_position).astype(jnp.bfloat16))
        values.append(far[:, HEAD_SIZE:].astype(jnp.bfloat16))
        key_index.append(far_index)
        key_request.append(jnp.where(far_index >= 0, far_request, -1))
    keys = jnp.concatenate(keys, axis=0)
    values = jnp.concatenate(values, axis=0)
    key_index = jnp.concatenate(key_index)
    key_request = jnp.concatenate(key_request)

    scores = jnp.einsum("qd,kd->qk", queries, keys, preferred_element_type=jnp.float32)
    scores = scores * HEAD_SIZE ** (-0.5)
    allowed = jnp.logical_and(
        key_request[None, :] == request[:, None], key_index[None, :] <= token_index[:, None]
    )
    masked = jnp.where(allowed, scores, NEGATIVE_FILL)
    weights = jnp.where(allowed, jnp.exp(masked - jnp.max(masked, axis=1, keepdims=True)), 0.0)
    totals = jnp.sum(weights, axis=1, keepdims=True)
    attended = (rank_product(weights.astype(jnp.bfloat16), values) / totals).astype(jnp.bfloat16)

    output_rank_rows = rank_product(
        attended, output_adapter_left.reshape(HEAD_SIZE, adapter_ids * ADAPTER_RANK)
    )
    down_rank_rows = rank_product(hidden_units, down_adapter_left)
    rank_part_out = jnp.concatenate(
        [
            slot_selector(output_rank_rows, every_id, adapter_id, ADAPTER_RANK),
            slot_selector(down_rank_rows, every_id, adapter_id, ADAPTER_RANK),
        ],
        axis=1,
    )
    rank_out_sum = sum_over_mlp(reorder(rank_part_out.astype(jnp.bfloat16), inverse, block))
    rank_output = reorder(rank_out_sum, order, block)
    own_count = slot_adapter.shape[0]
    own_ids = me * own_count + lax.iota(jnp.int32, own_count)
    rank_widened = widen_rows(rank_output, own_ids, adapter_id)
    output_rows = output_weight.reshape(HEAD_SIZE, model_width)

    def partial(first, count):
        rows = slice(first * block, (first + count) * block)
        total = (
            rank_product(attended[rows], output_rows)
            + rank_product(hidden_units[rows], down_weight)
            + rank_product(rank_widened[rows], output_adapter_right)
        )
        return [total[i * block : (i + 1) * block] for i in range(count)]

    def narrow(value):
        return value.astype(jnp.bfloat16)

    def wide(value):
        return value.astype(jnp.float32)

    a4, ax4 = partial(14, 2)
    chain_a = along_ring(narrow(a4 + wide(to_partner(narrow(ax4)))))
    chain_b = None
    for s in (3, 2, 1):
        a, b, ax, bx = partial(4 * s - 2, 4)
        add_a = bx + wide(to_partner(narrow(b)))
        add_b = ax + wide(to_partner(narrow(a)))
        chain_a = along_ring(narrow(wide(chain_a) + add_a))
        chain_b = along_ring(narrow(add_b if chain_b is None else wide(chain_b) + add_b))
    own_part, other_part = partial(0, 2)
    arrived = to_partner(narrow(wide(chain_b) + other_part))
    total = wide(chain_a) + wide(arrived) + own_part
    return (total + tokens.astype(jnp.float32) + output_bias).astype(jnp.bfloat16)


def solution(mesh):
    in_specs = (
        P(("req", "mlp"), None),
        P(),
        P(),
        P(None, "mlp", None),
        P("mlp", None, None),
        P(None, "mlp"),
        P("mlp"),
        P("mlp", None),
        P(),
        P(None, "mlp"),
        P(None, "mlp", None),
        P(None, "mlp"),
        P("mlp", None, None),
        P("mlp", None),
        P("mlp", None),
        P(),
        P(),
        P("mlp"),
    )
    out_specs = P(("req", "mlp"), None)
    return jax.shard_map(
        per_device, mesh=mesh, in_specs=in_specs, out_specs=out_specs, check_vma=False
    )
```

```python
import functools
import math

import jax
import jax.numpy as jnp
import numpy as np
from jax import lax
from jax.experimental import pallas as pl
from jax.experimental.pallas import tpu as pltpu
from jax.sharding import PartitionSpec as P

HEAD_SIZE = 256
ROT = 64
ADAPTER_RANK = 16
EPSILON = 1e-05
NEGATIVE_FILL = -1e30
RING = (0, 2, 4, 6, 7, 5, 3, 1)
PLACE = tuple(RING.index(pair) for pair in range(8))
CORE_PERM = [(i, i ^ 1) for i in range(16)]
RING_PERM = [(RING[i] * 2, RING[(i + 1) % 8] * 2) for i in range(8)] + [
    (RING[i] * 2 + 1, RING[(i - 1) % 8] * 2 + 1) for i in range(8)
]
SLOTS = 8
BLOCKS = 4
CORE, MLP, PAIRS, BASES = 0, 1, 2, 2 + SLOTS


def to_partner(value):
    return lax.ppermute(value, "mlp", CORE_PERM)


def along_ring(value):
    return lax.ppermute(value, "mlp", RING_PERM)


def rank_product(left_side, right_side):
    return jnp.dot(left_side, right_side, preferred_element_type=jnp.float32)


def across(left_side, right_side):
    return lax.dot_general(
        left_side, right_side, (((1,), (1,)), ((), ())), preferred_element_type=jnp.float32
    )


def spread_table(period, first, width):
    row = np.arange(32)[:, None]
    column = np.arange(width)[None, :]
    return jnp.asarray((row - first == column % period).astype(np.float32), jnp.bfloat16)


def params(mebibytes=20):
    return pltpu.CompilerParams(
        dimension_semantics=("arbitrary",), vmem_limit_bytes=mebibytes * 1024 * 1024
    )


def whole(array):
    return pl.BlockSpec(array.shape, lambda i, info: (0,) * array.ndim)


def slot_rows(rows, width):
    return pl.BlockSpec((rows, width), lambda i, info: (i, 0))


def pair_lanes(rows):
    return [
        pl.BlockSpec((32, rows), lambda i, info, h=half: (0, info[PAIRS + 2 * i + h]))
        for half in (0, 1)
    ]


def step_specs(rows, width):
    return [pl.BlockSpec((rows if k in (0, 4) else 2 * rows, width), lambda i, info: (0, 0)) for k in range(5)]


def load_step(step_refs, held_ref):
    i = pl.program_id(0)
    half = held_ref.shape[0] // 2

    @pl.when(i == 0)
    def _():
        held_ref[:half] = step_refs[0][...]
        held_ref[half:] = step_refs[4][...]

    for k in (1, 2, 3):

        @pl.when(i == k)
        def _(k=k):
            held_ref[...] = step_refs[k][...]


def swap_halves(info, lanes):
    half = lanes.shape[1] // 2
    return jnp.where(info[CORE] == 1, pltpu.roll(lanes, half, 1), lanes)


def lane_ids(shape, period):
    return (lax.broadcasted_iota(jnp.int32, shape, 1) // period).astype(jnp.float32)


def store_lanes(info, out_ref, lanes):
    width = lanes.shape[1] // 2
    for half in (0, 1):
        pair = info[PAIRS + 2 * pl.program_id(0) + half]
        at = pl.ds(pl.multiple_of(pair * width, width), width)
        part = lanes[:, half * width : (half + 1) * width]
        out_ref[:, at] = swap_halves(info, part).astype(out_ref.dtype)


def widened(info, rank_refs, spread_ref, adapter, column_id):
    lanes = [swap_halves(info, ref[...].astype(jnp.float32)) for ref in rank_refs]
    rows = jnp.transpose(jnp.concatenate(lanes, axis=1)).astype(jnp.bfloat16)
    spread = rank_product(rows, spread_ref[...])
    return jnp.where(column_id == adapter, spread, 0.0).astype(jnp.bfloat16)


def norm_kernel(x_ref, gain_ref, bias_ref, out_ref):
    values = x_ref[...].astype(jnp.float32)
    center = values - jnp.mean(values, axis=1, keepdims=True)
    spread = jnp.mean(center * center, axis=1, keepdims=True)
    scaled = center * lax.rsqrt(spread + EPSILON)
    out_ref[...] = (scaled * gain_ref[...] + bias_ref[...]).astype(out_ref.dtype)


def local_tokens(info, slot, shape, dim):
    rows = shape[dim] // 2
    at = lax.broadcasted_iota(jnp.int32, shape, dim)
    second = at >= rows
    at = jnp.where(second, at - rows, at) + info[CORE] * (rows // 2)
    at = jnp.where(at >= rows, at - rows, at)
    return (at + jnp.where(second, info[BASES + slot + 1], info[BASES + slot])).astype(jnp.float32)


def token_kernel(info, column_ref, row_ref, ids_ref, table_ref, meta_ref, turn_ref):
    rows = meta_ref.shape[0]
    count = row_ref.shape[1]
    earlier = lax.broadcasted_iota(jnp.int32, (count, count), 0) < lax.broadcasted_iota(
        jnp.int32, (count, count), 1
    )
    anchors = jnp.sum(jnp.where(earlier, column_ref[...], 0.0), axis=0, keepdims=True)
    endings = anchors + row_ref[...]
    token = local_tokens(info, 2 * pl.program_id(0), (rows, 1), 0)
    inside = jnp.logical_and(anchors <= token, token < endings)
    start = jnp.sum(jnp.where(inside, anchors, 0.0), axis=1, keepdims=True)
    adapter = jnp.sum(jnp.where(inside, ids_ref[...], 0.0), axis=1, keepdims=True)
    lane = lax.broadcasted_iota(jnp.int32, meta_ref.shape, 1)
    meta_ref[...] = jnp.where(lane < 64, start, adapter)
    angle = (token - start) * table_ref[0:1, :] - table_ref[1:2, :]
    turn_ref[...] = jnp.cos(angle) * table_ref[2:3, :]


def rank_kernel(info, *refs):
    steps, (meta_ref, slot_ref, fold_ref, out_ref, held_ref) = refs[:5], refs[5:]
    load_step(steps, held_ref)
    adapter = meta_ref[:, 64:65]
    chosen = jnp.where(slot_ref[...] == adapter, held_ref[...], 0.0).astype(jnp.bfloat16)
    store_lanes(info, out_ref, across(fold_ref[...], chosen))


def turn(part, table):
    width = table.shape[1]
    lane = lax.broadcasted_iota(jnp.int32, table.shape, 1)
    cos = jnp.where(lane < ROT, table, 1.0)
    sin = jnp.where(lane < ROT, pltpu.roll(table, width - ROT, 1), 0.0)
    head = part[:, :width]
    swapped = jnp.where(
        lane % 2 == 0, pltpu.roll(head, width - 1, 1), pltpu.roll(head, 1, 1)
    )
    return jnp.concatenate([head * cos + swapped * sin, part[:, width:]], axis=1)


def qkv_kernel(info, *refs):
    steps, refs = refs[:5], refs[5:]
    rank_refs, (meta_ref, turn_ref, spread_ref, right_ref) = refs[:2], refs[2:6]
    q_ref, k_ref, v_ref, held_ref = refs[6:]
    load_step(steps, held_ref)
    column_id = lane_ids((held_ref.shape[0], spread_ref.shape[1]), ADAPTER_RANK)
    wide = widened(info, rank_refs, spread_ref, meta_ref[:, 64:65], column_id)
    total = held_ref[...] + rank_product(wide, right_ref[...])
    table = turn_ref[...]
    q_ref[...] = (turn(total[:, :HEAD_SIZE], table) * HEAD_SIZE ** (-0.5)).astype(jnp.bfloat16)
    k_ref[...] = turn(total[:, HEAD_SIZE : 2 * HEAD_SIZE], table).astype(jnp.bfloat16)
    v_ref[...] = total[:, 2 * HEAD_SIZE :].astype(jnp.bfloat16)


def far_kernel(info, early_ref, late_ref, *refs):
    rank_refs, (meta_ref, turn_ref, spread_ref, right_ref) = refs[:2], refs[2:6]
    k_ref, v_ref, held_ref = refs[6:]
    i = pl.program_id(0)
    rows = held_ref.shape[0]
    half = rows // 2

    @pl.when(i == 0)
    def _():
        held_ref[:half] = early_ref[:half]
        held_ref[half:] = late_ref[rows:]

    @pl.when(jnp.logical_or(i == 1, i == 2))
    def _():
        held_ref[...] = early_ref[pl.ds(pl.multiple_of(half + (i - 1) * rows, half), rows), :]

    @pl.when(i == 3)
    def _():
        held_ref[...] = late_ref[:rows]

    column_id = lane_ids((rows, spread_ref.shape[1]), ADAPTER_RANK)
    wide = widened(info, rank_refs, spread_ref, meta_ref[:, 64:65], column_id)
    total = held_ref[...].astype(jnp.float32) + rank_product(wide, right_ref[...][:, HEAD_SIZE:])
    k_ref[...] = turn(total[:, :HEAD_SIZE], turn_ref[...]).astype(jnp.bfloat16)
    v_ref[...] = total[:, HEAD_SIZE:].astype(jnp.bfloat16)


def hidden_kernel(info, *refs):
    steps, refs = refs[:5], refs[5:]
    rank_refs, (meta_ref, spread_ref, right_ref, bias_ref, left_ref) = refs[:2], refs[2:7]
    hidden_ref, out_ref, held_ref = refs[7:]
    load_step(steps, held_ref)
    adapter = meta_ref[:, 64:65]
    column_id = lane_ids((held_ref.shape[0], spread_ref.shape[1]), ADAPTER_RANK)
    wide = widened(info, rank_refs, spread_ref, adapter, column_id)
    x = held_ref[...] + rank_product(wide, right_ref[...]) + bias_ref[...]
    inner = math.sqrt(2.0 / math.pi) * (x + 0.044715 * (x * x * x))
    hidden = (0.5 * x * (1.0 + jnp.tanh(inner))).astype(jnp.bfloat16)
    hidden_ref[...] = hidden
    products = rank_product(hidden, left_ref[...])
    chosen = jnp.where(column_id == adapter, products, 0.0).astype(jnp.bfloat16)
    store_lanes(info, out_ref, across(spread_ref[...], chosen))


def attention_kernel(req_count, info, *refs):
    q_ref, refs = refs[0], refs[1:]
    key_refs, value_refs, refs = refs[:req_count], refs[req_count : 2 * req_count], refs[2 * req_count :]
    meta_ref, spread_ref, left_ref, attended_ref, out_ref = refs[:5]
    top_ref, sum_ref, acc_ref = refs[5:]
    i = pl.program_id(0)
    rows = q_ref.shape[0]
    span = 2 * rows

    def twice(lanes):
        return jnp.concatenate([lanes] * (HEAD_SIZE // lanes.shape[1]), axis=1)

    start = meta_ref[:, 0:1]
    query = local_tokens(info, 2 * i, (rows, 1), 0)
    lowest, highest = jnp.min(start), jnp.max(query)
    top_ref[...] = jnp.full_like(top_ref, NEGATIVE_FILL)
    sum_ref[...] = jnp.zeros_like(sum_ref)
    acc_ref[...] = jnp.zeros_like(acc_ref)
    q = q_ref[...]
    pair = rows // 2
    for d in range(req_count):
        for half in (0, 1):
            slot = d * SLOTS + 4 * half
            needed = None
            for k in range(4):
                base = info[BASES + slot + k].astype(jnp.float32)
                meets = jnp.logical_and(base <= highest, base + (pair - 1) >= lowest)
                needed = meets if needed is None else jnp.logical_or(needed, meets)

            @pl.when(needed)
            def _(d=d, half=half, slot=slot):
                at = slice(half * span, (half + 1) * span)
                scores = across(q, key_refs[d][at, :])
                key = jnp.concatenate(
                    [local_tokens(info, slot + k, (1, rows), 1) for k in (0, 2)], axis=1
                )
                allowed = jnp.logical_and(key <= query, key >= start)
                scores = jnp.where(allowed, scores, NEGATIVE_FILL)
                top = top_ref[...]
                new_top = jnp.maximum(top, jnp.max(scores, axis=1, keepdims=True))
                weights = jnp.where(allowed, jnp.exp(scores - new_top[:, 0:1]), 0.0)
                scale = jnp.exp(top - new_top)
                top_ref[...] = new_top
                sum_ref[...] = sum_ref[...] * scale + jnp.sum(weights, axis=1, keepdims=True)
                acc_ref[...] = acc_ref[...] * twice(scale) + rank_product(
                    weights.astype(jnp.bfloat16), value_refs[d][at, :]
                )

    attended = (acc_ref[...] / twice(sum_ref[...])).astype(jnp.bfloat16)
    attended_ref[...] = attended
    products = rank_product(attended, left_ref[...])
    column_id = lane_ids(products.shape, ADAPTER_RANK)
    chosen = jnp.where(column_id == meta_ref[:, 64:65], products, 0.0).astype(jnp.bfloat16)
    store_lanes(info, out_ref, across(spread_ref[...], chosen))


def widen_kernel(info, first_ref, second_ref, meta_ref, spread_ref, out_ref):
    width = out_ref.shape[1]
    count = width // (4 * ADAPTER_RANK)
    column_id = lax.broadcasted_iota(jnp.int32, out_ref.shape, 1) // (2 * ADAPTER_RANK)
    partner = info[MLP] + 1 - 2 * info[CORE]
    column_id = column_id + jnp.where(
        column_id < count, info[MLP] * count, (partner - 1) * count
    )
    adapter = meta_ref[:, 64:65]
    out_ref[...] = widened(
        info, (first_ref, second_ref), spread_ref, adapter, column_id.astype(jnp.float32)
    )


def slot_call(kernel, info, operands, specs, outs, out_specs, scratch, flops, read, steps=BLOCKS, mib=20):
    return pl.pallas_call(
        kernel,
        grid_spec=pltpu.PrefetchScalarGridSpec(
            num_scalar_prefetch=1,
            grid=(steps,),
            in_specs=specs,
            out_specs=out_specs,
            scratch_shapes=scratch,
        ),
        out_shape=outs,
        compiler_params=params(mib),
        cost_estimate=pl.CostEstimate(flops=flops, bytes_accessed=read, transcendentals=0),
    )(info, *operands)


def shape(rows, width, dtype=jnp.bfloat16):
    return jax.ShapeDtypeStruct((rows, width), dtype)


def sum_over_mlp(value, bits):
    for bit in bits:
        value = value + lax.ppermute(value, "mlp", [(i, i ^ bit) for i in range(16)])
    return value


def narrow(value):
    return value.astype(jnp.bfloat16)


def wide(value):
    return value.astype(jnp.float32)


def per_device(
    tokens,
    layer_norm_gain,
    layer_norm_bias,
    query_key_weight,
    output_weight,
    up_weight,
    input_bias,
    down_weight,
    output_bias,
    input_adapter_left,
    query_key_value_right,
    up_adapter_right,
    output_adapter_left,
    down_adapter_left,
    output_adapter_right,
    lengths,
    request_adapter,
    slot_adapter,
):
    block = tokens.shape[0]
    model_width = tokens.shape[1]
    pair_rows = 2 * block
    group_rows = SLOTS * pair_rows
    req_count = lax.axis_size("req")
    group = lax.axis_index("req")
    me = lax.axis_index("mlp")
    block_rows = 2 * pair_rows
    table = np.zeros((req_count, 16, 2 + SLOTS * (1 + req_count)), np.int32)
    for g in range(req_count):
        for m in range(16):
            side = 2 * (m % 2) - 1
            steps = [0, 4] + [t for s in (1, 2, 3) for t in (side * s, -side * s)]
            pairs = [RING[(PLACE[m // 2] + t) % 8] for t in steps]
            firsts = [(g - d) * group_rows + p * pair_rows for d in range(req_count) for p in pairs]
            table[g, m] = [m % 2, m] + pairs + firsts
    info = lax.dynamic_slice(jnp.asarray(table), (group, me, 0), (1, 1, table.shape[2])).reshape(-1)

    own = pl.pallas_call(
        norm_kernel,
        out_shape=shape(block, model_width),
        cost_estimate=pl.CostEstimate(flops=block * model_width * 8, bytes_accessed=1 << 20, transcendentals=0),
    )(tokens, layer_norm_gain.reshape(1, -1), layer_norm_bias.reshape(1, -1))

    other = to_partner(own)
    a, b = along_ring(own), along_ring(other)
    first_part = jnp.concatenate([own, other], axis=0)
    first_part, near_left, near_right, slot_ids, tied_lengths, tied_ids, a = lax.optimization_barrier(
        (
            first_part,
            input_adapter_left,
            output_adapter_right,
            slot_adapter,
            lengths,
            request_adapter,
            a,
        )
    )
    parts = [first_part]
    for s in (1, 2, 3):
        if s > 1:
            a, b = along_ring(a), along_ring(b)
        parts.append(jnp.concatenate([a, b, to_partner(b), to_partner(a)], axis=0))
    a = along_ring(a)
    parts.append(jnp.concatenate([a, to_partner(a)], axis=0))

    pair_left = jnp.concatenate([near_left, to_partner(near_left)], axis=1)
    pair_right = jnp.concatenate([near_right, to_partner(near_right)], axis=0)
    slot_columns = wide(jnp.repeat(slot_ids, 2 * ADAPTER_RANK))[None, :]
    slot_columns = jnp.concatenate([slot_columns, to_partner(slot_columns)], axis=1)

    float_lengths = wide(tied_lengths)
    lane = np.arange(128)
    turn_rows = np.zeros((8, 128), np.float32)
    turn_rows[0] = np.exp(lane % ROT // 2 * (-2.0 * math.log(10000.0) / ROT))
    turn_rows[1] = np.where(lane < ROT, 0.0, math.pi / 2)
    turn_rows[2] = np.where(lane < ROT, 1.0, np.where(lane % 2 == 0, -1.0, 1.0))
    token_rows = req_count * group_rows
    token_args = [
        float_lengths[:, None],
        float_lengths[None, :],
        wide(tied_ids)[None, :],
        jnp.asarray(turn_rows),
    ]
    meta, turns = slot_call(
        token_kernel,
        info,
        token_args,
        [whole(x) for x in token_args],
        [shape(token_rows, 128, jnp.float32)] * 2,
        [slot_rows(block_rows, 128)] * 2,
        [],
        token_rows * 128 * 100,
        token_rows * 128 * 8,
        steps=req_count * BLOCKS,
    )

    qkv_rows = query_key_weight.reshape(model_width, 3 * HEAD_SIZE)
    adapter_columns = query_key_value_right.shape[0]
    qkv_right = query_key_value_right.reshape(adapter_columns, 3 * HEAD_SIZE)
    spread_first = spread_table(ADAPTER_RANK, 0, adapter_columns)
    spread_last = spread_table(ADAPTER_RANK, ADAPTER_RANK, adapter_columns)
    spread_own = spread_table(2 * ADAPTER_RANK, 0, pair_right.shape[0])

    base, up_base, left, shared = [], [], [], []
    for part in parts:
        left.append(rank_product(part, pair_left))
        product = rank_product(part, qkv_rows)
        base.append(product)
        shared.append(narrow(product[:, HEAD_SIZE:]))
        up_base.append(rank_product(part, up_weight))

    def to_group(value, d):
        return lax.ppermute(value, "req", [(g, g + d) for g in range(req_count - d)])

    early, late = jnp.concatenate(shared[:3], axis=0), jnp.concatenate(shared[3:], axis=0)
    far_base = [(to_group(early, d), to_group(late, d)) for d in range(1, req_count)]

    held = functools.partial(pltpu.VMEM, dtype=jnp.float32)
    meta_spec = slot_rows(block_rows, 128)
    all_lanes = pl.BlockSpec((32, group_rows), lambda i, info: (0, 0))
    rank_part = slot_call(
        rank_kernel,
        info,
        left + [meta, slot_columns, spread_own],
        step_specs(pair_rows, left[0].shape[1]) + [meta_spec, whole(slot_columns), whole(spread_own)],
        shape(32, group_rows),
        all_lanes,
        [held((block_rows, left[0].shape[1]))],
        2 * group_rows * 256 * 32,
        1 << 20,
    )
    rank_in = sum_over_mlp(rank_part, (2, 4, 8))

    hidden_width = up_weight.shape[1]
    bias_row = input_bias.reshape(1, -1)
    far_rank = [to_group(rank_in, d) for d in range(1, req_count)]
    queries, own_keys, own_values = slot_call(
        qkv_kernel,
        info,
        base + [rank_in, rank_in, meta, turns, spread_first, qkv_right],
        step_specs(pair_rows, 3 * HEAD_SIZE)
        + pair_lanes(pair_rows)
        + [meta_spec, meta_spec, whole(spread_first), whole(qkv_right)],
        [shape(group_rows, HEAD_SIZE)] * 3,
        [slot_rows(block_rows, HEAD_SIZE)] * 3,
        [held((block_rows, 3 * HEAD_SIZE))],
        2 * group_rows * adapter_columns * 3 * HEAD_SIZE,
        8 << 20,
    )
    hidden_args = [meta, spread_last, up_adapter_right, bias_row, down_adapter_left]
    hidden, hidden_rank = slot_call(
        hidden_kernel,
        info,
        up_base + [rank_in, rank_in] + hidden_args,
        step_specs(pair_rows, hidden_width)
        + pair_lanes(pair_rows)
        + [meta_spec]
        + [whole(x) for x in hidden_args[1:]],
        [shape(group_rows, hidden_width), shape(32, group_rows)],
        [slot_rows(block_rows, hidden_width), all_lanes],
        [held((block_rows, hidden_width))],
        4 * group_rows * adapter_columns * hidden_width,
        8 << 20,
    )
    keys, values = [own_keys], [own_values]
    for d in range(1, req_count):
        far_table = pl.BlockSpec((block_rows, 128), lambda i, info, f=d * BLOCKS: (f + i, 0))
        far_early, far_late = far_base[d - 1]
        far_keys, far_values = slot_call(
            far_kernel,
            info,
            [far_early, far_late]
            + [far_rank[d - 1], far_rank[d - 1], meta, turns, spread_first, qkv_right],
            [whole(far_early), whole(far_late)]
            + pair_lanes(pair_rows)
            + [far_table, far_table, whole(spread_first), whole(qkv_right)],
            [shape(group_rows, HEAD_SIZE)] * 2,
            [slot_rows(block_rows, HEAD_SIZE)] * 2,
            [pltpu.VMEM((block_rows, 2 * HEAD_SIZE), jnp.bfloat16)],
            2 * group_rows * adapter_columns * 2 * HEAD_SIZE,
            6 << 20,
        )
        keys.append(far_keys)
        values.append(far_values)

    output_left = output_adapter_left.reshape(HEAD_SIZE, adapter_columns)
    attended, attended_rank = slot_call(
        functools.partial(attention_kernel, req_count),
        info,
        [queries] + keys + values + [meta, spread_first, output_left],
        [slot_rows(block_rows, HEAD_SIZE)]
        + [whole(x) for x in keys + values]
        + [meta_spec, whole(spread_first), whole(output_left)],
        [shape(group_rows, HEAD_SIZE), shape(32, group_rows)],
        [slot_rows(block_rows, HEAD_SIZE), all_lanes],
        [
            held((block_rows, 128)),
            held((block_rows, 128)),
            held((block_rows, HEAD_SIZE)),
        ],
        4 * group_rows * group_rows * HEAD_SIZE,
        8 << 20,
        mib=16 + 3 * req_count,
    )
    rank_out = sum_over_mlp(attended_rank + hidden_rank, (1, 2, 4, 8))
    rank_widened = slot_call(
        widen_kernel,
        info,
        [rank_out, rank_out, meta, spread_own],
        pair_lanes(pair_rows) + [meta_spec, whole(spread_own)],
        shape(group_rows, pair_right.shape[0]),
        slot_rows(block_rows, pair_right.shape[0]),
        [],
        2 * group_rows * 32 * pair_right.shape[0],
        1 << 20,
    )
    output_rows = output_weight.reshape(HEAD_SIZE, model_width)

    def main(slot):
        rows = slice(slot * pair_rows, (slot + 1) * pair_rows)
        return rank_product(attended[rows], output_rows) + rank_product(hidden[rows], down_weight)

    def adapted(slot, half):
        first = slot * pair_rows + half * block
        return rank_product(rank_widened[first : first + block], pair_right)

    opposite = main(1)
    sums = {1: opposite[:block] + wide(to_partner(narrow(opposite[block:])))}
    for s in (3, 2, 1):
        arrived = wide(to_partner(narrow(main(2 * s))))
        mine = main(2 * s + 1)
        sums[2 * s + 1] = (mine[:block] + arrived[block:], mine[block:] + arrived[:block])
    chain_a = along_ring(narrow(sums[1] + adapted(1, 0)))
    chain_b = None
    for s in (3, 2, 1):
        slot = 2 * s + 1
        add_a = sums[slot][0] + adapted(slot, 0)
        add_b = sums[slot][1] + adapted(slot, 1)
        add_a, add_b = lax.optimization_barrier((add_a, add_b))
        if chain_b is None:
            chain_b = along_ring(narrow(add_b))
            chain_a = along_ring(narrow(wide(chain_a) + add_a))
        else:
            chain_a = along_ring(narrow(wide(chain_a) + add_a))
            chain_b = along_ring(narrow(wide(chain_b) + add_b))
    final = main(0)
    arrived = to_partner(narrow(wide(chain_b) + final[block:]))
    total = wide(chain_a) + wide(arrived) + final[:block] + adapted(0, 0)
    return narrow(total + wide(tokens) + output_bias)


def solution(mesh):
    in_specs = (
        P(("req", "mlp"), None),
        P(),
        P(),
        P(None, "mlp", None),
        P("mlp", None, None),
        P(None, "mlp"),
        P("mlp"),
        P("mlp", None),
        P(),
        P(None, "mlp"),
        P(None, "mlp", None),
        P(None, "mlp"),
        P("mlp", None, None),
        P("mlp", None),
        P("mlp", None),
        P(),
        P(),
        P("mlp"),
    )
    out_specs = P(("req", "mlp"), None)
    return jax.shard_map(
        per_device, mesh=mesh, in_specs=in_specs, out_specs=out_specs, check_vma=False
    )
```

```python
import functools
import math

import jax
import jax.numpy as jnp
import numpy as np
from jax import lax
from jax.experimental import pallas as pl
from jax.experimental.pallas import tpu as pltpu
from jax.sharding import PartitionSpec as P

HEAD_SIZE = 256
ROT = 64
ADAPTER_RANK = 16
EPSILON = 1e-05
NEGATIVE_FILL = -1e30
RING = (0, 2, 4, 6, 7, 5, 3, 1)
PLACE = tuple(RING.index(pair) for pair in range(8))
CORE_PERM = [(i, i ^ 1) for i in range(16)]
RING_PERM = [(RING[i] * 2, RING[(i + 1) % 8] * 2) for i in range(8)] + [
    (RING[i] * 2 + 1, RING[(i - 1) % 8] * 2 + 1) for i in range(8)
]
SLOTS = 8
BLOCKS = 4
CORE, MLP, PAIRS, BASES = 0, 1, 2, 2 + SLOTS


def to_partner(value):
    return lax.ppermute(value, "mlp", CORE_PERM)


def along_ring(value):
    return lax.ppermute(value, "mlp", RING_PERM)


def rank_product(left_side, right_side):
    return jnp.dot(left_side, right_side, preferred_element_type=jnp.float32)


def across(left_side, right_side):
    return lax.dot_general(
        left_side, right_side, (((1,), (1,)), ((), ())), preferred_element_type=jnp.float32
    )


def spread_table(period, first, width):
    row = np.arange(32)[:, None]
    column = np.arange(width)[None, :]
    return jnp.asarray((row - first == column % period).astype(np.float32), jnp.bfloat16)


def swap_halves(info, lanes):
    half = lanes.shape[1] // 2
    return jnp.where(info[CORE] == 1, pltpu.roll(lanes, half, 1), lanes)


def lane_ids(shape, period):
    return (lax.broadcasted_iota(jnp.int32, shape, 1) // period).astype(jnp.float32)


def pair_at(info, slot, rows):
    return pl.ds(pl.multiple_of(info[PAIRS + slot] * rows, rows), rows)


def store_lanes(info, out_ref, lanes, slot):
    width = out_ref.shape[1] // SLOTS
    for k in range(lanes.shape[1] // width):
        part = lanes[:, k * width : (k + 1) * width]
        out_ref[:, pair_at(info, slot + k, width)] = swap_halves(info, part).astype(out_ref.dtype)


def rank_rows(info, rank_ref, slot, count):
    width = rank_ref.shape[1] // SLOTS
    lanes = [
        swap_halves(info, rank_ref[:, pair_at(info, slot + k, width)].astype(jnp.float32))
        for k in range(count)
    ]
    lanes = lanes[0] if count == 1 else jnp.concatenate(lanes, axis=1)
    return jnp.transpose(lanes).astype(jnp.bfloat16)


def widened(rows, spread_ref, own):
    return jnp.where(own, rank_product(rows, spread_ref[...]), 0.0).astype(jnp.bfloat16)


def cosine(angle):
    turns = jnp.floor(angle * (1.0 / math.pi) + 0.5)
    rest = ((angle - turns * 3.140625) - turns * 9.67502593994140625e-4) - turns * 1.509957990978376e-7
    square = rest * rest
    value = jnp.full_like(square, 1.0 / 479001600.0)
    for factor in (-1.0 / 3628800.0, 1.0 / 40320.0, -1.0 / 720.0, 1.0 / 24.0, -0.5, 1.0):
        value = value * square + factor
    odd = turns - 2.0 * jnp.floor(turns * 0.5)
    return value * (1.0 - 2.0 * odd)


def norm_kernel(x_ref, gain_ref, bias_ref, out_ref):
    values = x_ref[...].astype(jnp.float32)
    center = values - jnp.mean(values, axis=1, keepdims=True)
    spread = jnp.mean(center * center, axis=1, keepdims=True)
    scaled = center * lax.rsqrt(spread + EPSILON)
    out_ref[...] = (scaled * gain_ref[...] + bias_ref[...]).astype(out_ref.dtype)


def local_tokens(info, slot, shape, dim):
    rows = shape[dim] // 2
    at = lax.broadcasted_iota(jnp.int32, shape, dim)
    second = at >= rows
    at = jnp.where(second, at - rows, at) + info[CORE] * (rows // 2)
    at = jnp.where(at >= rows, at - rows, at)
    return (at + jnp.where(second, info[BASES + slot + 1], info[BASES + slot])).astype(jnp.float32)


def token_kernel(info, column_ref, row_ref, ids_ref, table_ref, meta_ref, turn_ref):
    rows = 2 * 128
    count = row_ref.shape[1]
    earlier = lax.broadcasted_iota(jnp.int32, (count, count), 0) < lax.broadcasted_iota(
        jnp.int32, (count, count), 1
    )
    anchors = jnp.sum(jnp.where(earlier, column_ref[...], 0.0), axis=0, keepdims=True)
    endings = anchors + row_ref[...]
    ids = ids_ref[...]
    lane = lax.broadcasted_iota(jnp.int32, (rows, 128), 1)

    def one(block, _):
        token = local_tokens(info, 2 * block, (rows, 1), 0)
        inside = jnp.logical_and(anchors <= token, token < endings)
        start = jnp.sum(jnp.where(inside, anchors, 0.0), axis=1, keepdims=True)
        adapter = jnp.sum(jnp.where(inside, ids, 0.0), axis=1, keepdims=True)
        at = pl.ds(pl.multiple_of(block * rows, rows), rows)
        meta_ref[at, :] = jnp.where(lane < 64, start, adapter)
        angle = (token - start) * table_ref[0:1, :] - table_ref[1:2, :]
        turn_ref[at, :] = cosine(angle) * table_ref[2:3, :]
        return 0

    lax.fori_loop(0, meta_ref.shape[0] // rows, one, 0)


def rank_kernel(count, first_slot, info, *refs):
    x = jnp.concatenate([ref[...] for ref in refs[:count]], axis=0)
    left_ref, meta_ref, slot_ref, fold_ref, held_ref, out_ref = refs[count:]
    products = rank_product(x, left_ref[...])
    adapter = meta_ref[first_slot * 128 : first_slot * 128 + x.shape[0], 64:65]
    chosen = jnp.where(slot_ref[...] == adapter, products, 0.0).astype(jnp.bfloat16)
    out_ref[...] = held_ref[...]
    store_lanes(info, out_ref, across(fold_ref[...], chosen), first_slot)


def base_kernel(count, *refs):
    x = jnp.concatenate([ref[...] for ref in refs[:count]], axis=0)
    qkv_ref, up_ref, base_ref, up_base_ref, shared_ref = refs[count:]
    first = rank_product(x, qkv_ref[...])
    base_ref[...] = first
    shared_ref[...] = first[:, HEAD_SIZE:].astype(shared_ref.dtype)
    up_base_ref[...] = rank_product(x, up_ref[...])


def turn(part, table):
    width = table.shape[1]
    lane = lax.broadcasted_iota(jnp.int32, table.shape, 1)
    cos = jnp.where(lane < ROT, table, 1.0)
    sin = jnp.where(lane < ROT, pltpu.roll(table, width - ROT, 1), 0.0)
    head = part[:, :width]
    swapped = jnp.where(
        lane % 2 == 0, pltpu.roll(head, width - 1, 1), pltpu.roll(head, 1, 1)
    )
    return jnp.concatenate([head * cos + swapped * sin, part[:, width:]], axis=1)


def block_rows_of(refs, block):
    if block:
        return refs[block][...]
    return jnp.concatenate([refs[0][...], refs[4][...]], axis=0)


def inner_kernel(info, *refs):
    base_refs, up_refs, (rank_ref, meta_ref, turn_ref, first_ref, last_ref) = refs[:5], refs[5:10], refs[10:15]
    qkv_right_ref, up_right_ref, bias_ref, left_ref = refs[15:19]
    q_ref, k_ref, v_ref, hidden_ref, out_ref = refs[19:]
    rows = 256
    column_id = lane_ids((rows, first_ref.shape[1]), ADAPTER_RANK)
    for block in range(BLOCKS):
        at = slice(block * rows, (block + 1) * rows)
        own = column_id == meta_ref[at, 64:65]
        ranks = rank_rows(info, rank_ref, 2 * block, 2)
        total = block_rows_of(base_refs, block) + rank_product(
            widened(ranks, first_ref, own), qkv_right_ref[...]
        )
        table = turn_ref[at, :]
        q_ref[at, :] = (turn(total[:, :HEAD_SIZE], table) * HEAD_SIZE ** (-0.5)).astype(jnp.bfloat16)
        k_ref[at, :] = turn(total[:, HEAD_SIZE : 2 * HEAD_SIZE], table).astype(jnp.bfloat16)
        v_ref[at, :] = total[:, 2 * HEAD_SIZE :].astype(jnp.bfloat16)
        x = block_rows_of(up_refs, block) + rank_product(widened(ranks, last_ref, own), up_right_ref[...])
        x = x + bias_ref[...]
        inner = math.sqrt(2.0 / math.pi) * (x + 0.044715 * (x * x * x))
        hidden = (0.5 * x * (1.0 + jnp.tanh(inner))).astype(jnp.bfloat16)
        hidden_ref[at, :] = hidden
        chosen = jnp.where(own, rank_product(hidden, left_ref[...]), 0.0).astype(jnp.bfloat16)
        store_lanes(info, out_ref, across(last_ref[...], chosen), 2 * block)


def far_kernel(first_row, info, *refs):
    shared_refs, (rank_ref, meta_ref, turn_ref, spread_ref, right_ref, k_ref, v_ref) = refs[:5], refs[5:]
    rows = 256
    column_id = lane_ids((rows, spread_ref.shape[1]), ADAPTER_RANK)
    for block in range(BLOCKS):
        at = slice(block * rows, (block + 1) * rows)
        far_at = slice(first_row + block * rows, first_row + (block + 1) * rows)
        own = column_id == meta_ref[far_at, 64:65]
        wide = widened(rank_rows(info, rank_ref, 2 * block, 2), spread_ref, own)
        total = block_rows_of(shared_refs, block).astype(jnp.float32)
        total = total + rank_product(wide, right_ref[:, HEAD_SIZE:])
        k_ref[at, :] = turn(total[:, :HEAD_SIZE], turn_ref[far_at, :]).astype(jnp.bfloat16)
        v_ref[at, :] = total[:, HEAD_SIZE:].astype(jnp.bfloat16)


def attention_kernel(req_count, info, *refs):
    q_ref, refs = refs[0], refs[1:]
    key_refs, value_refs, refs = refs[:req_count], refs[req_count : 2 * req_count], refs[2 * req_count :]
    meta_ref, spread_ref, left_ref, hidden_rank_ref, attended_ref, out_ref = refs[:6]
    top_ref, sum_ref, acc_ref, fold_ref = refs[6:]
    rows = 256
    pair = rows // 2
    column_id = lane_ids((rows, left_ref.shape[1]), ADAPTER_RANK)

    def twice(lanes):
        return jnp.concatenate([lanes] * (HEAD_SIZE // lanes.shape[1]), axis=1)

    def one(block, _):
        at = pl.ds(pl.multiple_of(block * rows, rows), rows)
        start = meta_ref[at, 0:1]
        query = local_tokens(info, 2 * block, (rows, 1), 0)
        q = q_ref[at, :]

        def scores_of(d):
            scores = across(q, key_refs[d][...])
            key = jnp.concatenate(
                [local_tokens(info, d * SLOTS + k, (1, rows), 1) for k in range(0, SLOTS, 2)], axis=1
            )
            allowed = jnp.logical_and(key <= query, key >= start)
            return jnp.where(allowed, scores, NEGATIVE_FILL), allowed

        scores, _ = scores_of(0)
        top = jnp.max(scores, axis=1, keepdims=True)
        weights = jnp.exp(scores - top)
        top_ref[...] = jnp.broadcast_to(top, top_ref.shape)
        sum_ref[...] = jnp.broadcast_to(jnp.sum(weights, axis=1, keepdims=True), sum_ref.shape)
        acc_ref[...] = rank_product(weights.astype(jnp.bfloat16), value_refs[0][...])
        lowest = jnp.min(start)
        for d in range(1, req_count):
            highest = info[BASES + d * SLOTS] + pair
            for k in range(1, SLOTS):
                highest = jnp.maximum(highest, info[BASES + d * SLOTS + k] + pair)

            @pl.when(highest.astype(jnp.float32) > lowest)
            def _(d=d):
                scores, allowed = scores_of(d)
                top = top_ref[...]
                new_top = jnp.maximum(top, jnp.max(scores, axis=1, keepdims=True))
                weights = jnp.where(allowed, jnp.exp(scores - new_top[:, 0:1]), 0.0)
                scale = jnp.exp(top - new_top)
                top_ref[...] = new_top
                sum_ref[...] = sum_ref[...] * scale + jnp.sum(weights, axis=1, keepdims=True)
                acc_ref[...] = acc_ref[...] * twice(scale) + rank_product(
                    weights.astype(jnp.bfloat16), value_refs[d][...]
                )

        attended = (acc_ref[...] / twice(sum_ref[...])).astype(jnp.bfloat16)
        attended_ref[at, :] = attended
        chosen = jnp.where(column_id == meta_ref[at, 64:65], rank_product(attended, left_ref[...]), 0.0)
        store_lanes(info, fold_ref, across(spread_ref[...], chosen.astype(jnp.bfloat16)), 2 * block)
        return 0

    lax.fori_loop(0, BLOCKS, one, 0)
    out_ref[...] = (fold_ref[...] + hidden_rank_ref[...].astype(jnp.float32)).astype(out_ref.dtype)


def main_kernel(block, attended_ref, hidden_ref, output_ref, down_ref, kept_ref, sent_ref):
    rows = 256
    sent = sent_ref.shape[0]
    width = 512
    attended = attended_ref[block * rows : (block + 1) * rows, :]
    hidden = hidden_ref[block * rows : (block + 1) * rows, :]

    def one(step, _):
        at = pl.ds(pl.multiple_of(step * width, width), width)
        total = rank_product(attended, output_ref[:, at]) + rank_product(hidden, down_ref[:, at])
        if block:
            sent_ref[:, at] = total[:sent].astype(sent_ref.dtype)
            kept_ref[:, at] = total[sent:]
        else:
            kept_ref[:, at] = total[: rows - sent]
            sent_ref[:, at] = total[rows - sent :].astype(sent_ref.dtype)
        return 0

    lax.fori_loop(0, output_ref.shape[1] // width, one, 0)


def adapt_kernel(slot, first, info, rank_ref, meta_ref, spread_ref, right_ref, kept_ref, arrived_ref, *out_refs):
    pair = 128
    half = pair // 2
    columns = spread_ref.shape[1]
    count = columns // (4 * ADAPTER_RANK)
    column_id = lax.broadcasted_iota(jnp.int32, (pair, columns), 1) // (2 * ADAPTER_RANK)
    partner = info[MLP] + 1 - 2 * info[CORE]
    column_id = column_id + jnp.where(column_id < count, info[MLP] * count, (partner - 1) * count)
    own = column_id.astype(jnp.float32) == meta_ref[slot * pair : (slot + 1) * pair, 64:65]
    wide = widened(rank_rows(info, rank_ref, slot, 1), spread_ref, own)
    width = 512

    def one(step, _):
        at = pl.ds(pl.multiple_of(step * width, width), width)
        if len(out_refs) == 1:
            total = rank_product(wide[:half], right_ref[:, at]) + kept_ref[first : first + half, at]
            total = total + arrived_ref[:, at].astype(jnp.float32)
            out_refs[0][:, at] = total.astype(out_refs[0].dtype)
        else:
            total = rank_product(wide, right_ref[:, at]) + kept_ref[:, at]
            out_refs[0][:, at] = total[:half] + arrived_ref[half:, at].astype(jnp.float32)
            out_refs[1][:, at] = total[half:] + arrived_ref[:half, at].astype(jnp.float32)
        return 0

    lax.fori_loop(0, right_ref.shape[1] // width, one, 0)


def call(kernel, operands, outs, info=None, scratch=(), mib=24):
    vmem = pl.BlockSpec(memory_space=pltpu.VMEM)
    specs = [vmem] * len(operands)
    if info is not None:
        operands, specs = [info] + operands, [pl.BlockSpec(memory_space=pltpu.SMEM)] + specs
    return pl.pallas_call(
        kernel,
        in_specs=specs,
        out_specs=[vmem] * len(outs),
        out_shape=outs,
        scratch_shapes=scratch,
        compiler_params=pltpu.CompilerParams(vmem_limit_bytes=mib * 1024 * 1024),
        cost_estimate=pl.CostEstimate(flops=1000, bytes_accessed=1000, transcendentals=0),
    )(*operands)


def shape(rows, width, dtype=jnp.bfloat16):
    return jax.ShapeDtypeStruct((rows, width), dtype)


def sum_over_mlp(value, bits):
    for bit in bits:
        value = value + lax.ppermute(value, "mlp", [(i, i ^ bit) for i in range(16)])
    return value


def narrow(value):
    return value.astype(jnp.bfloat16)


def wide(value):
    return value.astype(jnp.float32)


def per_device(
    tokens,
    layer_norm_gain,
    layer_norm_bias,
    query_key_weight,
    output_weight,
    up_weight,
    input_bias,
    down_weight,
    output_bias,
    input_adapter_left,
    query_key_value_right,
    up_adapter_right,
    output_adapter_left,
    down_adapter_left,
    output_adapter_right,
    lengths,
    request_adapter,
    slot_adapter,
):
    block = tokens.shape[0]
    model_width = tokens.shape[1]
    pair_rows = 2 * block
    group_rows = SLOTS * pair_rows
    req_count = lax.axis_size("req")
    group = lax.axis_index("req")
    me = lax.axis_index("mlp")
    block_rows = 2 * pair_rows
    table = np.zeros((req_count, 16, 2 + SLOTS * (1 + req_count)), np.int32)
    for g in range(req_count):
        for m in range(16):
            side = 2 * (m % 2) - 1
            steps = [0, 4] + [t for s in (1, 2, 3) for t in (side * s, -side * s)]
            pairs = [RING[(PLACE[m // 2] + t) % 8] for t in steps]
            firsts = [(g - d) * group_rows + p * pair_rows for d in range(req_count) for p in pairs]
            table[g, m] = [m % 2, m] + pairs + firsts
    info = lax.dynamic_slice(jnp.asarray(table), (group, me, 0), (1, 1, table.shape[2])).reshape(-1)

    own = call(
        norm_kernel,
        [tokens, layer_norm_gain.reshape(1, -1), layer_norm_bias.reshape(1, -1)],
        [shape(block, model_width)],
    )[0]
    other = to_partner(own)
    ring_a, ring_b = along_ring(own), along_ring(other)
    pair_left = jnp.concatenate([input_adapter_left, to_partner(input_adapter_left)], axis=1)

    float_lengths = wide(lengths)
    lane = np.arange(128)
    turn_rows = np.zeros((8, 128), np.float32)
    turn_rows[0] = np.exp(lane % ROT // 2 * (-2.0 * math.log(10000.0) / ROT))
    turn_rows[1] = np.where(lane < ROT, 0.0, math.pi / 2)
    turn_rows[2] = np.where(lane < ROT, 1.0, np.where(lane % 2 == 0, -1.0, 1.0))
    token_rows = req_count * group_rows
    token_args = [
        float_lengths[:, None],
        float_lengths[None, :],
        wide(request_adapter)[None, :],
        jnp.asarray(turn_rows),
    ]
    meta, turns = call(token_kernel, token_args, [shape(token_rows, 128, jnp.float32)] * 2, info)

    qkv_rows = query_key_weight.reshape(model_width, 3 * HEAD_SIZE)
    adapter_columns = query_key_value_right.shape[0]
    qkv_right = query_key_value_right.reshape(adapter_columns, 3 * HEAD_SIZE)
    spread_first = spread_table(ADAPTER_RANK, 0, adapter_columns)
    spread_last = spread_table(ADAPTER_RANK, ADAPTER_RANK, adapter_columns)
    near_right = output_adapter_right
    slot_columns = wide(jnp.repeat(slot_adapter, 2 * ADAPTER_RANK))[None, :]
    slot_columns = jnp.concatenate([slot_columns, to_partner(slot_columns)], axis=1)
    own_columns = near_right.shape[0]
    spread_own = spread_table(2 * ADAPTER_RANK, 0, 2 * own_columns)
    hidden_width = up_weight.shape[1]

    def to_group(value, d):
        return lax.ppermute(value, "req", [(g, g + d) for g in range(req_count - d)])

    held = functools.partial(pltpu.VMEM, dtype=jnp.float32)

    def add_ranks(part, first_slot, so_far):
        return call(
            functools.partial(rank_kernel, len(part), first_slot),
            list(part) + [pair_left, meta, slot_columns, spread_own, so_far],
            [shape(32, group_rows)],
            info,
        )[0]

    def products_of(part):
        rows = len(part) * block
        return call(
            functools.partial(base_kernel, len(part)),
            list(part) + [qkv_rows, up_weight],
            [
                shape(rows, 3 * HEAD_SIZE, jnp.float32),
                shape(rows, hidden_width, jnp.float32),
                shape(rows, 2 * HEAD_SIZE),
            ],
        )

    def to_groups(value):
        return [to_group(value, d) for d in range(1, req_count)]

    def arrivals(a, b):
        return a, b, to_partner(b), to_partner(a)

    tie = lax.optimization_barrier
    own_part = (own, other)
    ring_a, meta, turns = tie((ring_a, meta, turns))
    zeroth = products_of(own_part)
    ring_b, zeroth, pair_left = tie((ring_b, zeroth, pair_left))
    part = arrivals(ring_a, ring_b)
    ring_a, ring_b = along_ring(ring_a), along_ring(ring_b)
    ranks = add_ranks(own_part, 0, jnp.zeros((32, group_rows), jnp.bfloat16))
    ranks = add_ranks(part, 2, ranks)
    first = products_of(part)
    ring_b, ranks, first = tie((ring_b, ranks, first))
    part = arrivals(ring_a, ring_b)
    ring_a, ring_b = along_ring(ring_a), along_ring(ring_b)
    far_right = to_partner(near_right)
    far_early = to_groups(jnp.concatenate([zeroth[2], first[2]], axis=0))
    ranks = add_ranks(part, 4, ranks)
    second = products_of(part)
    ring_b, ranks, second, far_right, far_early = tie((ring_b, ranks, second, far_right, far_early))
    far_middle = to_groups(second[2])
    part = arrivals(ring_a, ring_b)
    ring_a = along_ring(ring_a)
    ranks = add_ranks(part, 6, ranks)
    third = products_of(part)
    ring_a, ranks, third, far_middle = tie((ring_a, ranks, third, far_middle))
    part = (ring_a, to_partner(ring_a))
    ranks = add_ranks(part, 1, ranks)
    moved = lax.ppermute(ranks, "mlp", [(i, i ^ 2) for i in range(16)])
    fourth = products_of(part)
    ranks, fourth = tie((ranks + moved, fourth))
    far_late = to_groups(jnp.concatenate([third[2], fourth[2]], axis=0))
    rank_in = sum_over_mlp(ranks, (4, 8))
    products = (zeroth, first, second, third, fourth)

    bias_row = input_bias.reshape(1, -1)
    far_rank = to_groups(rank_in)
    queries, own_keys, own_values, hidden, hidden_rank = call(
        inner_kernel,
        [part[0] for part in products]
        + [part[1] for part in products]
        + [rank_in, meta, turns, spread_first, spread_last]
        + [qkv_right, up_adapter_right, bias_row, down_adapter_left],
        [shape(group_rows, HEAD_SIZE)] * 3 + [shape(group_rows, hidden_width), shape(32, group_rows)],
        info,
    )
    keys, values = [own_keys], [own_values]
    for d in range(1, req_count):
        early, late = far_early[d - 1], far_late[d - 1]
        shared = [early[:pair_rows], early[pair_rows:], far_middle[d - 1]]
        shared += [late[:block_rows], late[block_rows:]]
        far_keys, far_values = call(
            functools.partial(far_kernel, d * group_rows),
            shared + [far_rank[d - 1], meta, turns, spread_first, qkv_right],
            [shape(group_rows, HEAD_SIZE)] * 2,
            info,
        )
        keys.append(far_keys)
        values.append(far_values)

    output_left = output_adapter_left.reshape(HEAD_SIZE, adapter_columns)
    attended, rank_out = call(
        functools.partial(attention_kernel, req_count),
        [queries] + keys + values + [meta, spread_first, output_left, hidden_rank],
        [shape(group_rows, HEAD_SIZE), shape(32, group_rows)],
        info,
        [
            held((block_rows, 128)),
            held((block_rows, 128)),
            held((block_rows, HEAD_SIZE)),
            held((32, group_rows)),
        ],
    )
    output_rows = output_weight.reshape(HEAD_SIZE, model_width)

    def main(k, attended, hidden):
        sent = block if k == 0 else pair_rows
        return call(
            functools.partial(main_kernel, k),
            [attended, hidden, output_rows, down_weight],
            [shape(block_rows - sent, model_width, jnp.float32), shape(sent, model_width)],
        )

    kept, arrived, before = {}, {}, None
    for bit, k in zip((1, 2, 4, 8), (0, 3, 2, 1)):
        moved = lax.ppermute(rank_out, "mlp", [(i, i ^ bit) for i in range(16)])
        kept[k], sent = main(k, attended, hidden)
        rank_out, attended, sent = tie((rank_out + moved, attended, sent))
        if before is not None:
            rank_out, arrived[before] = tie((rank_out, arrived[before]))
        arrived[k], before = to_partner(sent), k

    pair_right = jnp.concatenate([near_right, far_right], axis=0)

    def adapt(slot, half, kept, first, arrived):
        if half:
            outs = [shape(block, model_width, jnp.bfloat16 if slot else jnp.float32)]
        else:
            outs = [shape(block, model_width, jnp.float32)] * 2
        return call(
            functools.partial(adapt_kernel, slot, first),
            [rank_out, meta, spread_own, pair_right, kept, arrived],
            outs,
            info,
        )

    chain_a = along_ring(adapt(1, True, kept[0], 2 * block, arrived[0])[0])
    chain_b = None
    for s in (3, 2, 1):
        add_a, add_b = adapt(2 * s + 1, False, kept[s], 0, arrived[s])
        if chain_b is None:
            chain_b = along_ring(narrow(add_b))
            chain_a = along_ring(narrow(wide(chain_a) + add_a))
        else:
            chain_a = along_ring(narrow(wide(chain_a) + add_a))
            chain_b = along_ring(narrow(wide(chain_b) + add_b))
    arrived = to_partner(narrow(wide(chain_b) + kept[0][block : 2 * block]))
    total = adapt(0, True, kept[0], 0, chain_a)[0] + wide(arrived)
    return narrow(total + wide(tokens) + output_bias)


def solution(mesh):
    in_specs = (
        P(("req", "mlp"), None),
        P(),
        P(),
        P(None, "mlp", None),
        P("mlp", None, None),
        P(None, "mlp"),
        P("mlp"),
        P("mlp", None),
        P(),
        P(None, "mlp"),
        P(None, "mlp", None),
        P(None, "mlp"),
        P("mlp", None, None),
        P("mlp", None),
        P("mlp", None),
        P(),
        P(),
        P("mlp"),
    )
    out_specs = P(("req", "mlp"), None)
    return jax.shard_map(
        per_device, mesh=mesh, in_specs=in_specs, out_specs=out_specs, check_vma=False
    )
```

```python
import functools
import math

import jax
import jax.numpy as jnp
import numpy as np
from jax import lax
from jax.experimental import pallas as pl
from jax.experimental.pallas import tpu as pltpu
from jax.sharding import PartitionSpec as P

HEAD_SIZE = 256
ROT = 64
ADAPTER_RANK = 16
EPSILON = 1e-05
NEGATIVE_FILL = -1e30
RING = (0, 2, 4, 6, 7, 5, 3, 1)
PLACE = tuple(RING.index(pair) for pair in range(8))
CORE_PERM = [(i, i ^ 1) for i in range(16)]
RING_PERM = [(RING[i] * 2, RING[(i + 1) % 8] * 2) for i in range(8)] + [
    (RING[i] * 2 + 1, RING[(i - 1) % 8] * 2 + 1) for i in range(8)
]
SLOTS = 8
BLOCKS = 4
CORE, MLP, PAIRS, BASES = 0, 1, 2, 2 + SLOTS


def to_partner(value):
    return lax.ppermute(value, "mlp", CORE_PERM)


def along_ring(value):
    return lax.ppermute(value, "mlp", RING_PERM)


def rank_product(left_side, right_side):
    return jnp.dot(left_side, right_side, preferred_element_type=jnp.float32)


def across(left_side, right_side):
    return lax.dot_general(
        left_side, right_side, (((1,), (1,)), ((), ())), preferred_element_type=jnp.float32
    )


def spread_table(period, first, width):
    row = np.arange(32)[:, None]
    column = np.arange(width)[None, :]
    return jnp.asarray((row - first == column % period).astype(np.float32), jnp.bfloat16)


def swap_halves(info, lanes):
    half = lanes.shape[1] // 2
    return jnp.where(info[CORE] == 1, pltpu.roll(lanes, half, 1), lanes)


def lane_ids(shape, period):
    return (lax.broadcasted_iota(jnp.int32, shape, 1) // period).astype(jnp.float32)


def pair_at(info, slot, rows):
    return pl.ds(pl.multiple_of(info[PAIRS + slot] * rows, rows), rows)


def store_lanes(info, out_ref, lanes, slots):
    width = out_ref.shape[1] // SLOTS
    for k, slot in enumerate(slots):
        part = lanes[:, k * width : (k + 1) * width]
        out_ref[:, pair_at(info, slot, width)] = swap_halves(info, part).astype(out_ref.dtype)


def rank_rows(info, rank_ref, slot, count):
    width = rank_ref.shape[1] // SLOTS
    lanes = [
        swap_halves(info, rank_ref[:, pair_at(info, slot + k, width)].astype(jnp.float32))
        for k in range(count)
    ]
    lanes = lanes[0] if count == 1 else jnp.concatenate(lanes, axis=1)
    return jnp.transpose(lanes).astype(jnp.bfloat16)


def widened(rows, spread_ref, own):
    return jnp.where(own, rank_product(rows, spread_ref[...]), 0.0).astype(jnp.bfloat16)


def cosine(angle):
    turns = jnp.floor(angle * (1.0 / math.pi) + 0.5)
    rest = ((angle - turns * 3.140625) - turns * 9.67502593994140625e-4) - turns * 1.509957990978376e-7
    square = rest * rest
    value = jnp.full_like(square, 1.0 / 479001600.0)
    for factor in (-1.0 / 3628800.0, 1.0 / 40320.0, -1.0 / 720.0, 1.0 / 24.0, -0.5, 1.0):
        value = value * square + factor
    odd = turns - 2.0 * jnp.floor(turns * 0.5)
    return value * (1.0 - 2.0 * odd)


def norm_kernel(x_ref, gain_ref, bias_ref, out_ref):
    values = x_ref[...].astype(jnp.float32)
    center = values - jnp.mean(values, axis=1, keepdims=True)
    spread = jnp.mean(center * center, axis=1, keepdims=True)
    scaled = center * lax.rsqrt(spread + EPSILON)
    out_ref[...] = (scaled * gain_ref[...] + bias_ref[...]).astype(out_ref.dtype)


def local_tokens(info, slot, shape, dim):
    rows = shape[dim] // 2
    at = lax.broadcasted_iota(jnp.int32, shape, dim)
    second = at >= rows
    at = jnp.where(second, at - rows, at) + info[CORE] * (rows // 2)
    at = jnp.where(at >= rows, at - rows, at)
    return (at + jnp.where(second, info[BASES + slot + 1], info[BASES + slot])).astype(jnp.float32)


def token_kernel(info, column_ref, row_ref, ids_ref, table_ref, meta_ref, turn_ref):
    rows = 2 * 128
    count = row_ref.shape[1]
    earlier = lax.broadcasted_iota(jnp.int32, (count, count), 0) < lax.broadcasted_iota(
        jnp.int32, (count, count), 1
    )
    anchors = jnp.sum(jnp.where(earlier, column_ref[...], 0.0), axis=0, keepdims=True)
    endings = anchors + row_ref[...]
    ids = ids_ref[...]
    lane = lax.broadcasted_iota(jnp.int32, (rows, 128), 1)

    def one(block, _):
        token = local_tokens(info, 2 * block, (rows, 1), 0)
        inside = jnp.logical_and(anchors <= token, token < endings)
        start = jnp.sum(jnp.where(inside, anchors, 0.0), axis=1, keepdims=True)
        adapter = jnp.sum(jnp.where(inside, ids, 0.0), axis=1, keepdims=True)
        at = pl.ds(pl.multiple_of(block * rows, rows), rows)
        meta_ref[at, :] = jnp.where(lane < 64, start, adapter)
        angle = (token - start) * table_ref[0:1, :] - table_ref[1:2, :]
        turn_ref[at, :] = cosine(angle) * table_ref[2:3, :]
        return 0

    lax.fori_loop(0, meta_ref.shape[0] // rows, one, 0)


def rank_kernel(count, slots, info, *refs):
    x = jnp.concatenate([ref[...] for ref in refs[:count]], axis=0)
    left_ref, meta_ref, slot_ref, fold_ref, held_ref, out_ref = refs[count:]
    products = rank_product(x, left_ref[...])
    adapter = jnp.concatenate([meta_ref[k * 128 : (k + 1) * 128, 64:65] for k in slots], axis=0)
    chosen = jnp.where(slot_ref[...] == adapter, products, 0.0).astype(jnp.bfloat16)
    out_ref[...] = held_ref[...]
    store_lanes(info, out_ref, across(fold_ref[...], chosen), slots)


def base_kernel(count, *refs):
    x = jnp.concatenate([ref[...] for ref in refs[:count]], axis=0)
    qkv_ref, up_ref, base_ref, up_base_ref, shared_ref = refs[count:]
    first = rank_product(x, qkv_ref[...])
    base_ref[...] = first
    shared_ref[...] = first[:, HEAD_SIZE:].astype(shared_ref.dtype)
    up_base_ref[...] = rank_product(x, up_ref[...])


def turn(part, table):
    width = table.shape[1]
    lane = lax.broadcasted_iota(jnp.int32, table.shape, 1)
    cos = jnp.where(lane < ROT, table, 1.0)
    sin = jnp.where(lane < ROT, pltpu.roll(table, width - ROT, 1), 0.0)
    head = part[:, :width]
    swapped = jnp.where(
        lane % 2 == 0, pltpu.roll(head, width - 1, 1), pltpu.roll(head, 1, 1)
    )
    return jnp.concatenate([head * cos + swapped * sin, part[:, width:]], axis=1)


def block_rows_of(refs, block):
    if block == 0:
        return jnp.concatenate([refs[0][:128], refs[3][128:]], axis=0)
    if block == 3:
        return jnp.concatenate([refs[2][...], refs[3][:128]], axis=0)
    return refs[0][128:] if block == 1 else refs[1][...]


def inner_kernel(info, *refs):
    base_refs, up_refs, (rank_ref, meta_ref, turn_ref, first_ref, last_ref) = refs[:4], refs[4:8], refs[8:13]
    qkv_right_ref, up_right_ref, bias_ref, left_ref = refs[13:17]
    q_ref, k_ref, v_ref, hidden_ref, out_ref = refs[17:]
    rows = 256
    column_id = lane_ids((rows, first_ref.shape[1]), ADAPTER_RANK)
    for block in range(BLOCKS):
        at = slice(block * rows, (block + 1) * rows)
        own = column_id == meta_ref[at, 64:65]
        ranks = rank_rows(info, rank_ref, 2 * block, 2)
        total = block_rows_of(base_refs, block) + rank_product(
            widened(ranks, first_ref, own), qkv_right_ref[...]
        )
        table = turn_ref[at, :]
        q_ref[at, :] = (turn(total[:, :HEAD_SIZE], table) * HEAD_SIZE ** (-0.5)).astype(jnp.bfloat16)
        k_ref[at, :] = turn(total[:, HEAD_SIZE : 2 * HEAD_SIZE], table).astype(jnp.bfloat16)
        v_ref[at, :] = total[:, 2 * HEAD_SIZE :].astype(jnp.bfloat16)
        x = block_rows_of(up_refs, block) + rank_product(widened(ranks, last_ref, own), up_right_ref[...])
        x = x + bias_ref[...]
        inner = math.sqrt(2.0 / math.pi) * (x + 0.044715 * (x * x * x))
        hidden = (0.5 * x * (1.0 + jnp.tanh(inner))).astype(jnp.bfloat16)
        hidden_ref[at, :] = hidden
        chosen = jnp.where(own, rank_product(hidden, left_ref[...]), 0.0).astype(jnp.bfloat16)
        store_lanes(info, out_ref, across(last_ref[...], chosen), (2 * block, 2 * block + 1))


def far_kernel(first_row, info, *refs):
    shared_refs, (rank_ref, meta_ref, turn_ref, spread_ref, right_ref, k_ref, v_ref) = refs[:4], refs[4:]
    rows = 256
    column_id = lane_ids((rows, spread_ref.shape[1]), ADAPTER_RANK)
    for block in range(BLOCKS):
        at = slice(block * rows, (block + 1) * rows)
        far_at = slice(first_row + block * rows, first_row + (block + 1) * rows)
        own = column_id == meta_ref[far_at, 64:65]
        wide = widened(rank_rows(info, rank_ref, 2 * block, 2), spread_ref, own)
        total = block_rows_of(shared_refs, block).astype(jnp.float32)
        total = total + rank_product(wide, right_ref[:, HEAD_SIZE:])
        k_ref[at, :] = turn(total[:, :HEAD_SIZE], turn_ref[far_at, :]).astype(jnp.bfloat16)
        v_ref[at, :] = total[:, HEAD_SIZE:].astype(jnp.bfloat16)


def attention_kernel(req_count, info, *refs):
    q_ref, refs = refs[0], refs[1:]
    key_refs, value_refs, refs = refs[:req_count], refs[req_count : 2 * req_count], refs[2 * req_count :]
    meta_ref, spread_ref, left_ref, hidden_rank_ref, attended_ref, out_ref = refs[:6]
    top_ref, sum_ref, acc_ref, fold_ref = refs[6:]
    rows = 256
    pair = rows // 2
    column_id = lane_ids((rows, left_ref.shape[1]), ADAPTER_RANK)

    def twice(lanes):
        return jnp.concatenate([lanes] * (HEAD_SIZE // lanes.shape[1]), axis=1)

    def one(block, _):
        at = pl.ds(pl.multiple_of(block * rows, rows), rows)
        start = meta_ref[at, 0:1]
        query = local_tokens(info, 2 * block, (rows, 1), 0)
        q = q_ref[at, :]

        def scores_of(d):
            scores = across(q, key_refs[d][...])
            key = jnp.concatenate(
                [local_tokens(info, d * SLOTS + k, (1, rows), 1) for k in range(0, SLOTS, 2)], axis=1
            )
            allowed = jnp.logical_and(key <= query, key >= start)
            return jnp.where(allowed, scores, NEGATIVE_FILL), allowed

        scores, _ = scores_of(0)
        top = jnp.max(scores, axis=1, keepdims=True)
        weights = jnp.exp(scores - top)
        top_ref[...] = jnp.broadcast_to(top, top_ref.shape)
        sum_ref[...] = jnp.broadcast_to(jnp.sum(weights, axis=1, keepdims=True), sum_ref.shape)
        acc_ref[...] = rank_product(weights.astype(jnp.bfloat16), value_refs[0][...])
        lowest = jnp.min(start)
        for d in range(1, req_count):
            highest = info[BASES + d * SLOTS] + pair
            for k in range(1, SLOTS):
                highest = jnp.maximum(highest, info[BASES + d * SLOTS + k] + pair)

            @pl.when(highest.astype(jnp.float32) > lowest)
            def _(d=d):
                scores, allowed = scores_of(d)
                top = top_ref[...]
                new_top = jnp.maximum(top, jnp.max(scores, axis=1, keepdims=True))
                weights = jnp.where(allowed, jnp.exp(scores - new_top[:, 0:1]), 0.0)
                scale = jnp.exp(top - new_top)
                top_ref[...] = new_top
                sum_ref[...] = sum_ref[...] * scale + jnp.sum(weights, axis=1, keepdims=True)
                acc_ref[...] = acc_ref[...] * twice(scale) + rank_product(
                    weights.astype(jnp.bfloat16), value_refs[d][...]
                )

        attended = (acc_ref[...] / twice(sum_ref[...])).astype(jnp.bfloat16)
        attended_ref[at, :] = attended
        chosen = jnp.where(column_id == meta_ref[at, 64:65], rank_product(attended, left_ref[...]), 0.0)
        store_lanes(
            info, fold_ref, across(spread_ref[...], chosen.astype(jnp.bfloat16)), (2 * block, 2 * block + 1)
        )
        return 0

    lax.fori_loop(0, BLOCKS, one, 0)
    out_ref[...] = (fold_ref[...] + hidden_rank_ref[...].astype(jnp.float32)).astype(out_ref.dtype)


def main_kernel(block, attended_ref, hidden_ref, output_ref, down_ref, kept_ref, sent_ref):
    rows = 256
    sent = sent_ref.shape[0]
    width = 512
    attended = attended_ref[block * rows : (block + 1) * rows, :]
    hidden = hidden_ref[block * rows : (block + 1) * rows, :]

    def one(step, _):
        at = pl.ds(pl.multiple_of(step * width, width), width)
        total = rank_product(attended, output_ref[:, at]) + rank_product(hidden, down_ref[:, at])
        if block:
            sent_ref[:, at] = total[:sent].astype(sent_ref.dtype)
            kept_ref[:, at] = total[sent:]
        else:
            kept_ref[:, at] = total[: rows - sent]
            sent_ref[:, at] = total[rows - sent :].astype(sent_ref.dtype)
        return 0

    lax.fori_loop(0, output_ref.shape[1] // width, one, 0)


def adapt_kernel(slot, first, info, rank_ref, meta_ref, spread_ref, right_ref, kept_ref, arrived_ref, *out_refs):
    pair = 128
    half = pair // 2
    columns = spread_ref.shape[1]
    count = columns // (4 * ADAPTER_RANK)
    column_id = lax.broadcasted_iota(jnp.int32, (pair, columns), 1) // (2 * ADAPTER_RANK)
    partner = info[MLP] + 1 - 2 * info[CORE]
    column_id = column_id + jnp.where(column_id < count, info[MLP] * count, (partner - 1) * count)
    own = column_id.astype(jnp.float32) == meta_ref[slot * pair : (slot + 1) * pair, 64:65]
    wide = widened(rank_rows(info, rank_ref, slot, 1), spread_ref, own)
    width = 512

    def one(step, _):
        at = pl.ds(pl.multiple_of(step * width, width), width)
        if len(out_refs) == 1:
            total = rank_product(wide[:half], right_ref[:, at]) + kept_ref[first : first + half, at]
            total = total + arrived_ref[:, at].astype(jnp.float32)
            out_refs[0][:, at] = total.astype(out_refs[0].dtype)
        else:
            total = rank_product(wide, right_ref[:, at]) + kept_ref[:, at]
            out_refs[0][:, at] = total[:half] + arrived_ref[half:, at].astype(jnp.float32)
            out_refs[1][:, at] = total[half:] + arrived_ref[:half, at].astype(jnp.float32)
        return 0

    lax.fori_loop(0, right_ref.shape[1] // width, one, 0)


def call(kernel, operands, outs, info=None, scratch=(), mib=24, flops=1000):
    vmem = pl.BlockSpec(memory_space=pltpu.VMEM)
    specs = [vmem] * len(operands)
    if info is not None:
        operands, specs = [info] + operands, [pl.BlockSpec(memory_space=pltpu.SMEM)] + specs
    return pl.pallas_call(
        kernel,
        in_specs=specs,
        out_specs=[vmem] * len(outs),
        out_shape=outs,
        scratch_shapes=scratch,
        compiler_params=pltpu.CompilerParams(vmem_limit_bytes=mib * 1024 * 1024),
        cost_estimate=pl.CostEstimate(flops=flops, bytes_accessed=1000, transcendentals=0),
    )(*operands)


def shape(rows, width, dtype=jnp.bfloat16):
    return jax.ShapeDtypeStruct((rows, width), dtype)


def sum_over_mlp(value, bits):
    for bit in bits:
        value = value + lax.ppermute(value, "mlp", [(i, i ^ bit) for i in range(16)])
    return value


def narrow(value):
    return value.astype(jnp.bfloat16)


def wide(value):
    return value.astype(jnp.float32)


def per_device(
    tokens,
    layer_norm_gain,
    layer_norm_bias,
    query_key_weight,
    output_weight,
    up_weight,
    input_bias,
    down_weight,
    output_bias,
    input_adapter_left,
    query_key_value_right,
    up_adapter_right,
    output_adapter_left,
    down_adapter_left,
    output_adapter_right,
    lengths,
    request_adapter,
    slot_adapter,
):
    block = tokens.shape[0]
    model_width = tokens.shape[1]
    pair_rows = 2 * block
    group_rows = SLOTS * pair_rows
    req_count = lax.axis_size("req")
    group = lax.axis_index("req")
    me = lax.axis_index("mlp")
    block_rows = 2 * pair_rows
    table = np.zeros((req_count, 16, 2 + SLOTS * (1 + req_count)), np.int32)
    for g in range(req_count):
        for m in range(16):
            side = 2 * (m % 2) - 1
            steps = [0, 4] + [t for s in (1, 2, 3) for t in (side * s, -side * s)]
            pairs = [RING[(PLACE[m // 2] + t) % 8] for t in steps]
            firsts = [(g - d) * group_rows + p * pair_rows for d in range(req_count) for p in pairs]
            table[g, m] = [m % 2, m] + pairs + firsts
    info = lax.dynamic_slice(jnp.asarray(table), (group, me, 0), (1, 1, table.shape[2])).reshape(-1)

    own = call(
        norm_kernel,
        [tokens, layer_norm_gain.reshape(1, -1), layer_norm_bias.reshape(1, -1)],
        [shape(block, model_width)],
    )[0]
    other = to_partner(own)
    ring_a, ring_b = along_ring(own), along_ring(other)
    pair_left = jnp.concatenate([input_adapter_left, to_partner(input_adapter_left)], axis=1)

    float_lengths = wide(lengths)
    lane = np.arange(128)
    turn_rows = np.zeros((8, 128), np.float32)
    turn_rows[0] = np.exp(lane % ROT // 2 * (-2.0 * math.log(10000.0) / ROT))
    turn_rows[1] = np.where(lane < ROT, 0.0, math.pi / 2)
    turn_rows[2] = np.where(lane < ROT, 1.0, np.where(lane % 2 == 0, -1.0, 1.0))
    token_rows = req_count * group_rows
    token_args = [
        float_lengths[:, None],
        float_lengths[None, :],
        wide(request_adapter)[None, :],
        jnp.asarray(turn_rows),
    ]
    meta, turns = call(token_kernel, token_args, [shape(token_rows, 128, jnp.float32)] * 2, info)

    qkv_rows = query_key_weight.reshape(model_width, 3 * HEAD_SIZE)
    adapter_columns = query_key_value_right.shape[0]
    qkv_right = query_key_value_right.reshape(adapter_columns, 3 * HEAD_SIZE)
    spread_first = spread_table(ADAPTER_RANK, 0, adapter_columns)
    spread_last = spread_table(ADAPTER_RANK, ADAPTER_RANK, adapter_columns)
    near_right = output_adapter_right
    slot_columns = wide(jnp.repeat(slot_adapter, 2 * ADAPTER_RANK))[None, :]
    slot_columns = jnp.concatenate([slot_columns, to_partner(slot_columns)], axis=1)
    own_columns = near_right.shape[0]
    spread_own = spread_table(2 * ADAPTER_RANK, 0, 2 * own_columns)
    hidden_width = up_weight.shape[1]

    def to_group(value, d):
        return lax.ppermute(value, "req", [(g, g + d) for g in range(req_count - d)])

    held = functools.partial(pltpu.VMEM, dtype=jnp.float32)

    def add_ranks(part, slots, so_far):
        return call(
            functools.partial(rank_kernel, len(part), slots),
            list(part) + [pair_left, meta, slot_columns, spread_own, so_far],
            [shape(32, group_rows)],
            info,
        )[0]

    def products_of(part, flops=1000):
        rows = len(part) * block
        return call(
            functools.partial(base_kernel, len(part)),
            list(part) + [qkv_rows, up_weight],
            [
                shape(rows, 3 * HEAD_SIZE, jnp.float32),
                shape(rows, hidden_width, jnp.float32),
                shape(rows, 2 * HEAD_SIZE),
            ],
            flops=flops,
        )

    def to_groups(value):
        return [to_group(value, d) for d in range(1, req_count)]

    def arrivals(a, b):
        return a, b, to_partner(b), to_partner(a)

    tie = lax.optimization_barrier
    own_part = (own, other)
    ring_a, meta, turns, pair_left = tie((ring_a, meta, turns, pair_left))
    ranks = add_ranks(own_part, (0,), jnp.zeros((32, group_rows), jnp.bfloat16))
    ring_b, ranks = tie((ring_b, ranks))
    part = arrivals(ring_a, ring_b)
    ring_a, ring_b = along_ring(ring_a), along_ring(ring_b)
    ranks = add_ranks(part, (2, 3), ranks)
    first = products_of(own_part + part)
    ring_b, ranks, first = tie((ring_b, ranks, first))
    part = arrivals(ring_a, ring_b)
    ring_a, ring_b = along_ring(ring_a), along_ring(ring_b)
    far_right = to_partner(near_right)
    far_early = to_groups(first[2])
    ranks = add_ranks(part, (4, 5), ranks)
    second = products_of(part)
    ring_b, ranks, second, far_right = tie((ring_b, ranks, second, far_right))
    part = arrivals(ring_a, ring_b)
    ring_a = along_ring(ring_a)
    third = products_of(part[:2], 2000000000)
    ranks = add_ranks(part[:2], (6,), ranks)
    ring_a, ranks, third = tie((ring_a, ranks, third))
    part = part[2:] + (ring_a, to_partner(ring_a))
    ranks = add_ranks(part, (7, 1), ranks)
    moved = lax.ppermute(ranks, "mlp", [(i, i ^ 2) for i in range(16)])
    fourth = products_of(part)
    ranks, fourth, far_early = tie((ranks + moved, fourth, far_early))
    far_middle = to_groups(second[2])
    far_late = to_groups(jnp.concatenate([third[2], fourth[2]], axis=0))
    rank_in = sum_over_mlp(ranks, (4, 8))
    products = (first, second, third, fourth)

    bias_row = input_bias.reshape(1, -1)
    far_rank = to_groups(rank_in)
    queries, own_keys, own_values, hidden, hidden_rank = call(
        inner_kernel,
        [part[0] for part in products]
        + [part[1] for part in products]
        + [rank_in, meta, turns, spread_first, spread_last]
        + [qkv_right, up_adapter_right, bias_row, down_adapter_left],
        [shape(group_rows, HEAD_SIZE)] * 3 + [shape(group_rows, hidden_width), shape(32, group_rows)],
        info,
    )
    keys, values = [own_keys], [own_values]
    for d in range(1, req_count):
        early, late = far_early[d - 1], far_late[d - 1]
        shared = [early, far_middle[d - 1], late[:pair_rows], late[pair_rows:]]
        far_keys, far_values = call(
            functools.partial(far_kernel, d * group_rows),
            shared + [far_rank[d - 1], meta, turns, spread_first, qkv_right],
            [shape(group_rows, HEAD_SIZE)] * 2,
            info,
        )
        keys.append(far_keys)
        values.append(far_values)

    output_left = output_adapter_left.reshape(HEAD_SIZE, adapter_columns)
    attended, rank_out = call(
        functools.partial(attention_kernel, req_count),
        [queries] + keys + values + [meta, spread_first, output_left, hidden_rank],
        [shape(group_rows, HEAD_SIZE), shape(32, group_rows)],
        info,
        [
            held((block_rows, 128)),
            held((block_rows, 128)),
            held((block_rows, HEAD_SIZE)),
            held((32, group_rows)),
        ],
    )
    output_rows = output_weight.reshape(HEAD_SIZE, model_width)

    def main(k, attended, hidden):
        sent = block if k == 0 else pair_rows
        return call(
            functools.partial(main_kernel, k),
            [attended, hidden, output_rows, down_weight],
            [shape(block_rows - sent, model_width, jnp.float32), shape(sent, model_width)],
        )

    kept, arrived, sent = {}, {}, {}
    for bit, k in zip((1, 2, 4, 8), (0, 3, 2, 1)):
        moved = lax.ppermute(rank_out, "mlp", [(i, i ^ bit) for i in range(16)])
        kept[k], sent[k] = main(k, attended, hidden)
        rank_out, attended, kept[k], sent[k] = tie((rank_out + moved, attended, kept[k], sent[k]))
        if k == 0:
            arrived[k] = to_partner(sent[k])
        if bit == 4:
            arrived[3] = to_partner(sent[3])
            rank_out, arrived[0] = tie((rank_out, arrived[0]))
    rank_out, arrived[3] = tie((rank_out, arrived[3]))
    pair_right = jnp.concatenate([near_right, far_right], axis=0)

    def adapt(slot, half, kept, first, arrived):
        if half:
            outs = [shape(block, model_width, jnp.bfloat16 if slot else jnp.float32)]
        else:
            outs = [shape(block, model_width, jnp.float32)] * 2
        return call(
            functools.partial(adapt_kernel, slot, first),
            [rank_out, meta, spread_own, pair_right, kept, arrived],
            outs,
            info,
        )

    chain_a = along_ring(adapt(1, True, kept[0], 2 * block, arrived[0])[0])
    chain_b = None
    for s in (3, 2, 1):
        add_a, add_b = adapt(2 * s + 1, False, kept[s], 0, arrived[s])
        if s > 1:
            arrived[s - 1] = to_partner(sent[s - 1])
        if chain_b is None:
            chain_b = along_ring(narrow(add_b))
            chain_a = along_ring(narrow(wide(chain_a) + add_a))
        else:
            chain_a = along_ring(narrow(wide(chain_a) + add_a))
            chain_b = along_ring(narrow(wide(chain_b) + add_b))
    own_sum = adapt(0, True, kept[0], 0, tokens)[0]
    chain_a, own_sum = tie((chain_a, own_sum))
    arrived_last = to_partner(narrow(wide(chain_b) + kept[0][block : 2 * block]))
    return narrow(wide(chain_a) + wide(arrived_last) + own_sum + output_bias)


def solution(mesh):
    in_specs = (
        P(("req", "mlp"), None),
        P(),
        P(),
        P(None, "mlp", None),
        P("mlp", None, None),
        P(None, "mlp"),
        P("mlp"),
        P("mlp", None),
        P(),
        P(None, "mlp"),
        P(None, "mlp", None),
        P(None, "mlp"),
        P("mlp", None, None),
        P("mlp", None),
        P("mlp", None),
        P(),
        P(),
        P("mlp"),
    )
    out_specs = P(("req", "mlp"), None)
    return jax.shard_map(
        per_device, mesh=mesh, in_specs=in_specs, out_specs=out_specs, check_vma=False
    )
```

```python
import functools
import math

import jax
import jax.numpy as jnp
import numpy as np
from jax import lax
from jax.experimental import pallas as pl
from jax.experimental.pallas import tpu as pltpu
from jax.sharding import PartitionSpec as P

HEAD_SIZE = 256
ROT = 64
ADAPTER_RANK = 16
EPSILON = 1e-05
NEGATIVE_FILL = -1e30
RING = (0, 2, 4, 6, 7, 5, 3, 1)
PLACE = tuple(RING.index(pair) for pair in range(8))
CORE_PERM = [(i, i ^ 1) for i in range(16)]
RING_PERM = [(RING[i] * 2, RING[(i + 1) % 8] * 2) for i in range(8)] + [
    (RING[i] * 2 + 1, RING[(i - 1) % 8] * 2 + 1) for i in range(8)
]
SLOTS = 8
BLOCKS = 4
CORE, MLP, PAIRS, PLACES, BASES = 0, 1, 2, 2 + SLOTS, 2 + 2 * SLOTS


def to_partner(value):
    return lax.ppermute(value, "mlp", CORE_PERM)


def along_ring(value):
    return lax.ppermute(value, "mlp", RING_PERM)


def rank_product(left_side, right_side):
    return jnp.dot(left_side, right_side, preferred_element_type=jnp.float32)


def across(left_side, right_side):
    return lax.dot_general(
        left_side, right_side, (((1,), (1,)), ((), ())), preferred_element_type=jnp.float32
    )


def spread_table(period, first, width):
    row = np.arange(32)[:, None]
    column = np.arange(width)[None, :]
    return jnp.asarray((row - first == column % period).astype(np.float32), jnp.bfloat16)


def swap_halves(info, lanes):
    half = lanes.shape[1] // 2
    return jnp.where(info[CORE] == 1, pltpu.roll(lanes, half, 1), lanes)


def lane_ids(shape, period):
    return (lax.broadcasted_iota(jnp.int32, shape, 1) // period).astype(jnp.float32)


def pair_at(info, slot, rows):
    return pl.ds(pl.multiple_of(info[PAIRS + slot] * rows, rows), rows)


def store_lanes(info, out_ref, lanes, slots):
    width = out_ref.shape[1] // SLOTS
    for k, slot in enumerate(slots):
        part = lanes[:, k * width : (k + 1) * width]
        out_ref[:, pair_at(info, slot, width)] = swap_halves(info, part).astype(out_ref.dtype)


def rank_rows(info, rank_ref, slot, count):
    width = rank_ref.shape[1] // SLOTS
    lanes = [
        swap_halves(info, rank_ref[:, pair_at(info, slot + k, width)].astype(jnp.float32))
        for k in range(count)
    ]
    lanes = lanes[0] if count == 1 else jnp.concatenate(lanes, axis=1)
    return jnp.transpose(lanes).astype(jnp.bfloat16)


def widened(rows, spread_ref, adapter, columns):
    tile = rank_product(rows, spread_ref[...]).astype(jnp.bfloat16)
    group = lax.broadcasted_iota(jnp.int32, tile.shape, 1) // ADAPTER_RANK
    apart = (adapter - group.astype(jnp.float32)).astype(jnp.bfloat16)
    step = tile.shape[1] // ADAPTER_RANK
    zero = jnp.zeros_like(tile)
    return jnp.concatenate(
        [jnp.where(apart == first, tile, zero) for first in range(0, columns // ADAPTER_RANK, step)], axis=1
    )


def folded(products, adapter, spread_ref):
    width = spread_ref.shape[1]
    group = lax.broadcasted_iota(jnp.int32, (products.shape[0], width), 1) // ADAPTER_RANK
    apart = adapter - group.astype(jnp.float32)
    total = None
    for first in range(0, products.shape[1], width):
        part = products[:, first : first + width]
        part = jnp.where(apart == float(first // ADAPTER_RANK), part, 0.0)
        total = part if total is None else total + part
    return across(spread_ref[...], total.astype(jnp.bfloat16))


def cosine(angle):
    turns = jnp.floor(angle * (1.0 / math.pi) + 0.5)
    rest = ((angle - turns * 3.140625) - turns * 9.67502593994140625e-4) - turns * 1.509957990978376e-7
    square = rest * rest
    value = jnp.full_like(square, 1.0 / 479001600.0)
    for factor in (-1.0 / 3628800.0, 1.0 / 40320.0, -1.0 / 720.0, 1.0 / 24.0, -0.5, 1.0):
        value = value * square + factor
    odd = turns - 2.0 * jnp.floor(turns * 0.5)
    return value * (1.0 - 2.0 * odd)


def norm_kernel(x_ref, gain_ref, bias_ref, out_ref):
    values = x_ref[...].astype(jnp.float32)
    center = values - jnp.mean(values, axis=1, keepdims=True)
    spread = jnp.mean(center * center, axis=1, keepdims=True)
    scaled = center * lax.rsqrt(spread + EPSILON)
    out_ref[...] = (scaled * gain_ref[...] + bias_ref[...]).astype(out_ref.dtype)


def local_tokens(info, slot, shape, dim):
    rows = shape[dim] // 2
    at = lax.broadcasted_iota(jnp.int32, shape, dim)
    second = at >= rows
    at = jnp.where(second, at - rows, at) + info[CORE] * (rows // 2)
    at = jnp.where(at >= rows, at - rows, at)
    return (at + jnp.where(second, info[BASES + slot + 1], info[BASES + slot])).astype(jnp.float32)


def token_kernel(info, column_ref, row_ref, ids_ref, table_ref, meta_ref, turn_ref):
    rows = 2 * 128
    count = row_ref.shape[1]
    earlier = lax.broadcasted_iota(jnp.int32, (count, count), 0) < lax.broadcasted_iota(
        jnp.int32, (count, count), 1
    )
    anchors = jnp.sum(jnp.where(earlier, column_ref[...], 0.0), axis=0, keepdims=True)
    endings = anchors + row_ref[...]
    ids = ids_ref[...]
    lane = lax.broadcasted_iota(jnp.int32, (rows, 128), 1)

    def one(block, _):
        token = local_tokens(info, 2 * block, (rows, 1), 0)
        inside = jnp.logical_and(anchors <= token, token < endings)
        start = jnp.sum(jnp.where(inside, anchors, 0.0), axis=1, keepdims=True)
        adapter = jnp.sum(jnp.where(inside, ids, 0.0), axis=1, keepdims=True)
        at = pl.ds(pl.multiple_of(block * rows, rows), rows)
        meta_ref[at, :] = jnp.where(lane < 64, start, adapter)
        angle = (token - start) * table_ref[0:1, :] - table_ref[1:2, :]
        turn_ref[at, :] = cosine(angle) * table_ref[2:3, :]
        return 0

    lax.fori_loop(0, meta_ref.shape[0] // rows, one, 0)


def rank_kernel(count, slots, info, *refs):
    x = jnp.concatenate([ref[...] for ref in refs[:count]], axis=0)
    left_ref, meta_ref, slot_ref, fold_ref, held_ref = refs[count : count + 5]
    out_ref = refs[-1]
    products = rank_product(x, left_ref[...])
    adapter = jnp.concatenate([meta_ref[k * 128 : (k + 1) * 128, 64:65] for k in slots], axis=0)
    chosen = jnp.where(slot_ref[...] == adapter, products, 0.0).astype(jnp.bfloat16)
    out_ref[...] = held_ref[...]
    store_lanes(info, out_ref, across(fold_ref[...], chosen), slots)


def base_kernel(count, *refs):
    x = jnp.concatenate([ref[...] for ref in refs[:count]], axis=0)
    qkv_ref, up_ref, base_ref, up_base_ref, shared_ref = refs[count:]
    first = rank_product(x, qkv_ref[...])
    base_ref[...] = first
    shared_ref[...] = first[:, HEAD_SIZE:].astype(shared_ref.dtype)
    up_base_ref[...] = rank_product(x, up_ref[...])


def turn(part, table):
    width = table.shape[1]
    lane = lax.broadcasted_iota(jnp.int32, table.shape, 1)
    cos = jnp.where(lane < ROT, table, 1.0)
    sin = jnp.where(lane < ROT, pltpu.roll(table, width - ROT, 1), 0.0)
    head = part[:, :width]
    swapped = jnp.where(
        lane % 2 == 0, pltpu.roll(head, width - 1, 1), pltpu.roll(head, 1, 1)
    )
    return jnp.concatenate([head * cos + swapped * sin, part[:, width:]], axis=1)


def block_rows_of(refs, block):
    if block == 0:
        return jnp.concatenate([refs[0][:128], refs[3][128:]], axis=0)
    if block == 3:
        return jnp.concatenate([refs[2][...], refs[3][:128]], axis=0)
    return refs[0][128:] if block == 1 else refs[1][...]


def inner_kernel(info, *refs):
    base_refs, up_refs, (rank_ref, meta_ref, turn_ref, first_ref, last_ref) = refs[:4], refs[4:8], refs[8:13]
    qkv_right_ref, up_right_ref, bias_ref, left_ref = refs[13:17]
    q_ref, k_ref, v_ref, hidden_ref, out_ref = refs[17:]
    rows = 256
    columns = qkv_right_ref.shape[0]
    for block in range(BLOCKS):
        at = slice(block * rows, (block + 1) * rows)
        adapter = meta_ref[at, 64:65]
        ranks = rank_rows(info, rank_ref, 2 * block, 2)
        total = block_rows_of(base_refs, block) + rank_product(
            widened(ranks, first_ref, adapter, columns), qkv_right_ref[...]
        )
        table = turn_ref[at, :]
        q_ref[at, :] = (turn(total[:, :HEAD_SIZE], table) * HEAD_SIZE ** (-0.5)).astype(jnp.bfloat16)
        k_ref[at, :] = turn(total[:, HEAD_SIZE : 2 * HEAD_SIZE], table).astype(jnp.bfloat16)
        v_ref[at, :] = total[:, 2 * HEAD_SIZE :].astype(jnp.bfloat16)
        wide = widened(ranks, last_ref, adapter, columns)
        x = block_rows_of(up_refs, block) + rank_product(wide, up_right_ref[...]) + bias_ref[...]
        inner = math.sqrt(2.0 / math.pi) * (x + 0.044715 * (x * x * x))
        hidden = (0.5 * x * (1.0 + jnp.tanh(inner))).astype(jnp.bfloat16)
        hidden_ref[at, :] = hidden
        lanes = folded(rank_product(hidden, left_ref[...]), adapter, last_ref)
        store_lanes(info, out_ref, lanes, (2 * block, 2 * block + 1))


def far_kernel(first_row, info, *refs):
    shared_refs, (rank_ref, meta_ref, turn_ref, spread_ref, right_ref, k_ref, v_ref) = refs[:4], refs[4:]
    rows = 256
    for block in range(BLOCKS):
        at = slice(block * rows, (block + 1) * rows)
        far_at = slice(first_row + block * rows, first_row + (block + 1) * rows)
        ranks = rank_rows(info, rank_ref, 2 * block, 2)
        wide = widened(ranks, spread_ref, meta_ref[far_at, 64:65], right_ref.shape[0])
        total = block_rows_of(shared_refs, block).astype(jnp.float32)
        total = total + rank_product(wide, right_ref[:, HEAD_SIZE:])
        k_ref[at, :] = turn(total[:, :HEAD_SIZE], turn_ref[far_at, :]).astype(jnp.bfloat16)
        v_ref[at, :] = total[:, HEAD_SIZE:].astype(jnp.bfloat16)


def attention_kernel(req_count, info, *refs):
    q_ref, refs = refs[0], refs[1:]
    key_refs, value_refs, refs = refs[:req_count], refs[req_count : 2 * req_count], refs[2 * req_count :]
    meta_ref, spread_ref, left_ref, hidden_rank_ref, attended_ref, out_ref = refs[:6]
    keys_ref, values_ref, top_ref, sum_ref, acc_ref, fold_ref = refs[6:]
    rows = 256
    pair = rows // 2
    group_rows = q_ref.shape[0]

    def twice(lanes):
        return jnp.concatenate([lanes] * (HEAD_SIZE // lanes.shape[1]), axis=1)

    def slot_rows(slot):
        return pl.ds(pl.multiple_of(slot * pair, pair), pair)

    for d in range(req_count):
        for k in range(SLOTS):
            at = slice((req_count - 1 - d) * group_rows + k * pair, (req_count - 1 - d) * group_rows + (k + 1) * pair)
            slot = slot_rows(info[PLACES + k])
            keys_ref[at, :] = key_refs[d][slot, :]
            values_ref[at, :] = value_refs[d][slot, :]
    first_token = info[BASES + info[PLACES]] - (req_count - 1) * group_rows

    def places(shape, dim):
        at = lax.broadcasted_iota(jnp.int32, shape, dim)
        second = at >= pair
        at = jnp.where(second, at - pair, at) + info[CORE] * (pair // 2)
        at = jnp.where(at >= pair, at - pair, at)
        return (at + jnp.where(second, pair, 0)).astype(jnp.float32)

    key_place = places((1, rows), 1)
    query_place = places((rows, 1), 0)

    def one(block, _):
        slots = [slot_rows(info[PLACES + 2 * block + k]) for k in (0, 1)]

        def both(ref):
            return jnp.concatenate([ref[at, :] for at in slots], axis=0)

        meta = both(meta_ref)
        start = meta[:, 0:1]
        number = (req_count - 1) * BLOCKS + block
        query = query_place + (first_token + number * rows).astype(jnp.float32)
        q = both(q_ref)
        lowest = jnp.min(start).astype(jnp.int32) - first_token
        top_ref[...] = jnp.full_like(top_ref, NEGATIVE_FILL)
        sum_ref[...] = jnp.zeros_like(sum_ref)
        acc_ref[...] = jnp.zeros_like(acc_ref)

        def chunk(j, _):
            at = pl.ds(pl.multiple_of(j * rows, rows), rows)
            scores = across(q, keys_ref[at, :])
            key = key_place + (first_token + j * rows).astype(jnp.float32)
            allowed = jnp.logical_and(key <= query, key >= start)
            scores = jnp.where(allowed, scores, NEGATIVE_FILL)
            top = top_ref[...]
            new_top = jnp.maximum(top, jnp.max(scores, axis=1, keepdims=True))
            weights = jnp.where(allowed, jnp.exp(scores - twice(new_top)), 0.0)
            scale = jnp.exp(top - new_top)
            top_ref[...] = new_top
            sum_ref[...] = sum_ref[...] * scale + jnp.sum(weights, axis=1, keepdims=True)
            acc_ref[...] = acc_ref[...] * twice(scale) + rank_product(
                weights.astype(jnp.bfloat16), values_ref[at, :]
            )
            return 0

        lax.fori_loop(lowest // rows, number + 1, chunk, 0)
        attended = (acc_ref[...] / twice(sum_ref[...])).astype(jnp.bfloat16)
        lanes = folded(rank_product(attended, left_ref[...]), meta[:, 64:65], spread_ref)
        for k in (0, 1):
            attended_ref[slots[k], :] = attended[k * pair : (k + 1) * pair]
            at = pl.ds(pl.multiple_of((2 * block + k) * pair, pair), pair)
            fold_ref[:, at] = swap_halves(info, lanes[:, k * pair : (k + 1) * pair])
        return 0

    lax.fori_loop(0, BLOCKS, one, 0)
    out_ref[...] = (fold_ref[...] + hidden_rank_ref[...].astype(jnp.float32)).astype(out_ref.dtype)


def main_kernel(block, attended_ref, hidden_ref, output_ref, down_ref, kept_ref, sent_ref):
    rows = 256
    sent = sent_ref.shape[0]
    width = 512
    attended = attended_ref[block * rows : (block + 1) * rows, :]
    hidden = hidden_ref[block * rows : (block + 1) * rows, :]

    def one(step, _):
        at = pl.ds(pl.multiple_of(step * width, width), width)
        total = rank_product(attended, output_ref[:, at]) + rank_product(hidden, down_ref[:, at])
        if block:
            sent_ref[:, at] = total[:sent].astype(sent_ref.dtype)
            kept_ref[:, at] = total[sent:]
        else:
            kept_ref[:, at] = total[: rows - sent]
            sent_ref[:, at] = total[rows - sent :].astype(sent_ref.dtype)
        return 0

    lax.fori_loop(0, output_ref.shape[1] // width, one, 0)


def adapt_kernel(slot, first, info, rank_ref, meta_ref, spread_ref, right_ref, kept_ref, arrived_ref, *out_refs):
    pair = 128
    half = pair // 2
    columns = spread_ref.shape[1]
    count = columns // (4 * ADAPTER_RANK)
    column_id = lax.broadcasted_iota(jnp.int32, (pair, columns), 1) // (2 * ADAPTER_RANK)
    partner = info[MLP] + 1 - 2 * info[CORE]
    column_id = column_id + jnp.where(column_id < count, info[MLP] * count, (partner - 1) * count)
    own = column_id.astype(jnp.float32) == meta_ref[slot * pair : (slot + 1) * pair, 64:65]
    spread = rank_product(rank_rows(info, rank_ref, slot, 1), spread_ref[...])
    wide = jnp.where(own, spread, 0.0).astype(jnp.bfloat16)
    width = 512

    def one(step, _):
        at = pl.ds(pl.multiple_of(step * width, width), width)
        if len(out_refs) == 1:
            total = rank_product(wide[:half], right_ref[:, at]) + kept_ref[first : first + half, at]
            total = total + arrived_ref[:, at].astype(jnp.float32)
            out_refs[0][:, at] = total.astype(out_refs[0].dtype)
        else:
            total = rank_product(wide, right_ref[:, at]) + kept_ref[:, at]
            out_refs[0][:, at] = total[:half] + arrived_ref[half:, at].astype(jnp.float32)
            out_refs[1][:, at] = total[half:] + arrived_ref[:half, at].astype(jnp.float32)
        return 0

    lax.fori_loop(0, right_ref.shape[1] // width, one, 0)


def call(kernel, operands, outs, info=None, scratch=(), mib=24, flops=1000):
    vmem = pl.BlockSpec(memory_space=pltpu.VMEM)
    specs = [vmem] * len(operands)
    if info is not None:
        operands, specs = [info] + operands, [pl.BlockSpec(memory_space=pltpu.SMEM)] + specs
    return pl.pallas_call(
        kernel,
        in_specs=specs,
        out_specs=[vmem] * len(outs),
        out_shape=outs,
        scratch_shapes=scratch,
        compiler_params=pltpu.CompilerParams(vmem_limit_bytes=mib * 1024 * 1024),
        cost_estimate=pl.CostEstimate(flops=flops, bytes_accessed=1000, transcendentals=0),
    )(*operands)


def shape(rows, width, dtype=jnp.bfloat16):
    return jax.ShapeDtypeStruct((rows, width), dtype)


def sum_over_mlp(value, bits):
    for bit in bits:
        value = value + lax.ppermute(value, "mlp", [(i, i ^ bit) for i in range(16)])
    return value


def narrow(value):
    return value.astype(jnp.bfloat16)


def wide(value):
    return value.astype(jnp.float32)


def per_device(
    tokens,
    layer_norm_gain,
    layer_norm_bias,
    query_key_weight,
    output_weight,
    up_weight,
    input_bias,
    down_weight,
    output_bias,
    input_adapter_left,
    query_key_value_right,
    up_adapter_right,
    output_adapter_left,
    down_adapter_left,
    output_adapter_right,
    lengths,
    request_adapter,
    slot_adapter,
):
    block = tokens.shape[0]
    model_width = tokens.shape[1]
    pair_rows = 2 * block
    group_rows = SLOTS * pair_rows
    req_count = lax.axis_size("req")
    group = lax.axis_index("req")
    me = lax.axis_index("mlp")
    block_rows = 2 * pair_rows
    table = np.zeros((req_count, 16, 2 + SLOTS * (2 + req_count)), np.int32)
    for g in range(req_count):
        for m in range(16):
            side = 2 * (m % 2) - 1
            steps = [0, 4] + [t for s in (1, 2, 3) for t in (side * s, -side * s)]
            pairs = [RING[(PLACE[m // 2] + t) % 8] for t in steps]
            firsts = [(g - d) * group_rows + p * pair_rows for d in range(req_count) for p in pairs]
            table[g, m] = [m % 2, m] + pairs + [pairs.index(p) for p in range(SLOTS)] + firsts
    info = lax.dynamic_slice(jnp.asarray(table), (group, me, 0), (1, 1, table.shape[2])).reshape(-1)

    own = call(
        norm_kernel,
        [tokens, layer_norm_gain.reshape(1, -1), layer_norm_bias.reshape(1, -1)],
        [shape(block, model_width)],
    )[0]
    other = to_partner(own)
    ring_a, ring_b = along_ring(own), along_ring(other)
    pair_left = jnp.concatenate([input_adapter_left, to_partner(input_adapter_left)], axis=1)

    float_lengths = wide(lengths)
    lane = np.arange(128)
    turn_rows = np.zeros((8, 128), np.float32)
    turn_rows[0] = np.exp(lane % ROT // 2 * (-2.0 * math.log(10000.0) / ROT))
    turn_rows[1] = np.where(lane < ROT, 0.0, math.pi / 2)
    turn_rows[2] = np.where(lane < ROT, 1.0, np.where(lane % 2 == 0, -1.0, 1.0))
    token_rows = req_count * group_rows
    token_args = [
        float_lengths[:, None],
        float_lengths[None, :],
        wide(request_adapter)[None, :],
        jnp.asarray(turn_rows),
    ]
    meta, turns = call(token_kernel, token_args, [shape(token_rows, 128, jnp.float32)] * 2, info)

    qkv_rows = query_key_weight.reshape(model_width, 3 * HEAD_SIZE)
    adapter_columns = query_key_value_right.shape[0]
    qkv_right = query_key_value_right.reshape(adapter_columns, 3 * HEAD_SIZE)
    spread_first = spread_table(ADAPTER_RANK, 0, 128)
    spread_last = spread_table(ADAPTER_RANK, ADAPTER_RANK, 128)
    near_right = output_adapter_right
    slot_columns = wide(jnp.repeat(slot_adapter, 2 * ADAPTER_RANK))[None, :]
    slot_columns = jnp.concatenate([slot_columns, to_partner(slot_columns)], axis=1)
    own_columns = near_right.shape[0]
    spread_own = spread_table(2 * ADAPTER_RANK, 0, 2 * own_columns)
    hidden_width = up_weight.shape[1]

    def to_group(value, d):
        return lax.ppermute(value, "req", [(g, g + d) for g in range(req_count - d)])

    held = functools.partial(pltpu.VMEM, dtype=jnp.float32)

    def add_ranks(part, slots, so_far, ahead=()):
        return call(
            functools.partial(rank_kernel, len(part), slots),
            list(part) + [pair_left, meta, slot_columns, spread_own, so_far, *ahead],
            [shape(32, group_rows)],
            info,
        )[0]

    def products_of(part, flops=1000):
        rows = len(part) * block
        return call(
            functools.partial(base_kernel, len(part)),
            list(part) + [qkv_rows, up_weight],
            [
                shape(rows, 3 * HEAD_SIZE, jnp.float32),
                shape(rows, hidden_width, jnp.float32),
                shape(rows, 2 * HEAD_SIZE),
            ],
            flops=flops,
        )

    def to_groups(value):
        return [to_group(value, d) for d in range(1, req_count)]

    def arrivals(a, b):
        return a, b, to_partner(b), to_partner(a)

    tie = lax.optimization_barrier
    own_part = (own, other)
    ring_a, meta, turns, pair_left = tie((ring_a, meta, turns, pair_left))
    ranks = add_ranks(own_part, (0,), jnp.zeros((32, group_rows), jnp.bfloat16), (qkv_rows, up_weight))
    ring_b, ranks = tie((ring_b, ranks))
    part = arrivals(ring_a, ring_b)
    ring_a, ring_b = along_ring(ring_a), along_ring(ring_b)
    ranks = add_ranks(part, (2, 3), ranks)
    first = products_of(own_part + part)
    ring_b, ranks, first = tie((ring_b, ranks, first))
    part = arrivals(ring_a, ring_b)
    ring_a, ring_b = along_ring(ring_a), along_ring(ring_b)
    far_right = to_partner(near_right)
    far_early = to_groups(first[2])
    ranks = add_ranks(part, (4, 5), ranks)
    second = products_of(part)
    ring_b, ranks, second, far_right, far_early = tie((ring_b, ranks, second, far_right, far_early))
    part = arrivals(ring_a, ring_b)
    ring_a = along_ring(ring_a)
    third = products_of(part[:2], 2000000000)
    ranks = add_ranks(part[:2], (6,), ranks)
    ring_a, ranks, third = tie((ring_a, ranks, third))
    part = part[2:] + (ring_a, to_partner(ring_a))
    ranks = add_ranks(part, (7, 1), ranks)
    moved = lax.ppermute(ranks, "mlp", [(i, i ^ 2) for i in range(16)])
    fourth = products_of(part)
    ranks, fourth = tie((ranks + moved, fourth))
    far_middle = to_groups(second[2])
    far_late = to_groups(jnp.concatenate([third[2], fourth[2]], axis=0))
    rank_in = sum_over_mlp(ranks, (4, 8))
    products = (first, second, third, fourth)

    bias_row = input_bias.reshape(1, -1)
    far_rank = to_groups(rank_in)
    queries, own_keys, own_values, hidden, hidden_rank = call(
        inner_kernel,
        [part[0] for part in products]
        + [part[1] for part in products]
        + [rank_in, meta, turns, spread_first, spread_last]
        + [qkv_right, up_adapter_right, bias_row, down_adapter_left],
        [shape(group_rows, HEAD_SIZE)] * 3 + [shape(group_rows, hidden_width), shape(32, group_rows)],
        info,
    )
    keys, values = [own_keys], [own_values]
    for d in range(1, req_count):
        early, late = far_early[d - 1], far_late[d - 1]
        shared = [early, far_middle[d - 1], late[:pair_rows], late[pair_rows:]]
        far_keys, far_values = call(
            functools.partial(far_kernel, d * group_rows),
            shared + [far_rank[d - 1], meta, turns, spread_first, qkv_right],
            [shape(group_rows, HEAD_SIZE)] * 2,
            info,
        )
        keys.append(far_keys)
        values.append(far_values)

    output_left = output_adapter_left.reshape(HEAD_SIZE, adapter_columns)
    attended, rank_out = call(
        functools.partial(attention_kernel, req_count),
        [queries] + keys + values + [meta, spread_first, output_left, hidden_rank],
        [shape(group_rows, HEAD_SIZE), shape(32, group_rows)],
        info,
        [
            pltpu.VMEM((req_count * group_rows, HEAD_SIZE), jnp.bfloat16),
            pltpu.VMEM((req_count * group_rows, HEAD_SIZE), jnp.bfloat16),
            held((block_rows, 128)),
            held((block_rows, 128)),
            held((block_rows, HEAD_SIZE)),
            held((32, group_rows)),
        ],
    )
    output_rows = output_weight.reshape(HEAD_SIZE, model_width)

    def main(k, attended, hidden):
        sent = block if k == 0 else pair_rows
        return call(
            functools.partial(main_kernel, k),
            [attended, hidden, output_rows, down_weight],
            [shape(block_rows - sent, model_width, jnp.float32), shape(sent, model_width)],
        )

    kept, arrived, sent = {}, {}, {}
    for bit, k in zip((1, 2, 4, 8), (0, 3, 2, 1)):
        moved = lax.ppermute(rank_out, "mlp", [(i, i ^ bit) for i in range(16)])
        kept[k], sent[k] = main(k, attended, hidden)
        rank_out, attended, kept[k], sent[k] = tie((rank_out + moved, attended, kept[k], sent[k]))
        if k == 0:
            arrived[k] = to_partner(sent[k])
        if bit == 4:
            arrived[3] = to_partner(sent[3])
            rank_out, arrived[0] = tie((rank_out, arrived[0]))
    rank_out, arrived[3] = tie((rank_out, arrived[3]))
    pair_right = jnp.concatenate([near_right, far_right], axis=0)

    def adapt(slot, half, kept, first, arrived):
        if half:
            outs = [shape(block, model_width, jnp.bfloat16 if slot else jnp.float32)]
        else:
            outs = [shape(block, model_width, jnp.float32)] * 2
        return call(
            functools.partial(adapt_kernel, slot, first),
            [rank_out, meta, spread_own, pair_right, kept, arrived],
            outs,
            info,
        )

    chain_a = along_ring(adapt(1, True, kept[0], 2 * block, arrived[0])[0])
    chain_b = None
    for s in (3, 2, 1):
        add_a, add_b = adapt(2 * s + 1, False, kept[s], 0, arrived[s])
        if s > 1:
            arrived[s - 1] = to_partner(sent[s - 1])
        if chain_b is None:
            chain_b = along_ring(narrow(add_b))
            chain_a = along_ring(narrow(wide(chain_a) + add_a))
        else:
            chain_a = along_ring(narrow(wide(chain_a) + add_a))
            chain_b = along_ring(narrow(wide(chain_b) + add_b))
    own_sum = adapt(0, True, kept[0], 0, tokens)[0]
    chain_a, own_sum = tie((chain_a, own_sum))
    arrived_last = to_partner(narrow(wide(chain_b) + kept[0][block : 2 * block]))
    return narrow(wide(chain_a) + wide(arrived_last) + own_sum + output_bias)


def solution(mesh):
    in_specs = (
        P(("req", "mlp"), None),
        P(),
        P(),
        P(None, "mlp", None),
        P("mlp", None, None),
        P(None, "mlp"),
        P("mlp"),
        P("mlp", None),
        P(),
        P(None, "mlp"),
        P(None, "mlp", None),
        P(None, "mlp"),
        P("mlp", None, None),
        P("mlp", None),
        P("mlp", None),
        P(),
        P(),
        P("mlp"),
    )
    out_specs = P(("req", "mlp"), None)
    return jax.shard_map(
        per_device, mesh=mesh, in_specs=in_specs, out_specs=out_specs, check_vma=False
    )
```

```python
import functools
import math

import jax
import jax.numpy as jnp
import numpy as np
from jax import lax
from jax.experimental import pallas as pl
from jax.experimental.pallas import tpu as pltpu
from jax.sharding import PartitionSpec as P

HEAD_SIZE = 256
ROT = 64
ADAPTER_RANK = 16
EPSILON = 1e-05
NEGATIVE_FILL = -1e30
RING = (0, 2, 4, 6, 7, 5, 3, 1)
PLACE = tuple(RING.index(pair) for pair in range(8))
CORE_PERM = [(i, i ^ 1) for i in range(16)]
RING_PERM = [(RING[i] * 2, RING[(i + 1) % 8] * 2) for i in range(8)] + [
    (RING[i] * 2 + 1, RING[(i - 1) % 8] * 2 + 1) for i in range(8)
]
SLOTS = 8
BLOCKS = 4
CORE, MLP, PAIRS, PLACES, BASES = 0, 1, 2, 2 + SLOTS, 2 + 2 * SLOTS


def to_partner(value):
    return lax.ppermute(value, "mlp", CORE_PERM)


def along_ring(value):
    return lax.ppermute(value, "mlp", RING_PERM)


def rank_product(left_side, right_side):
    return jnp.dot(left_side, right_side, preferred_element_type=jnp.float32)


def across(left_side, right_side):
    return lax.dot_general(
        left_side, right_side, (((1,), (1,)), ((), ())), preferred_element_type=jnp.float32
    )


def spread_table(period, first, width):
    row = np.arange(32)[:, None]
    column = np.arange(width)[None, :]
    return jnp.asarray((row - first == column % period).astype(np.float32), jnp.bfloat16)


def swap_halves(info, lanes):
    half = lanes.shape[1] // 2
    return jnp.where(info[CORE] == 1, pltpu.roll(lanes, half, 1), lanes)


def lane_ids(shape, period):
    return (lax.broadcasted_iota(jnp.int32, shape, 1) // period).astype(jnp.float32)


def pair_at(info, slot, rows):
    return pl.ds(pl.multiple_of(info[PAIRS + slot] * rows, rows), rows)


def store_lanes(info, out_ref, lanes, slots):
    width = out_ref.shape[1] // SLOTS
    for k, slot in enumerate(slots):
        part = lanes[:, k * width : (k + 1) * width]
        out_ref[:, pair_at(info, slot, width)] = swap_halves(info, part).astype(out_ref.dtype)


def rank_rows(info, rank_ref, slot, count):
    width = rank_ref.shape[1] // SLOTS
    lanes = [
        swap_halves(info, rank_ref[:, pair_at(info, slot + k, width)].astype(jnp.float32))
        for k in range(count)
    ]
    lanes = lanes[0] if count == 1 else jnp.concatenate(lanes, axis=1)
    return jnp.transpose(lanes).astype(jnp.bfloat16)


def widened(rows, spread_ref, adapter, columns):
    tile = rank_product(rows, spread_ref[...]).astype(jnp.bfloat16)
    group = lax.broadcasted_iota(jnp.int32, tile.shape, 1) // ADAPTER_RANK
    apart = (adapter - group.astype(jnp.float32)).astype(jnp.bfloat16)
    step = tile.shape[1] // ADAPTER_RANK
    zero = jnp.zeros_like(tile)
    return jnp.concatenate(
        [jnp.where(apart == first, tile, zero) for first in range(0, columns // ADAPTER_RANK, step)], axis=1
    )


def folded(products, adapter, spread_ref):
    width = spread_ref.shape[1]
    group = lax.broadcasted_iota(jnp.int32, (products.shape[0], width), 1) // ADAPTER_RANK
    apart = adapter - group.astype(jnp.float32)
    total = None
    for first in range(0, products.shape[1], width):
        part = products[:, first : first + width]
        part = jnp.where(apart == float(first // ADAPTER_RANK), part, 0.0)
        total = part if total is None else total + part
    return across(spread_ref[...], total.astype(jnp.bfloat16))


def cosine(angle):
    turns = jnp.floor(angle * (1.0 / math.pi) + 0.5)
    rest = ((angle - turns * 3.140625) - turns * 9.67502593994140625e-4) - turns * 1.509957990978376e-7
    square = rest * rest
    value = jnp.full_like(square, 1.0 / 479001600.0)
    for factor in (-1.0 / 3628800.0, 1.0 / 40320.0, -1.0 / 720.0, 1.0 / 24.0, -0.5, 1.0):
        value = value * square + factor
    odd = turns - 2.0 * jnp.floor(turns * 0.5)
    return value * (1.0 - 2.0 * odd)


def norm_kernel(x_ref, gain_ref, bias_ref, out_ref):
    values = x_ref[...].astype(jnp.float32)
    center = values - jnp.mean(values, axis=1, keepdims=True)
    spread = jnp.mean(center * center, axis=1, keepdims=True)
    scaled = center * lax.rsqrt(spread + EPSILON)
    out_ref[...] = (scaled * gain_ref[...] + bias_ref[...]).astype(out_ref.dtype)


def local_tokens(info, slot, shape, dim):
    rows = shape[dim] // 2
    at = lax.broadcasted_iota(jnp.int32, shape, dim)
    second = at >= rows
    at = jnp.where(second, at - rows, at) + info[CORE] * (rows // 2)
    at = jnp.where(at >= rows, at - rows, at)
    return (at + jnp.where(second, info[BASES + slot + 1], info[BASES + slot])).astype(jnp.float32)


def token_kernel(info, column_ref, row_ref, ids_ref, table_ref, meta_ref, turn_ref):
    rows = 2 * 128
    count = row_ref.shape[1]
    earlier = lax.broadcasted_iota(jnp.int32, (count, count), 0) < lax.broadcasted_iota(
        jnp.int32, (count, count), 1
    )
    anchors = jnp.sum(jnp.where(earlier, column_ref[...], 0.0), axis=0, keepdims=True)
    endings = anchors + row_ref[...]
    ids = ids_ref[...]
    lane = lax.broadcasted_iota(jnp.int32, (rows, 128), 1)

    def one(block, _):
        token = local_tokens(info, 2 * block, (rows, 1), 0)
        inside = jnp.logical_and(anchors <= token, token < endings)
        start = jnp.sum(jnp.where(inside, anchors, 0.0), axis=1, keepdims=True)
        adapter = jnp.sum(jnp.where(inside, ids, 0.0), axis=1, keepdims=True)
        at = pl.ds(pl.multiple_of(block * rows, rows), rows)
        meta_ref[at, :] = jnp.where(lane < 64, start, adapter)
        angle = (token - start) * table_ref[0:1, :] - table_ref[1:2, :]
        turn_ref[at, :] = cosine(angle) * table_ref[2:3, :]
        return 0

    lax.fori_loop(0, meta_ref.shape[0] // rows, one, 0)


def rank_kernel(count, slots, info, *refs):
    x = jnp.concatenate([ref[...] for ref in refs[:count]], axis=0)
    left_ref, meta_ref, slot_ref, fold_ref, held_ref = refs[count : count + 5]
    out_ref = refs[-1]
    products = rank_product(x, left_ref[...])
    adapter = jnp.concatenate([meta_ref[k * 128 : (k + 1) * 128, 64:65] for k in slots], axis=0)
    chosen = jnp.where(slot_ref[...] == adapter, products, 0.0).astype(jnp.bfloat16)
    out_ref[...] = held_ref[...]
    store_lanes(info, out_ref, across(fold_ref[...], chosen), slots)


def base_kernel(count, *refs):
    x = jnp.concatenate([ref[...] for ref in refs[:count]], axis=0)
    qkv_ref, up_ref, base_ref, up_base_ref, shared_ref = refs[count:]
    first = rank_product(x, qkv_ref[...])
    base_ref[...] = first
    shared_ref[...] = first[:, HEAD_SIZE:].astype(shared_ref.dtype)
    up_base_ref[...] = rank_product(x, up_ref[...])


def turn(part, table):
    width = table.shape[1]
    lane = lax.broadcasted_iota(jnp.int32, table.shape, 1)
    cos = jnp.where(lane < ROT, table, 1.0)
    sin = jnp.where(lane < ROT, pltpu.roll(table, width - ROT, 1), 0.0)
    head = part[:, :width]
    swapped = jnp.where(
        lane % 2 == 0, pltpu.roll(head, width - 1, 1), pltpu.roll(head, 1, 1)
    )
    return jnp.concatenate([head * cos + swapped * sin, part[:, width:]], axis=1)


def block_rows_of(refs, block):
    if block == 0:
        return jnp.concatenate([refs[0][:128], refs[3][128:]], axis=0)
    if block == 3:
        return jnp.concatenate([refs[2][...], refs[3][:128]], axis=0)
    return refs[0][128:] if block == 1 else refs[1][...]


def two_blocks(refs, index):
    return jnp.concatenate([block_rows_of(refs, 2 * index + k) for k in (0, 1)], axis=0)


def inner_kernel(info, *refs):
    base_refs, up_refs, (rank_ref, meta_ref, turn_ref, first_ref, last_ref) = refs[:4], refs[4:8], refs[8:13]
    qkv_right_ref, up_right_ref, bias_ref, left_ref = refs[13:17]
    q_ref, k_ref, v_ref, hidden_ref, out_ref = refs[17:]
    rows = 512
    columns = qkv_right_ref.shape[0]
    for block in range(BLOCKS // 2):
        at = slice(block * rows, (block + 1) * rows)
        adapter = meta_ref[at, 64:65]
        ranks = rank_rows(info, rank_ref, 4 * block, 4)
        total = two_blocks(base_refs, block) + rank_product(
            widened(ranks, first_ref, adapter, columns), qkv_right_ref[...]
        )
        table = turn_ref[at, :]
        q_ref[at, :] = (turn(total[:, :HEAD_SIZE], table) * HEAD_SIZE ** (-0.5)).astype(jnp.bfloat16)
        k_ref[at, :] = turn(total[:, HEAD_SIZE : 2 * HEAD_SIZE], table).astype(jnp.bfloat16)
        v_ref[at, :] = total[:, 2 * HEAD_SIZE :].astype(jnp.bfloat16)
        wide = widened(ranks, last_ref, adapter, columns)
        x = two_blocks(up_refs, block) + rank_product(wide, up_right_ref[...]) + bias_ref[...]
        inner = math.sqrt(2.0 / math.pi) * (x + 0.044715 * (x * x * x))
        hidden = (0.5 * x * (1.0 + jnp.tanh(inner))).astype(jnp.bfloat16)
        hidden_ref[at, :] = hidden
        lanes = folded(rank_product(hidden, left_ref[...]), adapter, last_ref)
        store_lanes(info, out_ref, lanes, range(4 * block, 4 * block + 4))


def far_kernel(first_row, info, *refs):
    shared_refs, (rank_ref, meta_ref, turn_ref, spread_ref, right_ref, k_ref, v_ref) = refs[:4], refs[4:]
    rows = 512
    for block in range(BLOCKS // 2):
        at = slice(block * rows, (block + 1) * rows)
        far_at = slice(first_row + block * rows, first_row + (block + 1) * rows)
        ranks = rank_rows(info, rank_ref, 4 * block, 4)
        wide = widened(ranks, spread_ref, meta_ref[far_at, 64:65], right_ref.shape[0])
        total = two_blocks(shared_refs, block).astype(jnp.float32)
        total = total + rank_product(wide, right_ref[:, HEAD_SIZE:])
        k_ref[at, :] = turn(total[:, :HEAD_SIZE], turn_ref[far_at, :]).astype(jnp.bfloat16)
        v_ref[at, :] = total[:, HEAD_SIZE:].astype(jnp.bfloat16)


def attention_kernel(req_count, info, *refs):
    q_ref, refs = refs[0], refs[1:]
    key_refs, value_refs, refs = refs[:req_count], refs[req_count : 2 * req_count], refs[2 * req_count :]
    meta_ref, spread_ref, left_ref, hidden_rank_ref, attended_ref, out_ref = refs[:6]
    keys_ref, values_ref, scores_ref, top_ref, sum_ref, acc_ref, fold_ref = refs[6:]
    rows = 256
    pair = rows // 2
    group_rows = q_ref.shape[0]

    def slot_rows(slot):
        return pl.ds(pl.multiple_of(slot * pair, pair), pair)

    for d in range(req_count):
        for k in range(SLOTS):
            at = slice((req_count - 1 - d) * group_rows + k * pair, (req_count - 1 - d) * group_rows + (k + 1) * pair)
            slot = slot_rows(info[PLACES + k])
            keys_ref[at, :] = key_refs[d][slot, :]
            values_ref[at, :] = value_refs[d][slot, :]
    first_token = info[BASES + info[PLACES]] - (req_count - 1) * group_rows

    def places(shape, dim):
        at = lax.broadcasted_iota(jnp.int32, shape, dim)
        second = at >= pair
        at = jnp.where(second, at - pair, at) + info[CORE] * (pair // 2)
        at = jnp.where(at >= pair, at - pair, at)
        return (at + jnp.where(second, pair, 0)).astype(jnp.float32)

    key_place = places((1, rows), 1)
    query_place = places((rows, 1), 0)

    def one(block, _):
        slots = [slot_rows(info[PLACES + 2 * block + k]) for k in (0, 1)]

        def both(ref):
            return jnp.concatenate([ref[at, :] for at in slots], axis=0)

        meta = both(meta_ref)
        start = meta[:, 0:1]
        number = (req_count - 1) * BLOCKS + block
        query = query_place + (first_token + number * rows).astype(jnp.float32)
        q = both(q_ref)
        lowest = jnp.min(start).astype(jnp.int32) - first_token
        top_ref[...] = jnp.full_like(top_ref, NEGATIVE_FILL)
        sum_ref[...] = jnp.zeros_like(sum_ref)
        acc_ref[...] = jnp.zeros_like(acc_ref)

        def score(j, _):
            at = pl.ds(pl.multiple_of(j * rows, rows), rows)
            scores = across(q, keys_ref[at, :])
            key = key_place + (first_token + j * rows).astype(jnp.float32)
            allowed = jnp.logical_and(key <= query, key >= start)
            scores = jnp.where(allowed, scores, NEGATIVE_FILL)
            scores_ref[:, at] = scores
            top_ref[...] = jnp.maximum(top_ref[...], jnp.maximum(scores[:, :pair], scores[:, pair:]))
            return 0

        lax.fori_loop(lowest // rows, number + 1, score, 0)
        top = jnp.max(top_ref[...], axis=1, keepdims=True)

        def weigh(j, _):
            at = pl.ds(pl.multiple_of(j * rows, rows), rows)
            weights = jnp.exp(scores_ref[:, at] - top)
            sum_ref[...] = sum_ref[...] + (weights[:, :pair] + weights[:, pair:])
            acc_ref[...] = acc_ref[...] + rank_product(weights.astype(jnp.bfloat16), values_ref[at, :])
            return 0

        lax.fori_loop(lowest // rows, number + 1, weigh, 0)
        total = jnp.sum(sum_ref[...], axis=1, keepdims=True)
        attended = (acc_ref[...] / total).astype(jnp.bfloat16)
        lanes = folded(rank_product(attended, left_ref[...]), meta[:, 64:65], spread_ref)
        for k in (0, 1):
            attended_ref[slots[k], :] = attended[k * pair : (k + 1) * pair]
            at = pl.ds(pl.multiple_of((2 * block + k) * pair, pair), pair)
            fold_ref[:, at] = swap_halves(info, lanes[:, k * pair : (k + 1) * pair])
        return 0

    lax.fori_loop(0, BLOCKS, one, 0)
    out_ref[...] = (fold_ref[...] + hidden_rank_ref[...].astype(jnp.float32)).astype(out_ref.dtype)


def main_kernel(block, attended_ref, hidden_ref, output_ref, down_ref, kept_ref, sent_ref):
    rows = 256
    sent = sent_ref.shape[0]
    width = 512
    attended = attended_ref[block * rows : (block + 1) * rows, :]
    hidden = hidden_ref[block * rows : (block + 1) * rows, :]

    for step in range(output_ref.shape[1] // width):
        at = slice(step * width, (step + 1) * width)
        total = rank_product(attended, output_ref[:, at]) + rank_product(hidden, down_ref[:, at])
        if block:
            sent_ref[:, at] = total[:sent].astype(sent_ref.dtype)
            kept_ref[:, at] = total[sent:]
        else:
            kept_ref[:, at] = total[: rows - sent]
            sent_ref[:, at] = total[rows - sent :].astype(sent_ref.dtype)


def adapt_kernel(slot, first, info, rank_ref, meta_ref, spread_ref, right_ref, kept_ref, arrived_ref, *out_refs):
    pair = 128
    half = pair // 2
    columns = spread_ref.shape[1]
    count = columns // (4 * ADAPTER_RANK)
    column_id = lax.broadcasted_iota(jnp.int32, (pair, columns), 1) // (2 * ADAPTER_RANK)
    partner = info[MLP] + 1 - 2 * info[CORE]
    column_id = column_id + jnp.where(column_id < count, info[MLP] * count, (partner - 1) * count)
    own = column_id.astype(jnp.float32) == meta_ref[slot * pair : (slot + 1) * pair, 64:65]
    spread = rank_product(rank_rows(info, rank_ref, slot, 1), spread_ref[...])
    wide = jnp.where(own, spread, 0.0).astype(jnp.bfloat16)
    width = 512

    for step in range(right_ref.shape[1] // width):
        at = slice(step * width, (step + 1) * width)
        if len(out_refs) == 1:
            total = rank_product(wide[:half], right_ref[:, at]) + kept_ref[first : first + half, at]
            total = total + arrived_ref[:, at].astype(jnp.float32)
            out_refs[0][:, at] = total.astype(out_refs[0].dtype)
        else:
            total = rank_product(wide, right_ref[:, at]) + kept_ref[:, at]
            out_refs[0][:, at] = total[:half] + arrived_ref[half:, at].astype(jnp.float32)
            out_refs[1][:, at] = total[half:] + arrived_ref[:half, at].astype(jnp.float32)


def call(kernel, operands, outs, info=None, scratch=(), mib=24, flops=1000):
    vmem = pl.BlockSpec(memory_space=pltpu.VMEM)
    specs = [vmem] * len(operands)
    if info is not None:
        operands, specs = [info] + operands, [pl.BlockSpec(memory_space=pltpu.SMEM)] + specs
    return pl.pallas_call(
        kernel,
        in_specs=specs,
        out_specs=[vmem] * len(outs),
        out_shape=outs,
        scratch_shapes=scratch,
        compiler_params=pltpu.CompilerParams(vmem_limit_bytes=mib * 1024 * 1024),
        cost_estimate=pl.CostEstimate(flops=flops, bytes_accessed=1000, transcendentals=0),
    )(*operands)


def shape(rows, width, dtype=jnp.bfloat16):
    return jax.ShapeDtypeStruct((rows, width), dtype)


def sum_over_mlp(value, bits):
    for bit in bits:
        value = value + lax.ppermute(value, "mlp", [(i, i ^ bit) for i in range(16)])
    return value


def narrow(value):
    return value.astype(jnp.bfloat16)


def wide(value):
    return value.astype(jnp.float32)


def per_device(
    tokens,
    layer_norm_gain,
    layer_norm_bias,
    query_key_weight,
    output_weight,
    up_weight,
    input_bias,
    down_weight,
    output_bias,
    input_adapter_left,
    query_key_value_right,
    up_adapter_right,
    output_adapter_left,
    down_adapter_left,
    output_adapter_right,
    lengths,
    request_adapter,
    slot_adapter,
):
    block = tokens.shape[0]
    model_width = tokens.shape[1]
    pair_rows = 2 * block
    group_rows = SLOTS * pair_rows
    req_count = lax.axis_size("req")
    group = lax.axis_index("req")
    me = lax.axis_index("mlp")
    block_rows = 2 * pair_rows
    table = np.zeros((req_count, 16, 2 + SLOTS * (2 + req_count)), np.int32)
    for g in range(req_count):
        for m in range(16):
            side = 2 * (m % 2) - 1
            steps = [0, 4] + [t for s in (1, 2, 3) for t in (side * s, -side * s)]
            pairs = [RING[(PLACE[m // 2] + t) % 8] for t in steps]
            firsts = [(g - d) * group_rows + p * pair_rows for d in range(req_count) for p in pairs]
            table[g, m] = [m % 2, m] + pairs + [pairs.index(p) for p in range(SLOTS)] + firsts
    info = lax.dynamic_slice(jnp.asarray(table), (group, me, 0), (1, 1, table.shape[2])).reshape(-1)

    own = call(
        norm_kernel,
        [tokens, layer_norm_gain.reshape(1, -1), layer_norm_bias.reshape(1, -1)],
        [shape(block, model_width)],
    )[0]
    other = to_partner(own)
    ring_a, ring_b = along_ring(own), along_ring(other)
    pair_left = jnp.concatenate([input_adapter_left, to_partner(input_adapter_left)], axis=1)

    float_lengths = wide(lengths)
    lane = np.arange(128)
    turn_rows = np.zeros((8, 128), np.float32)
    turn_rows[0] = np.exp(lane % ROT // 2 * (-2.0 * math.log(10000.0) / ROT))
    turn_rows[1] = np.where(lane < ROT, 0.0, math.pi / 2)
    turn_rows[2] = np.where(lane < ROT, 1.0, np.where(lane % 2 == 0, -1.0, 1.0))
    token_rows = req_count * group_rows
    token_args = [
        float_lengths[:, None],
        float_lengths[None, :],
        wide(request_adapter)[None, :],
        jnp.asarray(turn_rows),
    ]
    meta, turns = call(token_kernel, token_args, [shape(token_rows, 128, jnp.float32)] * 2, info)

    qkv_rows = query_key_weight.reshape(model_width, 3 * HEAD_SIZE)
    adapter_columns = query_key_value_right.shape[0]
    qkv_right = query_key_value_right.reshape(adapter_columns, 3 * HEAD_SIZE)
    spread_first = spread_table(ADAPTER_RANK, 0, 128)
    spread_last = spread_table(ADAPTER_RANK, ADAPTER_RANK, 128)
    near_right = output_adapter_right
    slot_columns = wide(jnp.repeat(slot_adapter, 2 * ADAPTER_RANK))[None, :]
    slot_columns = jnp.concatenate([slot_columns, to_partner(slot_columns)], axis=1)
    own_columns = near_right.shape[0]
    spread_own = spread_table(2 * ADAPTER_RANK, 0, 2 * own_columns)
    hidden_width = up_weight.shape[1]

    def to_group(value, d):
        return lax.ppermute(value, "req", [(g, g + d) for g in range(req_count - d)])

    held = functools.partial(pltpu.VMEM, dtype=jnp.float32)

    def add_ranks(part, slots, so_far, ahead=()):
        return call(
            functools.partial(rank_kernel, len(part), slots),
            list(part) + [pair_left, meta, slot_columns, spread_own, so_far, *ahead],
            [shape(32, group_rows)],
            info,
        )[0]

    def products_of(part, flops=1000):
        rows = len(part) * block
        return call(
            functools.partial(base_kernel, len(part)),
            list(part) + [qkv_rows, up_weight],
            [
                shape(rows, 3 * HEAD_SIZE, jnp.float32),
                shape(rows, hidden_width, jnp.float32),
                shape(rows, 2 * HEAD_SIZE),
            ],
            flops=flops,
        )

    def to_groups(value):
        return [to_group(value, d) for d in range(1, req_count)]

    def arrivals(a, b):
        return a, b, to_partner(b), to_partner(a)

    tie = lax.optimization_barrier
    own_part = (own, other)
    ring_a, meta, turns, pair_left = tie((ring_a, meta, turns, pair_left))
    ranks = add_ranks(own_part, (0,), jnp.zeros((32, group_rows), jnp.bfloat16), (qkv_rows, up_weight))
    ring_b, ranks = tie((ring_b, ranks))
    part = arrivals(ring_a, ring_b)
    ring_a, ring_b = along_ring(ring_a), along_ring(ring_b)
    ranks = add_ranks(part, (2, 3), ranks)
    first = products_of(own_part + part)
    ring_b, ranks, first = tie((ring_b, ranks, first))
    part = arrivals(ring_a, ring_b)
    ring_a, ring_b = along_ring(ring_a), along_ring(ring_b)
    far_right = to_partner(near_right)
    far_early = to_groups(first[2])
    ranks = add_ranks(part, (4, 5), ranks)
    second = products_of(part)
    ring_b, ranks, second, far_right = tie((ring_b, ranks, second, far_right))
    part = arrivals(ring_a, ring_b)
    ring_a = along_ring(ring_a)
    held_rows, far_early = tie((part[:2], far_early))
    third = products_of(held_rows, 2000000000)
    ranks = add_ranks(held_rows, (6,), ranks)
    ring_a, ranks, third = tie((ring_a, ranks, third))
    part = part[2:] + (ring_a, to_partner(ring_a))
    ranks = add_ranks(part, (7, 1), ranks)
    moved = lax.ppermute(ranks, "mlp", [(i, i ^ 2) for i in range(16)])
    fourth = products_of(part)
    ranks, fourth = tie((ranks + moved, fourth))
    far_middle = to_groups(second[2])
    far_late = to_groups(jnp.concatenate([third[2], fourth[2]], axis=0))
    rank_in = sum_over_mlp(ranks, (4, 8))
    products = (first, second, third, fourth)

    bias_row = input_bias.reshape(1, -1)
    far_rank = to_groups(rank_in)
    queries, own_keys, own_values, hidden, hidden_rank = call(
        inner_kernel,
        [part[0] for part in products]
        + [part[1] for part in products]
        + [rank_in, meta, turns, spread_first, spread_last]
        + [qkv_right, up_adapter_right, bias_row, down_adapter_left],
        [shape(group_rows, HEAD_SIZE)] * 3 + [shape(group_rows, hidden_width), shape(32, group_rows)],
        info,
    )
    keys, values = [own_keys], [own_values]
    for d in range(1, req_count):
        early, late = far_early[d - 1], far_late[d - 1]
        shared = [early, far_middle[d - 1], late[:pair_rows], late[pair_rows:]]
        far_keys, far_values = call(
            functools.partial(far_kernel, d * group_rows),
            shared + [far_rank[d - 1], meta, turns, spread_first, qkv_right],
            [shape(group_rows, HEAD_SIZE)] * 2,
            info,
        )
        keys.append(far_keys)
        values.append(far_values)

    output_left = output_adapter_left.reshape(HEAD_SIZE, adapter_columns)
    attended, rank_out = call(
        functools.partial(attention_kernel, req_count),
        [queries] + keys + values + [meta, spread_first, output_left, hidden_rank],
        [shape(group_rows, HEAD_SIZE), shape(32, group_rows)],
        info,
        [
            pltpu.VMEM((req_count * group_rows, HEAD_SIZE), jnp.bfloat16),
            pltpu.VMEM((req_count * group_rows, HEAD_SIZE), jnp.bfloat16),
            held((block_rows, req_count * group_rows)),
            held((block_rows, 128)),
            held((block_rows, 128)),
            held((block_rows, HEAD_SIZE)),
            held((32, group_rows)),
        ],
    )
    output_rows = output_weight.reshape(HEAD_SIZE, model_width)

    def main(k, attended, hidden):
        sent = block if k == 0 else pair_rows
        return call(
            functools.partial(main_kernel, k),
            [attended, hidden, output_rows, down_weight],
            [shape(block_rows - sent, model_width, jnp.float32), shape(sent, model_width)],
        )

    kept, arrived, sent = {}, {}, {}
    for bit, k in zip((1, 2, 4, 8), (0, 3, 2, 1)):
        moved = lax.ppermute(rank_out, "mlp", [(i, i ^ bit) for i in range(16)])
        kept[k], sent[k] = main(k, attended, hidden)
        rank_out, attended, kept[k], sent[k] = tie((rank_out + moved, attended, kept[k], sent[k]))
        if k == 0:
            arrived[k] = to_partner(sent[k])
        if bit == 4:
            arrived[3] = to_partner(sent[3])
            rank_out, arrived[0] = tie((rank_out, arrived[0]))
    rank_out, arrived[3] = tie((rank_out, arrived[3]))
    pair_right = jnp.concatenate([near_right, far_right], axis=0)

    def adapt(slot, half, kept, first, arrived):
        if half:
            outs = [shape(block, model_width, jnp.bfloat16 if slot else jnp.float32)]
        else:
            outs = [shape(block, model_width, jnp.float32)] * 2
        return call(
            functools.partial(adapt_kernel, slot, first),
            [rank_out, meta, spread_own, pair_right, kept, arrived],
            outs,
            info,
        )

    chain_a = along_ring(adapt(1, True, kept[0], 2 * block, arrived[0])[0])
    chain_b = None
    for s in (3, 2, 1):
        add_a, add_b = adapt(2 * s + 1, False, kept[s], 0, arrived[s])
        if s > 1:
            arrived[s - 1] = to_partner(sent[s - 1])
        if chain_b is None:
            chain_b = along_ring(narrow(add_b))
            chain_a = along_ring(narrow(wide(chain_a) + add_a))
        else:
            chain_a = along_ring(narrow(wide(chain_a) + add_a))
            chain_b = along_ring(narrow(wide(chain_b) + add_b))
    own_sum = adapt(0, True, kept[0], 0, tokens)[0]
    chain_a, own_sum = tie((chain_a, own_sum))
    arrived_last = to_partner(narrow(wide(chain_b) + kept[0][block : 2 * block]))
    return narrow(wide(chain_a) + wide(arrived_last) + own_sum + output_bias)


def solution(mesh):
    in_specs = (
        P(("req", "mlp"), None),
        P(),
        P(),
        P(None, "mlp", None),
        P("mlp", None, None),
        P(None, "mlp"),
        P("mlp"),
        P("mlp", None),
        P(),
        P(None, "mlp"),
        P(None, "mlp", None),
        P(None, "mlp"),
        P("mlp", None, None),
        P("mlp", None),
        P("mlp", None),
        P(),
        P(),
        P("mlp"),
    )
    out_specs = P(("req", "mlp"), None)
    return jax.shard_map(
        per_device, mesh=mesh, in_specs=in_specs, out_specs=out_specs, check_vma=False
    )
```

```python
import functools
import math

import jax
import jax.numpy as jnp
import numpy as np
from jax import lax
from jax.experimental import pallas as pl
from jax.experimental.pallas import tpu as pltpu
from jax.sharding import PartitionSpec as P

HEAD_SIZE = 256
ROT = 64
ADAPTER_RANK = 16
EPSILON = 1e-05
NEGATIVE_FILL = -1e30
RING = (0, 2, 4, 6, 7, 5, 3, 1)
PLACE = tuple(RING.index(pair) for pair in range(8))
CORE_PERM = [(i, i ^ 1) for i in range(16)]
RING_PERM = [(RING[i] * 2, RING[(i + 1) % 8] * 2) for i in range(8)] + [
    (RING[i] * 2 + 1, RING[(i - 1) % 8] * 2 + 1) for i in range(8)
]
SLOTS = 8
BLOCKS = 4
CORE, MLP, PAIRS, PLACES, BASES = 0, 1, 2, 2 + SLOTS, 2 + 2 * SLOTS


def to_partner(value):
    return lax.ppermute(value, "mlp", CORE_PERM)


def along_ring(value):
    return lax.ppermute(value, "mlp", RING_PERM)


def rank_product(left_side, right_side):
    return jnp.dot(left_side, right_side, preferred_element_type=jnp.float32)


def across(left_side, right_side):
    return lax.dot_general(
        left_side, right_side, (((1,), (1,)), ((), ())), preferred_element_type=jnp.float32
    )


def spread_table(period, first, width):
    row = np.arange(32)[:, None]
    column = np.arange(width)[None, :]
    return jnp.asarray((row - first == column % period).astype(np.float32), jnp.bfloat16)


def swap_halves(info, lanes):
    half = lanes.shape[1] // 2
    return jnp.where(info[CORE] == 1, pltpu.roll(lanes, half, 1), lanes)


def lane_ids(shape, period):
    return (lax.broadcasted_iota(jnp.int32, shape, 1) // period).astype(jnp.float32)


def pair_at(info, slot, rows):
    return pl.ds(pl.multiple_of(info[PAIRS + slot] * rows, rows), rows)


def store_lanes(info, out_ref, lanes, slots):
    width = out_ref.shape[1] // SLOTS
    for k, slot in enumerate(slots):
        part = lanes[:, k * width : (k + 1) * width]
        out_ref[:, pair_at(info, slot, width)] = swap_halves(info, part).astype(out_ref.dtype)


def rank_rows(info, rank_ref, slot, count):
    width = rank_ref.shape[1] // SLOTS
    lanes = [
        swap_halves(info, rank_ref[:, pair_at(info, slot + k, width)].astype(jnp.float32))
        for k in range(count)
    ]
    lanes = lanes[0] if count == 1 else jnp.concatenate(lanes, axis=1)
    return jnp.transpose(lanes).astype(jnp.bfloat16)


def widened(rows, spread_ref, adapter, columns):
    tile = rank_product(rows, spread_ref[...]).astype(jnp.bfloat16)
    group = lax.broadcasted_iota(jnp.int32, tile.shape, 1) // ADAPTER_RANK
    apart = (adapter - group.astype(jnp.float32)).astype(jnp.bfloat16)
    step = tile.shape[1] // ADAPTER_RANK
    zero = jnp.zeros_like(tile)
    return jnp.concatenate(
        [jnp.where(apart == first, tile, zero) for first in range(0, columns // ADAPTER_RANK, step)], axis=1
    )


def folded(products, adapter, spread_ref):
    width = spread_ref.shape[1]
    group = lax.broadcasted_iota(jnp.int32, (products.shape[0], width), 1) // ADAPTER_RANK
    apart = adapter - group.astype(jnp.float32)
    total = None
    for first in range(0, products.shape[1], width):
        part = products[:, first : first + width]
        part = jnp.where(apart == float(first // ADAPTER_RANK), part, 0.0)
        total = part if total is None else total + part
    return across(spread_ref[...], total.astype(jnp.bfloat16))


def cosine(angle):
    turns = jnp.floor(angle * (1.0 / math.pi) + 0.5)
    rest = ((angle - turns * 3.140625) - turns * 9.67502593994140625e-4) - turns * 1.509957990978376e-7
    square = rest * rest
    value = jnp.full_like(square, 1.0 / 479001600.0)
    for factor in (-1.0 / 3628800.0, 1.0 / 40320.0, -1.0 / 720.0, 1.0 / 24.0, -0.5, 1.0):
        value = value * square + factor
    odd = turns - 2.0 * jnp.floor(turns * 0.5)
    return value * (1.0 - 2.0 * odd)


def norm_kernel(x_hbm, gain_hbm, bias_hbm, out_ref, x_ref, gain_ref, bias_ref, sems):
    pairs = ((x_hbm, x_ref), (gain_hbm, gain_ref), (bias_hbm, bias_ref))
    copies = [pltpu.make_async_copy(a, b, sems.at[k]) for k, (a, b) in enumerate(pairs)]
    for copy in copies:
        copy.start()
    copies[0].wait()
    values = x_ref[...].astype(jnp.float32)
    center = values - jnp.mean(values, axis=1, keepdims=True)
    spread = jnp.mean(center * center, axis=1, keepdims=True)
    scaled = center * lax.rsqrt(spread + EPSILON)
    copies[1].wait()
    copies[2].wait()
    out_ref[...] = (scaled * gain_ref[...] + bias_ref[...]).astype(out_ref.dtype)


def local_tokens(info, slot, shape, dim):
    rows = shape[dim] // 2
    at = lax.broadcasted_iota(jnp.int32, shape, dim)
    second = at >= rows
    at = jnp.where(second, at - rows, at) + info[CORE] * (rows // 2)
    at = jnp.where(at >= rows, at - rows, at)
    return (at + jnp.where(second, info[BASES + slot + 1], info[BASES + slot])).astype(jnp.float32)


def token_kernel(info, column_ref, row_ref, ids_ref, table_ref, meta_ref, turn_ref):
    rows = 2 * 128
    count = row_ref.shape[1]
    earlier = lax.broadcasted_iota(jnp.int32, (count, count), 0) < lax.broadcasted_iota(
        jnp.int32, (count, count), 1
    )
    anchors = jnp.sum(jnp.where(earlier, column_ref[...], 0.0), axis=0, keepdims=True)
    endings = anchors + row_ref[...]
    ids = ids_ref[...]
    lane = lax.broadcasted_iota(jnp.int32, (rows, 128), 1)

    def one(block, _):
        token = local_tokens(info, 2 * block, (rows, 1), 0)
        inside = jnp.logical_and(anchors <= token, token < endings)
        start = jnp.sum(jnp.where(inside, anchors, 0.0), axis=1, keepdims=True)
        adapter = jnp.sum(jnp.where(inside, ids, 0.0), axis=1, keepdims=True)
        at = pl.ds(pl.multiple_of(block * rows, rows), rows)
        meta_ref[at, :] = jnp.where(lane < 64, start, adapter)
        angle = (token - start) * table_ref[0:1, :] - table_ref[1:2, :]
        turn_ref[at, :] = cosine(angle) * table_ref[2:3, :]
        return 0

    lax.fori_loop(0, meta_ref.shape[0] // rows, one, 0)


def rank_kernel(count, slots, info, *refs):
    x = jnp.concatenate([ref[...] for ref in refs[:count]], axis=0)
    left_ref, meta_ref, slot_ref, fold_ref, held_ref = refs[count : count + 5]
    out_ref = refs[-1]
    products = rank_product(x, left_ref[...])
    adapter = jnp.concatenate([meta_ref[k * 128 : (k + 1) * 128, 64:65] for k in slots], axis=0)
    chosen = jnp.where(slot_ref[...] == adapter, products, 0.0).astype(jnp.bfloat16)
    out_ref[...] = held_ref[...]
    store_lanes(info, out_ref, across(fold_ref[...], chosen), slots)


def base_kernel(count, *refs):
    x = jnp.concatenate([ref[...] for ref in refs[:count]], axis=0)
    qkv_ref, up_ref, base_ref, up_base_ref, shared_ref = refs[count:]
    first = rank_product(x, qkv_ref[...])
    base_ref[...] = first
    shared_ref[...] = first[:, HEAD_SIZE:].astype(shared_ref.dtype)
    up_base_ref[...] = rank_product(x, up_ref[...])


def turn(part, table):
    width = table.shape[1]
    lane = lax.broadcasted_iota(jnp.int32, table.shape, 1)
    cos = jnp.where(lane < ROT, table, 1.0)
    sin = jnp.where(lane < ROT, pltpu.roll(table, width - ROT, 1), 0.0)
    head = part[:, :width]
    swapped = jnp.where(
        lane % 2 == 0, pltpu.roll(head, width - 1, 1), pltpu.roll(head, 1, 1)
    )
    return jnp.concatenate([head * cos + swapped * sin, part[:, width:]], axis=1)


def block_rows_of(refs, block):
    if block == 0:
        return jnp.concatenate([refs[0][:128], refs[3][128:]], axis=0)
    if block == 3:
        return jnp.concatenate([refs[2][...], refs[3][:128]], axis=0)
    return refs[0][128:] if block == 1 else refs[1][...]


def two_blocks(refs, index):
    return jnp.concatenate([block_rows_of(refs, 2 * index + k) for k in (0, 1)], axis=0)


def inner_kernel(info, *refs):
    base_refs, up_refs, (rank_ref, meta_ref, turn_ref, first_ref, last_ref) = refs[:4], refs[4:8], refs[8:13]
    qkv_right_ref, up_right_ref, bias_ref, left_ref = refs[13:17]
    q_ref, k_ref, v_ref, hidden_ref, out_ref = refs[17:]
    rows = 512
    columns = qkv_right_ref.shape[0]
    for block in range(BLOCKS // 2):
        at = slice(block * rows, (block + 1) * rows)
        adapter = meta_ref[at, 64:65]
        ranks = rank_rows(info, rank_ref, 4 * block, 4)
        total = two_blocks(base_refs, block) + rank_product(
            widened(ranks, first_ref, adapter, columns), qkv_right_ref[...]
        )
        table = turn_ref[at, :]
        q_ref[at, :] = (turn(total[:, :HEAD_SIZE], table) * HEAD_SIZE ** (-0.5)).astype(jnp.bfloat16)
        k_ref[at, :] = turn(total[:, HEAD_SIZE : 2 * HEAD_SIZE], table).astype(jnp.bfloat16)
        v_ref[at, :] = total[:, 2 * HEAD_SIZE :].astype(jnp.bfloat16)
        wide = widened(ranks, last_ref, adapter, columns)
        x = two_blocks(up_refs, block) + rank_product(wide, up_right_ref[...]) + bias_ref[...]
        inner = math.sqrt(2.0 / math.pi) * (x + 0.044715 * (x * x * x))
        hidden = (0.5 * x * (1.0 + jnp.tanh(inner))).astype(jnp.bfloat16)
        hidden_ref[at, :] = hidden
        lanes = folded(rank_product(hidden, left_ref[...]), adapter, last_ref)
        store_lanes(info, out_ref, lanes, range(4 * block, 4 * block + 4))


def far_kernel(first_row, info, *refs):
    shared_refs, (rank_ref, meta_ref, turn_ref, spread_ref, right_ref, k_ref, v_ref) = refs[:4], refs[4:]
    rows = 512
    for block in range(BLOCKS // 2):
        at = slice(block * rows, (block + 1) * rows)
        far_at = slice(first_row + block * rows, first_row + (block + 1) * rows)
        ranks = rank_rows(info, rank_ref, 4 * block, 4)
        wide = widened(ranks, spread_ref, meta_ref[far_at, 64:65], right_ref.shape[0])
        total = two_blocks(shared_refs, block).astype(jnp.float32)
        total = total + rank_product(wide, right_ref[:, HEAD_SIZE:])
        k_ref[at, :] = turn(total[:, :HEAD_SIZE], turn_ref[far_at, :]).astype(jnp.bfloat16)
        v_ref[at, :] = total[:, HEAD_SIZE:].astype(jnp.bfloat16)


def attention_kernel(req_count, info, *refs):
    q_ref, refs = refs[0], refs[1:]
    key_refs, value_refs, refs = refs[:req_count], refs[req_count : 2 * req_count], refs[2 * req_count :]
    meta_ref, spread_ref, left_ref, hidden_rank_ref, attended_ref, out_ref = refs[:6]
    keys_ref, values_ref, scores_ref, top_ref, sum_ref, acc_ref, fold_ref = refs[6:]
    span = 256
    rows = 2 * span
    pair = span // 2
    group_rows = q_ref.shape[0]

    def slot_rows(slot):
        return pl.ds(pl.multiple_of(slot * pair, pair), pair)

    for d in range(req_count):
        for k in range(SLOTS):
            at = slice((req_count - 1 - d) * group_rows + k * pair, (req_count - 1 - d) * group_rows + (k + 1) * pair)
            slot = slot_rows(info[PLACES + k])
            keys_ref[at, :] = key_refs[d][slot, :]
            values_ref[at, :] = value_refs[d][slot, :]
    first_token = info[BASES + info[PLACES]] - (req_count - 1) * group_rows

    def places(shape, dim):
        at = lax.broadcasted_iota(jnp.int32, shape, dim)
        before = at // pair * pair
        at = at - before + info[CORE] * (pair // 2)
        return (before + jnp.where(at >= pair, at - pair, at)).astype(jnp.float32)

    key_place = places((1, span), 1)
    query_place = places((rows, 1), 0)

    def one(block, _):
        slots = [slot_rows(info[PLACES + 4 * block + k]) for k in range(4)]

        def both(ref):
            return jnp.concatenate([ref[at, :] for at in slots], axis=0)

        meta = both(meta_ref)
        start = meta[:, 0:1]
        number = (req_count - 1) * BLOCKS + 2 * block
        query = query_place + (first_token + number * span).astype(jnp.float32)
        q = both(q_ref)
        lowest = jnp.min(start).astype(jnp.int32) - first_token
        top_ref[...] = jnp.full_like(top_ref, NEGATIVE_FILL)
        sum_ref[...] = jnp.zeros_like(sum_ref)
        acc_ref[...] = jnp.zeros_like(acc_ref)

        def score(j, _):
            at = pl.ds(pl.multiple_of(j * span, span), span)
            scores = across(q, keys_ref[at, :])
            key = key_place + (first_token + j * span).astype(jnp.float32)
            allowed = jnp.logical_and(key <= query, key >= start)
            scores = jnp.where(allowed, scores, NEGATIVE_FILL)
            scores_ref[:, at] = scores
            top_ref[...] = jnp.maximum(top_ref[...], jnp.maximum(scores[:, :pair], scores[:, pair:]))
            return 0

        lax.fori_loop(lowest // span, number + 2, score, 0)
        top = jnp.max(top_ref[...], axis=1, keepdims=True)

        def weigh(j, _):
            at = pl.ds(pl.multiple_of(j * span, span), span)
            weights = jnp.exp(scores_ref[:, at] - top)
            sum_ref[...] = sum_ref[...] + (weights[:, :pair] + weights[:, pair:])
            acc_ref[...] = acc_ref[...] + rank_product(weights.astype(jnp.bfloat16), values_ref[at, :])
            return 0

        lax.fori_loop(lowest // span, number + 2, weigh, 0)
        total = jnp.sum(sum_ref[...], axis=1, keepdims=True)
        attended = (acc_ref[...] / total).astype(jnp.bfloat16)
        lanes = folded(rank_product(attended, left_ref[...]), meta[:, 64:65], spread_ref)
        for k in range(4):
            attended_ref[slots[k], :] = attended[k * pair : (k + 1) * pair]
            at = pl.ds(pl.multiple_of((4 * block + k) * pair, pair), pair)
            fold_ref[:, at] = swap_halves(info, lanes[:, k * pair : (k + 1) * pair])
        return 0

    lax.fori_loop(0, BLOCKS // 2, one, 0)
    out_ref[...] = (fold_ref[...] + hidden_rank_ref[...].astype(jnp.float32)).astype(out_ref.dtype)


def main_kernel(block, attended_ref, hidden_ref, output_ref, down_ref, kept_ref, sent_ref):
    rows = 256
    sent = sent_ref.shape[0]
    width = 512
    attended = attended_ref[block * rows : (block + 1) * rows, :]
    hidden = hidden_ref[block * rows : (block + 1) * rows, :]

    for step in range(output_ref.shape[1] // width):
        at = slice(step * width, (step + 1) * width)
        total = rank_product(attended, output_ref[:, at]) + rank_product(hidden, down_ref[:, at])
        if block:
            sent_ref[:, at] = total[:sent].astype(sent_ref.dtype)
            kept_ref[:, at] = total[sent:]
        else:
            kept_ref[:, at] = total[: rows - sent]
            sent_ref[:, at] = total[rows - sent :].astype(sent_ref.dtype)


def adapt_kernel(slot, first, info, rank_ref, meta_ref, spread_ref, right_ref, kept_ref, arrived_ref, *out_refs):
    pair = 128
    half = pair // 2
    columns = spread_ref.shape[1]
    count = columns // (4 * ADAPTER_RANK)
    column_id = lax.broadcasted_iota(jnp.int32, (pair, columns), 1) // (2 * ADAPTER_RANK)
    partner = info[MLP] + 1 - 2 * info[CORE]
    column_id = column_id + jnp.where(column_id < count, info[MLP] * count, (partner - 1) * count)
    own = column_id.astype(jnp.float32) == meta_ref[slot * pair : (slot + 1) * pair, 64:65]
    spread = rank_product(rank_rows(info, rank_ref, slot, 1), spread_ref[...])
    wide = jnp.where(own, spread, 0.0).astype(jnp.bfloat16)
    width = 512

    for step in range(right_ref.shape[1] // width):
        at = slice(step * width, (step + 1) * width)
        if len(out_refs) == 1:
            total = rank_product(wide[:half], right_ref[:, at]) + kept_ref[first : first + half, at]
            total = total + arrived_ref[:, at].astype(jnp.float32)
            out_refs[0][:, at] = total.astype(out_refs[0].dtype)
        else:
            total = rank_product(wide, right_ref[:, at]) + kept_ref[:, at]
            out_refs[0][:, at] = total[:half] + arrived_ref[half:, at].astype(jnp.float32)
            out_refs[1][:, at] = total[half:] + arrived_ref[:half, at].astype(jnp.float32)


def call(kernel, operands, outs, info=None, scratch=(), mib=24, flops=1000, space=pltpu.VMEM):
    vmem = pl.BlockSpec(memory_space=pltpu.VMEM)
    specs = [pl.BlockSpec(memory_space=space)] * len(operands)
    if info is not None:
        operands, specs = [info] + operands, [pl.BlockSpec(memory_space=pltpu.SMEM)] + specs
    return pl.pallas_call(
        kernel,
        in_specs=specs,
        out_specs=[vmem] * len(outs),
        out_shape=outs,
        scratch_shapes=scratch,
        compiler_params=pltpu.CompilerParams(vmem_limit_bytes=mib * 1024 * 1024),
        cost_estimate=pl.CostEstimate(flops=flops, bytes_accessed=1000, transcendentals=0),
    )(*operands)


def shape(rows, width, dtype=jnp.bfloat16):
    return jax.ShapeDtypeStruct((rows, width), dtype)


def sum_over_mlp(value, bits):
    for bit in bits:
        value = value + lax.ppermute(value, "mlp", [(i, i ^ bit) for i in range(16)])
    return value


def narrow(value):
    return value.astype(jnp.bfloat16)


def wide(value):
    return value.astype(jnp.float32)


def per_device(
    tokens,
    layer_norm_gain,
    layer_norm_bias,
    query_key_weight,
    output_weight,
    up_weight,
    input_bias,
    down_weight,
    output_bias,
    input_adapter_left,
    query_key_value_right,
    up_adapter_right,
    output_adapter_left,
    down_adapter_left,
    output_adapter_right,
    lengths,
    request_adapter,
    slot_adapter,
):
    block = tokens.shape[0]
    model_width = tokens.shape[1]
    pair_rows = 2 * block
    group_rows = SLOTS * pair_rows
    req_count = lax.axis_size("req")
    group = lax.axis_index("req")
    me = lax.axis_index("mlp")
    block_rows = 2 * pair_rows
    table = np.zeros((req_count, 16, 2 + SLOTS * (2 + req_count)), np.int32)
    for g in range(req_count):
        for m in range(16):
            side = 2 * (m % 2) - 1
            steps = [0, 4] + [t for s in (1, 2, 3) for t in (side * s, -side * s)]
            pairs = [RING[(PLACE[m // 2] + t) % 8] for t in steps]
            firsts = [(g - d) * group_rows + p * pair_rows for d in range(req_count) for p in pairs]
            table[g, m] = [m % 2, m] + pairs + [pairs.index(p) for p in range(SLOTS)] + firsts
    info = lax.dynamic_slice(jnp.asarray(table), (group, me, 0), (1, 1, table.shape[2])).reshape(-1)

    norm_args = [tokens, layer_norm_gain.reshape(1, -1), layer_norm_bias.reshape(1, -1)]
    own = call(
        norm_kernel,
        norm_args,
        [shape(block, model_width)],
        scratch=[pltpu.VMEM(x.shape, x.dtype) for x in norm_args] + [pltpu.SemaphoreType.DMA((3,))],
        space=pl.ANY,
    )[0]
    other = to_partner(own)
    ring_a, ring_b = along_ring(own), along_ring(other)
    pair_left = jnp.concatenate([input_adapter_left, to_partner(input_adapter_left)], axis=1)

    float_lengths = wide(lengths)
    lane = np.arange(128)
    turn_rows = np.zeros((8, 128), np.float32)
    turn_rows[0] = np.exp(lane % ROT // 2 * (-2.0 * math.log(10000.0) / ROT))
    turn_rows[1] = np.where(lane < ROT, 0.0, math.pi / 2)
    turn_rows[2] = np.where(lane < ROT, 1.0, np.where(lane % 2 == 0, -1.0, 1.0))
    token_rows = req_count * group_rows
    token_args = [
        float_lengths[:, None],
        float_lengths[None, :],
        wide(request_adapter)[None, :],
        jnp.asarray(turn_rows),
    ]
    meta, turns = call(token_kernel, token_args, [shape(token_rows, 128, jnp.float32)] * 2, info)

    qkv_rows = query_key_weight.reshape(model_width, 3 * HEAD_SIZE)
    adapter_columns = query_key_value_right.shape[0]
    qkv_right = query_key_value_right.reshape(adapter_columns, 3 * HEAD_SIZE)
    spread_first = spread_table(ADAPTER_RANK, 0, 128)
    spread_last = spread_table(ADAPTER_RANK, ADAPTER_RANK, 128)
    near_right = output_adapter_right
    slot_columns = wide(jnp.repeat(slot_adapter, 2 * ADAPTER_RANK))[None, :]
    slot_columns = jnp.concatenate([slot_columns, to_partner(slot_columns)], axis=1)
    own_columns = near_right.shape[0]
    spread_own = spread_table(2 * ADAPTER_RANK, 0, 2 * own_columns)
    hidden_width = up_weight.shape[1]

    def to_group(value, d):
        return lax.ppermute(value, "req", [(g, g + d) for g in range(req_count - d)])

    held = functools.partial(pltpu.VMEM, dtype=jnp.float32)

    def add_ranks(part, slots, so_far, ahead=()):
        return call(
            functools.partial(rank_kernel, len(part), slots),
            list(part) + [pair_left, meta, slot_columns, spread_own, so_far, *ahead],
            [shape(32, group_rows)],
            info,
        )[0]

    def products_of(part, flops=1000):
        rows = len(part) * block
        return call(
            functools.partial(base_kernel, len(part)),
            list(part) + [qkv_rows, up_weight],
            [
                shape(rows, 3 * HEAD_SIZE, jnp.float32),
                shape(rows, hidden_width, jnp.float32),
                shape(rows, 2 * HEAD_SIZE),
            ],
            flops=flops,
        )

    def to_groups(value):
        return [to_group(value, d) for d in range(1, req_count)]

    def arrivals(a, b):
        return a, b, to_partner(b), to_partner(a)

    tie = lax.optimization_barrier
    own_part = (own, other)
    ring_a, meta, turns, pair_left = tie((ring_a, meta, turns, pair_left))
    ranks = add_ranks(own_part, (0,), jnp.zeros((32, group_rows), jnp.bfloat16), (qkv_rows, up_weight))
    ring_b, ranks = tie((ring_b, ranks))
    part = arrivals(ring_a, ring_b)
    ring_a, ring_b = along_ring(ring_a), along_ring(ring_b)
    ranks = add_ranks(part, (2, 3), ranks)
    first = products_of(own_part + part)
    ring_b, ranks, first = tie((ring_b, ranks, first))
    part = arrivals(ring_a, ring_b)
    ring_a, ring_b = along_ring(ring_a), along_ring(ring_b)
    far_right = to_partner(near_right)
    far_early = to_groups(first[2])
    ranks = add_ranks(part, (4, 5), ranks)
    second = products_of(part)
    ring_b, ranks, second, far_right = tie((ring_b, ranks, second, far_right))
    part = arrivals(ring_a, ring_b)
    ring_a = along_ring(ring_a)
    held_rows = part[:2]
    third = products_of(held_rows, 2000000000)
    ranks = add_ranks(held_rows, (6,), ranks)
    ring_a, ranks, third, far_early = tie((ring_a, ranks, third, far_early))
    part = part[2:] + (ring_a, to_partner(ring_a))
    ranks = add_ranks(part, (7, 1), ranks)
    moved = lax.ppermute(ranks, "mlp", [(i, i ^ 2) for i in range(16)])
    fourth = products_of(part)
    ranks, fourth = tie((ranks + moved, fourth))
    far_late = to_groups(jnp.concatenate([second[2], third[2], fourth[2]], axis=0))
    rank_in = sum_over_mlp(ranks, (4, 8))
    products = (first, second, third, fourth)

    bias_row = input_bias.reshape(1, -1)
    far_rank = to_groups(rank_in)
    queries, own_keys, own_values, hidden, hidden_rank = call(
        inner_kernel,
        [part[0] for part in products]
        + [part[1] for part in products]
        + [rank_in, meta, turns, spread_first, spread_last]
        + [qkv_right, up_adapter_right, bias_row, down_adapter_left],
        [shape(group_rows, HEAD_SIZE)] * 3 + [shape(group_rows, hidden_width), shape(32, group_rows)],
        info,
    )
    keys, values = [own_keys], [own_values]
    for d in range(1, req_count):
        early, late = far_early[d - 1], far_late[d - 1]
        ends = (0, block_rows, block_rows + pair_rows, 2 * block_rows + pair_rows)
        shared = [early] + [late[ends[k] : ends[k + 1]] for k in range(3)]
        far_keys, far_values = call(
            functools.partial(far_kernel, d * group_rows),
            shared + [far_rank[d - 1], meta, turns, spread_first, qkv_right],
            [shape(group_rows, HEAD_SIZE)] * 2,
            info,
        )
        keys.append(far_keys)
        values.append(far_values)

    output_left = output_adapter_left.reshape(HEAD_SIZE, adapter_columns)
    attended, rank_out = call(
        functools.partial(attention_kernel, req_count),
        [queries] + keys + values + [meta, spread_first, output_left, hidden_rank],
        [shape(group_rows, HEAD_SIZE), shape(32, group_rows)],
        info,
        [
            pltpu.VMEM((req_count * group_rows, HEAD_SIZE), jnp.bfloat16),
            pltpu.VMEM((req_count * group_rows, HEAD_SIZE), jnp.bfloat16),
            held((2 * block_rows, req_count * group_rows)),
            held((2 * block_rows, 128)),
            held((2 * block_rows, 128)),
            held((2 * block_rows, HEAD_SIZE)),
            held((32, group_rows)),
        ],
        mib=24 + 3 * req_count,
    )
    output_rows = output_weight.reshape(HEAD_SIZE, model_width)

    def main(k, attended, hidden):
        sent = block if k == 0 else pair_rows
        return call(
            functools.partial(main_kernel, k),
            [attended, hidden, output_rows, down_weight],
            [shape(block_rows - sent, model_width, jnp.float32), shape(sent, model_width)],
        )

    kept, arrived, sent = {}, {}, {}
    for bit, k in zip((1, 2, 4, 8), (0, 3, 2, 1)):
        moved = lax.ppermute(rank_out, "mlp", [(i, i ^ bit) for i in range(16)])
        kept[k], sent[k] = main(k, attended, hidden)
        rank_out, attended, kept[k], sent[k] = tie((rank_out + moved, attended, kept[k], sent[k]))
        if k == 0:
            arrived[k] = to_partner(sent[k])
        if bit == 4:
            arrived[3] = to_partner(sent[3])
            rank_out, arrived[0] = tie((rank_out, arrived[0]))
    rank_out, arrived[3] = tie((rank_out, arrived[3]))
    pair_right = jnp.concatenate([near_right, far_right], axis=0)

    def adapt(slot, half, kept, first, arrived):
        if half:
            outs = [shape(block, model_width, jnp.bfloat16 if slot else jnp.float32)]
        else:
            outs = [shape(block, model_width, jnp.float32)] * 2
        return call(
            functools.partial(adapt_kernel, slot, first),
            [rank_out, meta, spread_own, pair_right, kept, arrived],
            outs,
            info,
        )

    chain_a = along_ring(adapt(1, True, kept[0], 2 * block, arrived[0])[0])
    chain_b = None
    for s in (3, 2, 1):
        add_a, add_b = adapt(2 * s + 1, False, kept[s], 0, arrived[s])
        if s > 1:
            arrived[s - 1] = to_partner(sent[s - 1])
        if chain_b is None:
            chain_b = along_ring(narrow(add_b))
            chain_a = along_ring(narrow(wide(chain_a) + add_a))
        else:
            chain_a = along_ring(narrow(wide(chain_a) + add_a))
            chain_b = along_ring(narrow(wide(chain_b) + add_b))
    own_sum = adapt(0, True, kept[0], 0, tokens)[0]
    chain_a, own_sum = tie((chain_a, own_sum))
    arrived_last = to_partner(narrow(wide(chain_b) + kept[0][block : 2 * block]))
    return narrow(wide(chain_a) + wide(arrived_last) + own_sum + output_bias)


def solution(mesh):
    in_specs = (
        P(("req", "mlp"), None),
        P(),
        P(),
        P(None, "mlp", None),
        P("mlp", None, None),
        P(None, "mlp"),
        P("mlp"),
        P("mlp", None),
        P(),
        P(None, "mlp"),
        P(None, "mlp", None),
        P(None, "mlp"),
        P("mlp", None, None),
        P("mlp", None),
        P("mlp", None),
        P(),
        P(),
        P("mlp"),
    )
    out_specs = P(("req", "mlp"), None)
    return jax.shard_map(
        per_device, mesh=mesh, in_specs=in_specs, out_specs=out_specs, check_vma=False
    )
```

```python
import functools
import math

import jax
import jax.numpy as jnp
import numpy as np
from jax import lax
from jax.experimental import pallas as pl
from jax.experimental.pallas import tpu as pltpu
from jax.sharding import PartitionSpec as P

HEAD_SIZE = 256
ROT = 64
ADAPTER_RANK = 16
EPSILON = 1e-05
NEGATIVE_FILL = -1e30
RING = (0, 2, 4, 6, 7, 5, 3, 1)
PLACE = tuple(RING.index(pair) for pair in range(8))
CORE_PERM = [(i, i ^ 1) for i in range(16)]
RING_PERM = [(RING[i] * 2, RING[(i + 1) % 8] * 2) for i in range(8)] + [
    (RING[i] * 2 + 1, RING[(i - 1) % 8] * 2 + 1) for i in range(8)
]
SLOTS = 8
BLOCKS = 4
CORE, MLP, PAIRS, PLACES, BASES = 0, 1, 2, 2 + SLOTS, 2 + 2 * SLOTS


def to_partner(value):
    return lax.ppermute(value, "mlp", CORE_PERM)


def along_ring(value):
    return lax.ppermute(value, "mlp", RING_PERM)


def rank_product(left_side, right_side):
    return jnp.dot(left_side, right_side, preferred_element_type=jnp.float32)


def across(left_side, right_side):
    return lax.dot_general(
        left_side, right_side, (((1,), (1,)), ((), ())), preferred_element_type=jnp.float32
    )


def spread_table(period, first, width):
    row = np.arange(32)[:, None]
    column = np.arange(width)[None, :]
    return jnp.asarray((row - first == column % period).astype(np.float32), jnp.bfloat16)


def swap_halves(info, lanes):
    half = lanes.shape[1] // 2
    return jnp.where(info[CORE] == 1, pltpu.roll(lanes, half, 1), lanes)


def lane_ids(shape, period):
    return (lax.broadcasted_iota(jnp.int32, shape, 1) // period).astype(jnp.float32)


def pair_at(info, slot, rows):
    return pl.ds(pl.multiple_of(info[PAIRS + slot] * rows, rows), rows)


def store_lanes(info, out_ref, lanes, slots):
    width = out_ref.shape[1] // SLOTS
    for k, slot in enumerate(slots):
        part = lanes[:, k * width : (k + 1) * width]
        out_ref[:, pair_at(info, slot, width)] = swap_halves(info, part).astype(out_ref.dtype)


def rank_rows(info, rank_ref, slot, count):
    width = rank_ref.shape[1] // SLOTS
    lanes = [
        swap_halves(info, rank_ref[:, pair_at(info, slot + k, width)].astype(jnp.float32))
        for k in range(count)
    ]
    lanes = lanes[0] if count == 1 else jnp.concatenate(lanes, axis=1)
    return jnp.transpose(lanes).astype(jnp.bfloat16)


def widened(rows, spread_ref, adapter, columns):
    tile = rank_product(rows, spread_ref[...]).astype(jnp.bfloat16)
    group = lax.broadcasted_iota(jnp.int32, tile.shape, 1) // ADAPTER_RANK
    apart = (adapter - group.astype(jnp.float32)).astype(jnp.bfloat16)
    step = tile.shape[1] // ADAPTER_RANK
    zero = jnp.zeros_like(tile)
    return jnp.concatenate(
        [jnp.where(apart == first, tile, zero) for first in range(0, columns // ADAPTER_RANK, step)], axis=1
    )


def folded(products, adapter, spread_ref):
    width = spread_ref.shape[1]
    group = lax.broadcasted_iota(jnp.int32, (products.shape[0], width), 1) // ADAPTER_RANK
    apart = adapter - group.astype(jnp.float32)
    total = None
    for first in range(0, products.shape[1], width):
        part = products[:, first : first + width]
        part = jnp.where(apart == float(first // ADAPTER_RANK), part, 0.0)
        total = part if total is None else total + part
    return across(spread_ref[...], total.astype(jnp.bfloat16))


def cosine(angle):
    turns = jnp.floor(angle * (1.0 / math.pi) + 0.5)
    rest = ((angle - turns * 3.140625) - turns * 9.67502593994140625e-4) - turns * 1.509957990978376e-7
    square = rest * rest
    value = jnp.full_like(square, 1.0 / 479001600.0)
    for factor in (-1.0 / 3628800.0, 1.0 / 40320.0, -1.0 / 720.0, 1.0 / 24.0, -0.5, 1.0):
        value = value * square + factor
    odd = turns - 2.0 * jnp.floor(turns * 0.5)
    return value * (1.0 - 2.0 * odd)


def norm_kernel(x_hbm, gain_hbm, bias_hbm, out_ref, x_ref, gain_ref, bias_ref, sems):
    pairs = ((x_hbm, x_ref), (gain_hbm, gain_ref), (bias_hbm, bias_ref))
    copies = [pltpu.make_async_copy(a, b, sems.at[k]) for k, (a, b) in enumerate(pairs)]
    for copy in copies:
        copy.start()
    copies[0].wait()
    values = x_ref[...].astype(jnp.float32)
    center = values - jnp.mean(values, axis=1, keepdims=True)
    spread = jnp.mean(center * center, axis=1, keepdims=True)
    scaled = center * lax.rsqrt(spread + EPSILON)
    copies[1].wait()
    copies[2].wait()
    out_ref[...] = (scaled * gain_ref[...] + bias_ref[...]).astype(out_ref.dtype)


def local_tokens(info, slot, shape, dim):
    rows = shape[dim] // 2
    at = lax.broadcasted_iota(jnp.int32, shape, dim)
    second = at >= rows
    at = jnp.where(second, at - rows, at) + info[CORE] * (rows // 2)
    at = jnp.where(at >= rows, at - rows, at)
    return (at + jnp.where(second, info[BASES + slot + 1], info[BASES + slot])).astype(jnp.float32)


def token_kernel(info, column_ref, row_ref, ids_ref, table_ref, *refs):
    count = (len(refs) - 3) // 2
    meta_ref, turn_ref = refs[count : count + 2]
    pairs = zip(refs[:count], refs[count + 2 : -1])
    copies = [pltpu.make_async_copy(a, b, refs[-1].at[k]) for k, (a, b) in enumerate(pairs)]
    for copy in copies:
        copy.start()
    rows = 2 * 128
    count = row_ref.shape[1]
    earlier = lax.broadcasted_iota(jnp.int32, (count, count), 0) < lax.broadcasted_iota(
        jnp.int32, (count, count), 1
    )
    anchors = jnp.sum(jnp.where(earlier, column_ref[...], 0.0), axis=0, keepdims=True)
    endings = anchors + row_ref[...]
    ids = ids_ref[...]
    lane = lax.broadcasted_iota(jnp.int32, (rows, 128), 1)

    def one(block, _):
        token = local_tokens(info, 2 * block, (rows, 1), 0)
        inside = jnp.logical_and(anchors <= token, token < endings)
        start = jnp.sum(jnp.where(inside, anchors, 0.0), axis=1, keepdims=True)
        adapter = jnp.sum(jnp.where(inside, ids, 0.0), axis=1, keepdims=True)
        at = pl.ds(pl.multiple_of(block * rows, rows), rows)
        meta_ref[at, :] = jnp.where(lane < 64, start, adapter)
        angle = (token - start) * table_ref[0:1, :] - table_ref[1:2, :]
        turn_ref[at, :] = cosine(angle) * table_ref[2:3, :]
        return 0

    lax.fori_loop(0, meta_ref.shape[0] // rows, one, 0)
    for copy in copies:
        copy.wait()


def rank_kernel(count, slots, info, *refs):
    x = jnp.concatenate([ref[...] for ref in refs[:count]], axis=0)
    left_ref, meta_ref, slot_ref, fold_ref, held_ref = refs[count : count + 5]
    out_ref = refs[-1]
    products = rank_product(x, left_ref[...])
    adapter = jnp.concatenate([meta_ref[k * 128 : (k + 1) * 128, 64:65] for k in slots], axis=0)
    chosen = jnp.where(slot_ref[...] == adapter, products, 0.0).astype(jnp.bfloat16)
    out_ref[...] = held_ref[...]
    store_lanes(info, out_ref, across(fold_ref[...], chosen), slots)


def base_kernel(count, *refs):
    x = jnp.concatenate([ref[...] for ref in refs[:count]], axis=0)
    qkv_ref, up_ref, base_ref, up_base_ref, shared_ref = refs[count:]
    first = rank_product(x, qkv_ref[...])
    base_ref[...] = first
    shared_ref[...] = first[:, HEAD_SIZE:].astype(shared_ref.dtype)
    up_base_ref[...] = rank_product(x, up_ref[...])


def turn(part, table):
    width = table.shape[1]
    lane = lax.broadcasted_iota(jnp.int32, table.shape, 1)
    cos = jnp.where(lane < ROT, table, 1.0)
    sin = jnp.where(lane < ROT, pltpu.roll(table, width - ROT, 1), 0.0)
    head = part[:, :width]
    swapped = jnp.where(
        lane % 2 == 0, pltpu.roll(head, width - 1, 1), pltpu.roll(head, 1, 1)
    )
    return jnp.concatenate([head * cos + swapped * sin, part[:, width:]], axis=1)


def block_rows_of(refs, block):
    if block == 0:
        return jnp.concatenate([refs[0][:128], refs[3][128:]], axis=0)
    if block == 3:
        return jnp.concatenate([refs[2][...], refs[3][:128]], axis=0)
    return refs[0][128:] if block == 1 else refs[1][...]


def two_blocks(refs, index):
    return jnp.concatenate([block_rows_of(refs, 2 * index + k) for k in (0, 1)], axis=0)


def inner_kernel(info, *refs):
    base_refs, up_refs, (rank_ref, meta_ref, turn_ref, first_ref, last_ref) = refs[:4], refs[4:8], refs[8:13]
    qkv_right_ref, up_right_ref, bias_ref, left_ref = refs[13:17]
    q_ref, k_ref, v_ref, hidden_ref, out_ref = refs[17:]
    rows = 512
    columns = qkv_right_ref.shape[0]
    for block in range(BLOCKS // 2):
        at = slice(block * rows, (block + 1) * rows)
        adapter = meta_ref[at, 64:65]
        ranks = rank_rows(info, rank_ref, 4 * block, 4)
        total = two_blocks(base_refs, block) + rank_product(
            widened(ranks, first_ref, adapter, columns), qkv_right_ref[...]
        )
        table = turn_ref[at, :]
        q_ref[at, :] = (turn(total[:, :HEAD_SIZE], table) * HEAD_SIZE ** (-0.5)).astype(jnp.bfloat16)
        k_ref[at, :] = turn(total[:, HEAD_SIZE : 2 * HEAD_SIZE], table).astype(jnp.bfloat16)
        v_ref[at, :] = total[:, 2 * HEAD_SIZE :].astype(jnp.bfloat16)
        wide = widened(ranks, last_ref, adapter, columns)
        x = two_blocks(up_refs, block) + rank_product(wide, up_right_ref[...]) + bias_ref[...]
        inner = math.sqrt(2.0 / math.pi) * (x + 0.044715 * (x * x * x))
        hidden = (0.5 * x * (1.0 + jnp.tanh(inner))).astype(jnp.bfloat16)
        hidden_ref[at, :] = hidden
        lanes = folded(rank_product(hidden, left_ref[...]), adapter, last_ref)
        store_lanes(info, out_ref, lanes, range(4 * block, 4 * block + 4))


def far_kernel(first_row, info, *refs):
    shared_refs, (rank_ref, meta_ref, turn_ref, spread_ref, right_ref, k_ref, v_ref) = refs[:4], refs[4:]
    rows = 512
    for block in range(BLOCKS // 2):
        at = slice(block * rows, (block + 1) * rows)
        far_at = slice(first_row + block * rows, first_row + (block + 1) * rows)
        ranks = rank_rows(info, rank_ref, 4 * block, 4)
        wide = widened(ranks, spread_ref, meta_ref[far_at, 64:65], right_ref.shape[0])
        total = two_blocks(shared_refs, block).astype(jnp.float32)
        total = total + rank_product(wide, right_ref[:, HEAD_SIZE:])
        k_ref[at, :] = turn(total[:, :HEAD_SIZE], turn_ref[far_at, :]).astype(jnp.bfloat16)
        v_ref[at, :] = total[:, HEAD_SIZE:].astype(jnp.bfloat16)


def attention_kernel(req_count, info, *refs):
    q_ref, refs = refs[0], refs[1:]
    key_refs, value_refs, refs = refs[:req_count], refs[req_count : 2 * req_count], refs[2 * req_count :]
    meta_ref, spread_ref, left_ref, hidden_rank_ref, attended_ref, out_ref = refs[:6]
    keys_ref, values_ref, scores_ref, top_ref, sum_ref, acc_ref, fold_ref = refs[6:]
    span = 256
    rows = 2 * span
    pair = span // 2
    group_rows = q_ref.shape[0]

    def slot_rows(slot):
        return pl.ds(pl.multiple_of(slot * pair, pair), pair)

    for d in range(req_count):
        for k in range(SLOTS):
            at = slice((req_count - 1 - d) * group_rows + k * pair, (req_count - 1 - d) * group_rows + (k + 1) * pair)
            slot = slot_rows(info[PLACES + k])
            keys_ref[at, :] = key_refs[d][slot, :]
            values_ref[at, :] = value_refs[d][slot, :]
    first_token = info[BASES + info[PLACES]] - (req_count - 1) * group_rows

    def places(shape, dim):
        at = lax.broadcasted_iota(jnp.int32, shape, dim)
        before = at // pair * pair
        at = at - before + info[CORE] * (pair // 2)
        return (before + jnp.where(at >= pair, at - pair, at)).astype(jnp.float32)

    key_place = places((1, span), 1)
    query_place = places((rows, 1), 0)

    def one(block, _):
        slots = [slot_rows(info[PLACES + 4 * block + k]) for k in range(4)]

        def both(ref):
            return jnp.concatenate([ref[at, :] for at in slots], axis=0)

        meta = both(meta_ref)
        start = meta[:, 0:1]
        number = (req_count - 1) * BLOCKS + 2 * block
        query = query_place + (first_token + number * span).astype(jnp.float32)
        q = both(q_ref)
        lowest = jnp.min(start).astype(jnp.int32) - first_token
        top_ref[...] = jnp.full_like(top_ref, NEGATIVE_FILL)
        sum_ref[...] = jnp.zeros_like(sum_ref)
        acc_ref[...] = jnp.zeros_like(acc_ref)

        def score(j, _):
            at = pl.ds(pl.multiple_of(j * span, span), span)
            scores = across(q, keys_ref[at, :])
            key = key_place + (first_token + j * span).astype(jnp.float32)
            allowed = jnp.logical_and(key <= query, key >= start)
            scores = jnp.where(allowed, scores, NEGATIVE_FILL)
            scores_ref[:, at] = scores
            top_ref[...] = jnp.maximum(top_ref[...], jnp.maximum(scores[:, :pair], scores[:, pair:]))
            return 0

        lax.fori_loop(lowest // span, number + 2, score, 0)
        top = jnp.max(top_ref[...], axis=1, keepdims=True)

        def weigh(j, _):
            at = pl.ds(pl.multiple_of(j * span, span), span)
            weights = jnp.exp(scores_ref[:, at] - top)
            sum_ref[...] = sum_ref[...] + (weights[:, :pair] + weights[:, pair:])
            acc_ref[...] = acc_ref[...] + rank_product(weights.astype(jnp.bfloat16), values_ref[at, :])
            return 0

        lax.fori_loop(lowest // span, number + 2, weigh, 0)
        total = jnp.sum(sum_ref[...], axis=1, keepdims=True)
        attended = (acc_ref[...] / total).astype(jnp.bfloat16)
        lanes = folded(rank_product(attended, left_ref[...]), meta[:, 64:65], spread_ref)
        for k in range(4):
            attended_ref[slots[k], :] = attended[k * pair : (k + 1) * pair]
            at = pl.ds(pl.multiple_of((4 * block + k) * pair, pair), pair)
            fold_ref[:, at] = swap_halves(info, lanes[:, k * pair : (k + 1) * pair])
        return 0

    lax.fori_loop(0, BLOCKS // 2, one, 0)
    out_ref[...] = (fold_ref[...] + hidden_rank_ref[...].astype(jnp.float32)).astype(out_ref.dtype)


def main_kernel(block, attended_ref, hidden_ref, output_ref, down_ref, kept_ref, sent_ref):
    rows = 256
    sent = sent_ref.shape[0]
    width = 512
    attended = attended_ref[block * rows : (block + 1) * rows, :]
    hidden = hidden_ref[block * rows : (block + 1) * rows, :]

    for step in range(output_ref.shape[1] // width):
        at = slice(step * width, (step + 1) * width)
        total = rank_product(attended, output_ref[:, at]) + rank_product(hidden, down_ref[:, at])
        if block:
            sent_ref[:, at] = total[:sent].astype(sent_ref.dtype)
            kept_ref[:, at] = total[sent:]
        else:
            kept_ref[:, at] = total[: rows - sent]
            sent_ref[:, at] = total[rows - sent :].astype(sent_ref.dtype)


def adapt_kernel(slot, first, info, rank_ref, meta_ref, spread_ref, right_ref, kept_ref, arrived_ref, *out_refs):
    pair = 128
    half = pair // 2
    columns = spread_ref.shape[1]
    count = columns // (4 * ADAPTER_RANK)
    column_id = lax.broadcasted_iota(jnp.int32, (pair, columns), 1) // (2 * ADAPTER_RANK)
    partner = info[MLP] + 1 - 2 * info[CORE]
    column_id = column_id + jnp.where(column_id < count, info[MLP] * count, (partner - 1) * count)
    own = column_id.astype(jnp.float32) == meta_ref[slot * pair : (slot + 1) * pair, 64:65]
    spread = rank_product(rank_rows(info, rank_ref, slot, 1), spread_ref[...])
    wide = jnp.where(own, spread, 0.0).astype(jnp.bfloat16)
    width = 512

    for step in range(right_ref.shape[1] // width):
        at = slice(step * width, (step + 1) * width)
        if len(out_refs) == 1:
            total = rank_product(wide[:half], right_ref[:, at]) + kept_ref[first : first + half, at]
            total = total + arrived_ref[:, at].astype(jnp.float32)
            out_refs[0][:, at] = total.astype(out_refs[0].dtype)
        else:
            total = rank_product(wide, right_ref[:, at]) + kept_ref[:, at]
            out_refs[0][:, at] = total[:half] + arrived_ref[half:, at].astype(jnp.float32)
            out_refs[1][:, at] = total[half:] + arrived_ref[:half, at].astype(jnp.float32)


def call(kernel, operands, outs, info=None, scratch=(), mib=24, flops=1000, space=pltpu.VMEM, in_hbm=0):
    vmem = pl.BlockSpec(memory_space=pltpu.VMEM)
    specs = [pl.BlockSpec(memory_space=space)] * (len(operands) - in_hbm)
    specs += [pl.BlockSpec(memory_space=pltpu.HBM)] * in_hbm
    if info is not None:
        operands, specs = [info] + operands, [pl.BlockSpec(memory_space=pltpu.SMEM)] + specs
    return pl.pallas_call(
        kernel,
        in_specs=specs,
        out_specs=[vmem] * len(outs),
        out_shape=outs,
        scratch_shapes=scratch,
        compiler_params=pltpu.CompilerParams(vmem_limit_bytes=mib * 1024 * 1024),
        cost_estimate=pl.CostEstimate(flops=flops, bytes_accessed=1000, transcendentals=0),
    )(*operands)


def shape(rows, width, dtype=jnp.bfloat16):
    return jax.ShapeDtypeStruct((rows, width), dtype)


def sum_over_mlp(value, bits):
    for bit in bits:
        value = value + lax.ppermute(value, "mlp", [(i, i ^ bit) for i in range(16)])
    return value


def narrow(value):
    return value.astype(jnp.bfloat16)


def wide(value):
    return value.astype(jnp.float32)


def per_device(
    tokens,
    layer_norm_gain,
    layer_norm_bias,
    query_key_weight,
    output_weight,
    up_weight,
    input_bias,
    down_weight,
    output_bias,
    input_adapter_left,
    query_key_value_right,
    up_adapter_right,
    output_adapter_left,
    down_adapter_left,
    output_adapter_right,
    lengths,
    request_adapter,
    slot_adapter,
):
    block = tokens.shape[0]
    model_width = tokens.shape[1]
    pair_rows = 2 * block
    group_rows = SLOTS * pair_rows
    req_count = lax.axis_size("req")
    group = lax.axis_index("req")
    me = lax.axis_index("mlp")
    block_rows = 2 * pair_rows
    table = np.zeros((req_count, 16, 2 + SLOTS * (2 + req_count)), np.int32)
    for g in range(req_count):
        for m in range(16):
            side = 2 * (m % 2) - 1
            steps = [0, 4] + [t for s in (1, 2, 3) for t in (side * s, -side * s)]
            pairs = [RING[(PLACE[m // 2] + t) % 8] for t in steps]
            firsts = [(g - d) * group_rows + p * pair_rows for d in range(req_count) for p in pairs]
            table[g, m] = [m % 2, m] + pairs + [pairs.index(p) for p in range(SLOTS)] + firsts
    info = lax.dynamic_slice(jnp.asarray(table), (group, me, 0), (1, 1, table.shape[2])).reshape(-1)

    norm_args = [tokens, layer_norm_gain.reshape(1, -1), layer_norm_bias.reshape(1, -1)]
    norm_args = [pltpu.with_memory_space_constraint(x, pltpu.HBM) for x in norm_args]
    own = call(
        norm_kernel,
        norm_args,
        [shape(block, model_width)],
        scratch=[pltpu.VMEM(x.shape, x.dtype) for x in norm_args] + [pltpu.SemaphoreType.DMA((3,))],
        space=pltpu.HBM,
    )[0]
    other = to_partner(own)
    ring_a, ring_b = along_ring(own), along_ring(other)
    pair_left = jnp.concatenate([input_adapter_left, to_partner(input_adapter_left)], axis=1)

    float_lengths = wide(lengths)
    lane = np.arange(128)
    turn_rows = np.zeros((8, 128), np.float32)
    turn_rows[0] = np.exp(lane % ROT // 2 * (-2.0 * math.log(10000.0) / ROT))
    turn_rows[1] = np.where(lane < ROT, 0.0, math.pi / 2)
    turn_rows[2] = np.where(lane < ROT, 1.0, np.where(lane % 2 == 0, -1.0, 1.0))
    token_rows = req_count * group_rows
    token_args = [
        float_lengths[:, None],
        float_lengths[None, :],
        wide(request_adapter)[None, :],
        jnp.asarray(turn_rows),
    ]
    weights = [query_key_weight.reshape(model_width, 3 * HEAD_SIZE), up_weight]
    weights = [pltpu.with_memory_space_constraint(x, pltpu.HBM) for x in weights]
    meta, turns, qkv_rows, up_rows = call(
        token_kernel,
        token_args + weights,
        [shape(token_rows, 128, jnp.float32)] * 2 + [shape(*x.shape) for x in weights],
        info,
        [pltpu.SemaphoreType.DMA((2,))],
        in_hbm=2,
    )

    adapter_columns = query_key_value_right.shape[0]
    qkv_right = query_key_value_right.reshape(adapter_columns, 3 * HEAD_SIZE)
    spread_first = spread_table(ADAPTER_RANK, 0, 128)
    spread_last = spread_table(ADAPTER_RANK, ADAPTER_RANK, 128)
    near_right = output_adapter_right
    slot_columns = wide(jnp.repeat(slot_adapter, 2 * ADAPTER_RANK))[None, :]
    slot_columns = jnp.concatenate([slot_columns, to_partner(slot_columns)], axis=1)
    own_columns = near_right.shape[0]
    spread_own = spread_table(2 * ADAPTER_RANK, 0, 2 * own_columns)
    hidden_width = up_weight.shape[1]

    def to_group(value, d):
        return lax.ppermute(value, "req", [(g, g + d) for g in range(req_count - d)])

    held = functools.partial(pltpu.VMEM, dtype=jnp.float32)

    def add_ranks(part, slots, so_far):
        return call(
            functools.partial(rank_kernel, len(part), slots),
            list(part) + [pair_left, meta, slot_columns, spread_own, so_far],
            [shape(32, group_rows)],
            info,
        )[0]

    def products_of(part, flops=1000):
        rows = len(part) * block
        return call(
            functools.partial(base_kernel, len(part)),
            list(part) + [qkv_rows, up_rows],
            [
                shape(rows, 3 * HEAD_SIZE, jnp.float32),
                shape(rows, hidden_width, jnp.float32),
                shape(rows, 2 * HEAD_SIZE),
            ],
            flops=flops,
        )

    def to_groups(value):
        return [to_group(value, d) for d in range(1, req_count)]

    def arrivals(a, b):
        return a, b, to_partner(b), to_partner(a)

    tie = lax.optimization_barrier
    own_part = (own, other)
    ring_a, meta, turns, pair_left = tie((ring_a, meta, turns, pair_left))
    ranks = add_ranks(own_part, (0,), jnp.zeros((32, group_rows), jnp.bfloat16))
    ring_b, ranks = tie((ring_b, ranks))
    part = arrivals(ring_a, ring_b)
    ring_a, ring_b = along_ring(ring_a), along_ring(ring_b)
    ranks = add_ranks(part, (2, 3), ranks)
    first = products_of(own_part + part)
    ring_b, ranks, first = tie((ring_b, ranks, first))
    part = arrivals(ring_a, ring_b)
    ring_a, ring_b = along_ring(ring_a), along_ring(ring_b)
    far_right = to_partner(near_right)
    far_early = to_groups(first[2])
    ranks = add_ranks(part, (4, 5), ranks)
    second = products_of(part)
    ring_b, ranks, second, far_right = tie((ring_b, ranks, second, far_right))
    part = arrivals(ring_a, ring_b)
    ring_a = along_ring(ring_a)
    held_rows = part[:2]
    third = products_of(held_rows, 2000000000)
    ranks = add_ranks(held_rows, (6,), ranks)
    ring_a, ranks, third, far_early = tie((ring_a, ranks, third, far_early))
    part = part[2:] + (ring_a, to_partner(ring_a))
    ranks = add_ranks(part, (7, 1), ranks)
    moved = lax.ppermute(ranks, "mlp", [(i, i ^ 2) for i in range(16)])
    fourth = products_of(part)
    ranks, fourth = tie((ranks + moved, fourth))
    far_late = to_groups(jnp.concatenate([second[2], third[2], fourth[2]], axis=0))
    rank_in = sum_over_mlp(ranks, (4, 8))
    products = (first, second, third, fourth)

    bias_row = input_bias.reshape(1, -1)
    far_rank = to_groups(rank_in)
    queries, own_keys, own_values, hidden, hidden_rank = call(
        inner_kernel,
        [part[0] for part in products]
        + [part[1] for part in products]
        + [rank_in, meta, turns, spread_first, spread_last]
        + [qkv_right, up_adapter_right, bias_row, down_adapter_left],
        [shape(group_rows, HEAD_SIZE)] * 3 + [shape(group_rows, hidden_width), shape(32, group_rows)],
        info,
    )
    keys, values = [own_keys], [own_values]
    for d in range(1, req_count):
        early, late = far_early[d - 1], far_late[d - 1]
        ends = (0, block_rows, block_rows + pair_rows, 2 * block_rows + pair_rows)
        shared = [early] + [late[ends[k] : ends[k + 1]] for k in range(3)]
        far_keys, far_values = call(
            functools.partial(far_kernel, d * group_rows),
            shared + [far_rank[d - 1], meta, turns, spread_first, qkv_right],
            [shape(group_rows, HEAD_SIZE)] * 2,
            info,
        )
        keys.append(far_keys)
        values.append(far_values)

    output_left = output_adapter_left.reshape(HEAD_SIZE, adapter_columns)
    attended, rank_out = call(
        functools.partial(attention_kernel, req_count),
        [queries] + keys + values + [meta, spread_first, output_left, hidden_rank],
        [shape(group_rows, HEAD_SIZE), shape(32, group_rows)],
        info,
        [
            pltpu.VMEM((req_count * group_rows, HEAD_SIZE), jnp.bfloat16),
            pltpu.VMEM((req_count * group_rows, HEAD_SIZE), jnp.bfloat16),
            held((2 * block_rows, req_count * group_rows)),
            held((2 * block_rows, 128)),
            held((2 * block_rows, 128)),
            held((2 * block_rows, HEAD_SIZE)),
            held((32, group_rows)),
        ],
        mib=24 + 3 * req_count,
    )
    output_rows = output_weight.reshape(HEAD_SIZE, model_width)

    def main(k, attended, hidden):
        sent = block if k == 0 else pair_rows
        return call(
            functools.partial(main_kernel, k),
            [attended, hidden, output_rows, down_weight],
            [shape(block_rows - sent, model_width, jnp.float32), shape(sent, model_width)],
        )

    kept, arrived, sent = {}, {}, {}
    for bit, k in zip((1, 2, 4, 8), (0, 3, 2, 1)):
        moved = lax.ppermute(rank_out, "mlp", [(i, i ^ bit) for i in range(16)])
        kept[k], sent[k] = main(k, attended, hidden)
        rank_out, attended, kept[k], sent[k] = tie((rank_out + moved, attended, kept[k], sent[k]))
        if k == 0:
            arrived[k] = to_partner(sent[k])
        if bit == 4:
            arrived[3] = to_partner(sent[3])
            rank_out, arrived[0] = tie((rank_out, arrived[0]))
    rank_out, arrived[3] = tie((rank_out, arrived[3]))
    pair_right = jnp.concatenate([near_right, far_right], axis=0)

    def adapt(slot, half, kept, first, arrived):
        if half:
            outs = [shape(block, model_width, jnp.bfloat16 if slot else jnp.float32)]
        else:
            outs = [shape(block, model_width, jnp.float32)] * 2
        return call(
            functools.partial(adapt_kernel, slot, first),
            [rank_out, meta, spread_own, pair_right, kept, arrived],
            outs,
            info,
        )

    chain_a = along_ring(adapt(1, True, kept[0], 2 * block, arrived[0])[0])
    chain_b = None
    for s in (3, 2, 1):
        add_a, add_b = adapt(2 * s + 1, False, kept[s], 0, arrived[s])
        if s > 1:
            arrived[s - 1] = to_partner(sent[s - 1])
        if chain_b is None:
            chain_b = along_ring(narrow(add_b))
            chain_a = along_ring(narrow(wide(chain_a) + add_a))
        else:
            chain_a = along_ring(narrow(wide(chain_a) + add_a))
            chain_b = along_ring(narrow(wide(chain_b) + add_b))
    own_sum = adapt(0, True, kept[0], 0, tokens)[0]
    chain_a, own_sum = tie((chain_a, own_sum))
    arrived_last = to_partner(narrow(wide(chain_b) + kept[0][block : 2 * block]))
    return narrow(wide(chain_a) + wide(arrived_last) + own_sum + output_bias)


def solution(mesh):
    in_specs = (
        P(("req", "mlp"), None),
        P(),
        P(),
        P(None, "mlp", None),
        P("mlp", None, None),
        P(None, "mlp"),
        P("mlp"),
        P("mlp", None),
        P(),
        P(None, "mlp"),
        P(None, "mlp", None),
        P(None, "mlp"),
        P("mlp", None, None),
        P("mlp", None),
        P("mlp", None),
        P(),
        P(),
        P("mlp"),
    )
    out_specs = P(("req", "mlp"), None)
    return jax.shard_map(
        per_device, mesh=mesh, in_specs=in_specs, out_specs=out_specs, check_vma=False
    )
```

```python
import functools
import math

import jax
import jax.numpy as jnp
import numpy as np
from jax import lax
from jax.experimental import pallas as pl
from jax.experimental.pallas import tpu as pltpu
from jax.sharding import PartitionSpec as P

HEAD_SIZE = 256
ROT = 64
ADAPTER_RANK = 16
EPSILON = 1e-05
NEGATIVE_FILL = -1e30
RING = (0, 2, 4, 6, 7, 5, 3, 1)
PLACE = tuple(RING.index(pair) for pair in range(8))
CORE_PERM = [(i, i ^ 1) for i in range(16)]
RING_PERM = [(RING[i] * 2, RING[(i + 1) % 8] * 2) for i in range(8)] + [
    (RING[i] * 2 + 1, RING[(i - 1) % 8] * 2 + 1) for i in range(8)
]
SLOTS = 8
BLOCKS = 4
CORE, MLP, PAIRS, PLACES, BASES = 0, 1, 2, 2 + SLOTS, 2 + 2 * SLOTS


def to_partner(value):
    return lax.ppermute(value, "mlp", CORE_PERM)


def along_ring(value):
    return lax.ppermute(value, "mlp", RING_PERM)


def rank_product(left_side, right_side):
    return jnp.dot(left_side, right_side, preferred_element_type=jnp.float32)


def across(left_side, right_side):
    return lax.dot_general(
        left_side, right_side, (((1,), (1,)), ((), ())), preferred_element_type=jnp.float32
    )


def spread_table(period, first, width):
    row = np.arange(32)[:, None]
    column = np.arange(width)[None, :]
    return jnp.asarray((row - first == column % period).astype(np.float32), jnp.bfloat16)


def swap_halves(info, lanes):
    half = lanes.shape[1] // 2
    return jnp.where(info[CORE] == 1, pltpu.roll(lanes, half, 1), lanes)


def lane_ids(shape, period):
    return (lax.broadcasted_iota(jnp.int32, shape, 1) // period).astype(jnp.float32)


def pair_at(info, slot, rows):
    return pl.ds(pl.multiple_of(info[PAIRS + slot] * rows, rows), rows)


def store_lanes(info, out_ref, lanes, slots):
    width = out_ref.shape[1] // SLOTS
    for k, slot in enumerate(slots):
        part = lanes[:, k * width : (k + 1) * width]
        out_ref[:, pair_at(info, slot, width)] = swap_halves(info, part).astype(out_ref.dtype)


def rank_rows(info, rank_ref, slot, count):
    width = rank_ref.shape[1] // SLOTS
    lanes = [
        swap_halves(info, rank_ref[:, pair_at(info, slot + k, width)].astype(jnp.float32))
        for k in range(count)
    ]
    lanes = lanes[0] if count == 1 else jnp.concatenate(lanes, axis=1)
    return jnp.transpose(lanes).astype(jnp.bfloat16)


def widened(rows, spread_ref, adapter, columns):
    tile = rank_product(rows, spread_ref[...]).astype(jnp.bfloat16)
    group = lax.broadcasted_iota(jnp.int32, tile.shape, 1) // ADAPTER_RANK
    apart = (adapter - group.astype(jnp.float32)).astype(jnp.bfloat16)
    step = tile.shape[1] // ADAPTER_RANK
    zero = jnp.zeros_like(tile)
    return jnp.concatenate(
        [jnp.where(apart == first, tile, zero) for first in range(0, columns // ADAPTER_RANK, step)], axis=1
    )


def folded(products, adapter, spread_ref):
    width = spread_ref.shape[1]
    group = lax.broadcasted_iota(jnp.int32, (products.shape[0], width), 1) // ADAPTER_RANK
    apart = adapter - group.astype(jnp.float32)
    total = None
    for first in range(0, products.shape[1], width):
        part = products[:, first : first + width]
        part = jnp.where(apart == float(first // ADAPTER_RANK), part, 0.0)
        total = part if total is None else total + part
    return across(spread_ref[...], total.astype(jnp.bfloat16))


def cosine(angle):
    turns = jnp.floor(angle * (1.0 / math.pi) + 0.5)
    rest = ((angle - turns * 3.140625) - turns * 9.67502593994140625e-4) - turns * 1.509957990978376e-7
    square = rest * rest
    value = jnp.full_like(square, 1.0 / 479001600.0)
    for factor in (-1.0 / 3628800.0, 1.0 / 40320.0, -1.0 / 720.0, 1.0 / 24.0, -0.5, 1.0):
        value = value * square + factor
    odd = turns - 2.0 * jnp.floor(turns * 0.5)
    return value * (1.0 - 2.0 * odd)


def norm_kernel(x_hbm, gain_hbm, bias_hbm, out_ref, x_ref, gain_ref, bias_ref, sems):
    pairs = ((x_hbm, x_ref), (gain_hbm, gain_ref), (bias_hbm, bias_ref))
    copies = [pltpu.make_async_copy(a, b, sems.at[k]) for k, (a, b) in enumerate(pairs)]
    for copy in copies:
        copy.start()
    copies[0].wait()
    values = x_ref[...].astype(jnp.float32)
    center = values - jnp.mean(values, axis=1, keepdims=True)
    spread = jnp.mean(center * center, axis=1, keepdims=True)
    scaled = center * lax.rsqrt(spread + EPSILON)
    copies[1].wait()
    copies[2].wait()
    out_ref[...] = (scaled * gain_ref[...] + bias_ref[...]).astype(out_ref.dtype)


def local_tokens(info, slot, shape, dim):
    rows = shape[dim] // 2
    at = lax.broadcasted_iota(jnp.int32, shape, dim)
    second = at >= rows
    at = jnp.where(second, at - rows, at) + info[CORE] * (rows // 2)
    at = jnp.where(at >= rows, at - rows, at)
    return (at + jnp.where(second, info[BASES + slot + 1], info[BASES + slot])).astype(jnp.float32)


def token_kernel(info, column_ref, row_ref, ids_ref, table_ref, *refs):
    count = (len(refs) - 3) // 2
    meta_ref, turn_ref = refs[count : count + 2]
    pairs = zip(refs[:count], refs[count + 2 : -1])
    copies = [pltpu.make_async_copy(a, b, refs[-1].at[k]) for k, (a, b) in enumerate(pairs)]
    for copy in copies:
        copy.start()
    rows = 2 * 128
    count = row_ref.shape[1]
    earlier = lax.broadcasted_iota(jnp.int32, (count, count), 0) < lax.broadcasted_iota(
        jnp.int32, (count, count), 1
    )
    anchors = jnp.sum(jnp.where(earlier, column_ref[...], 0.0), axis=0, keepdims=True)
    endings = anchors + row_ref[...]
    ids = ids_ref[...]
    lane = lax.broadcasted_iota(jnp.int32, (rows, 128), 1)

    def one(block, _):
        token = local_tokens(info, 2 * block, (rows, 1), 0)
        inside = jnp.logical_and(anchors <= token, token < endings)
        start = jnp.sum(jnp.where(inside, anchors, 0.0), axis=1, keepdims=True)
        adapter = jnp.sum(jnp.where(inside, ids, 0.0), axis=1, keepdims=True)
        at = pl.ds(pl.multiple_of(block * rows, rows), rows)
        meta_ref[at, :] = jnp.where(lane < 64, start, adapter)
        angle = (token - start) * table_ref[0:1, :] - table_ref[1:2, :]
        turn_ref[at, :] = cosine(angle) * table_ref[2:3, :]
        return 0

    lax.fori_loop(0, meta_ref.shape[0] // rows, one, 0)
    for copy in copies:
        copy.wait()


def rank_kernel(count, slots, info, *refs):
    x = jnp.concatenate([ref[...] for ref in refs[:count]], axis=0)
    left_ref, meta_ref, slot_ref, fold_ref, held_ref = refs[count : count + 5]
    out_ref = refs[-1]
    products = rank_product(x, left_ref[...])
    adapter = jnp.concatenate([meta_ref[k * 128 : (k + 1) * 128, 64:65] for k in slots], axis=0)
    chosen = jnp.where(slot_ref[...] == adapter, products, 0.0).astype(jnp.bfloat16)
    out_ref[...] = held_ref[...]
    store_lanes(info, out_ref, across(fold_ref[...], chosen), slots)


def base_kernel(count, *refs):
    x = jnp.concatenate([ref[...] for ref in refs[:count]], axis=0)
    qkv_ref, up_ref, base_ref, up_base_ref, shared_ref = refs[count:]
    first = rank_product(x, qkv_ref[...])
    base_ref[...] = first
    shared_ref[...] = first[:, HEAD_SIZE:].astype(shared_ref.dtype)
    up_base_ref[...] = rank_product(x, up_ref[...])


def turn(part, table):
    width = table.shape[1]
    lane = lax.broadcasted_iota(jnp.int32, table.shape, 1)
    cos = jnp.where(lane < ROT, table, 1.0)
    sin = jnp.where(lane < ROT, pltpu.roll(table, width - ROT, 1), 0.0)
    head = part[:, :width]
    swapped = jnp.where(
        lane % 2 == 0, pltpu.roll(head, width - 1, 1), pltpu.roll(head, 1, 1)
    )
    return jnp.concatenate([head * cos + swapped * sin, part[:, width:]], axis=1)


def block_rows_of(refs, block):
    if block == 0:
        return jnp.concatenate([refs[0][:128], refs[3][128:]], axis=0)
    if block == 3:
        return jnp.concatenate([refs[2][...], refs[3][:128]], axis=0)
    return refs[0][128:] if block == 1 else refs[1][...]


def two_blocks(refs, index):
    return jnp.concatenate([block_rows_of(refs, 2 * index + k) for k in (0, 1)], axis=0)


def inner_kernel(info, *refs):
    base_refs, up_refs, (rank_ref, meta_ref, turn_ref, first_ref, last_ref) = refs[:4], refs[4:8], refs[8:13]
    qkv_right_ref, up_right_ref, bias_ref, left_ref = refs[13:17]
    q_ref, k_ref, v_ref, hidden_ref, out_ref = refs[17:]
    rows = 512
    columns = qkv_right_ref.shape[0]
    for block in range(BLOCKS // 2):
        at = slice(block * rows, (block + 1) * rows)
        adapter = meta_ref[at, 64:65]
        ranks = rank_rows(info, rank_ref, 4 * block, 4)
        total = two_blocks(base_refs, block) + rank_product(
            widened(ranks, first_ref, adapter, columns), qkv_right_ref[...]
        )
        table = turn_ref[at, :]
        q_ref[at, :] = (turn(total[:, :HEAD_SIZE], table) * HEAD_SIZE ** (-0.5)).astype(jnp.bfloat16)
        k_ref[at, :] = turn(total[:, HEAD_SIZE : 2 * HEAD_SIZE], table).astype(jnp.bfloat16)
        v_ref[at, :] = total[:, 2 * HEAD_SIZE :].astype(jnp.bfloat16)
        wide = widened(ranks, last_ref, adapter, columns)
        x = two_blocks(up_refs, block) + rank_product(wide, up_right_ref[...]) + bias_ref[...]
        inner = math.sqrt(2.0 / math.pi) * (x + 0.044715 * (x * x * x))
        hidden = (0.5 * x * (1.0 + jnp.tanh(inner))).astype(jnp.bfloat16)
        hidden_ref[at, :] = hidden
        lanes = folded(rank_product(hidden, left_ref[...]), adapter, last_ref)
        store_lanes(info, out_ref, lanes, range(4 * block, 4 * block + 4))


def far_kernel(first_row, info, *refs):
    shared_refs, (rank_ref, meta_ref, turn_ref, spread_ref, right_ref, k_ref, v_ref) = refs[:4], refs[4:]
    rows = 512
    for block in range(BLOCKS // 2):
        at = slice(block * rows, (block + 1) * rows)
        far_at = slice(first_row + block * rows, first_row + (block + 1) * rows)
        ranks = rank_rows(info, rank_ref, 4 * block, 4)
        wide = widened(ranks, spread_ref, meta_ref[far_at, 64:65], right_ref.shape[0])
        total = two_blocks(shared_refs, block).astype(jnp.float32)
        total = total + rank_product(wide, right_ref[:, HEAD_SIZE:])
        k_ref[at, :] = turn(total[:, :HEAD_SIZE], turn_ref[far_at, :]).astype(jnp.bfloat16)
        v_ref[at, :] = total[:, HEAD_SIZE:].astype(jnp.bfloat16)


def attention_kernel(req_count, info, *refs):
    q_ref, refs = refs[0], refs[1:]
    key_refs, value_refs, refs = refs[:req_count], refs[req_count : 2 * req_count], refs[2 * req_count :]
    meta_ref, spread_ref, left_ref, hidden_rank_ref, attended_ref, out_ref = refs[:6]
    keys_ref, values_ref, scores_ref, top_ref, sum_ref, acc_ref, fold_ref = refs[6:]
    span = 256
    rows = 2 * span
    pair = span // 2
    group_rows = q_ref.shape[0]

    def slot_rows(slot):
        return pl.ds(pl.multiple_of(slot * pair, pair), pair)

    for d in range(req_count):
        for k in range(SLOTS):
            at = slice((req_count - 1 - d) * group_rows + k * pair, (req_count - 1 - d) * group_rows + (k + 1) * pair)
            slot = slot_rows(info[PLACES + k])
            keys_ref[at, :] = key_refs[d][slot, :]
            values_ref[at, :] = value_refs[d][slot, :]
    first_token = info[BASES + info[PLACES]] - (req_count - 1) * group_rows

    def places(shape, dim):
        at = lax.broadcasted_iota(jnp.int32, shape, dim)
        before = at // pair * pair
        at = at - before + info[CORE] * (pair // 2)
        return (before + jnp.where(at >= pair, at - pair, at)).astype(jnp.float32)

    key_place = places((1, span), 1)
    query_place = places((rows, 1), 0)

    def one(block, _):
        slots = [slot_rows(info[PLACES + 4 * block + k]) for k in range(4)]

        def both(ref):
            return jnp.concatenate([ref[at, :] for at in slots], axis=0)

        meta = both(meta_ref)
        start = meta[:, 0:1]
        number = (req_count - 1) * BLOCKS + 2 * block
        query = query_place + (first_token + number * span).astype(jnp.float32)
        q = both(q_ref)
        lowest = jnp.min(start).astype(jnp.int32) - first_token
        top_ref[...] = jnp.full_like(top_ref, NEGATIVE_FILL)
        sum_ref[...] = jnp.zeros_like(sum_ref)
        acc_ref[...] = jnp.zeros_like(acc_ref)

        def score(j, _):
            at = pl.ds(pl.multiple_of(j * span, span), span)
            scores = across(q, keys_ref[at, :])
            key = key_place + (first_token + j * span).astype(jnp.float32)
            allowed = jnp.logical_and(key <= query, key >= start)
            scores = jnp.where(allowed, scores, NEGATIVE_FILL)
            scores_ref[:, at] = scores
            top_ref[...] = jnp.maximum(top_ref[...], jnp.maximum(scores[:, :pair], scores[:, pair:]))
            return 0

        lax.fori_loop(lowest // span, number + 2, score, 0)
        top = jnp.max(top_ref[...], axis=1, keepdims=True)

        def weigh(j, _):
            at = pl.ds(pl.multiple_of(j * span, span), span)
            weights = jnp.exp(scores_ref[:, at] - top)
            sum_ref[...] = sum_ref[...] + (weights[:, :pair] + weights[:, pair:])
            acc_ref[...] = acc_ref[...] + rank_product(weights.astype(jnp.bfloat16), values_ref[at, :])
            return 0

        lax.fori_loop(lowest // span, number + 2, weigh, 0)
        total = jnp.sum(sum_ref[...], axis=1, keepdims=True)
        attended = (acc_ref[...] / total).astype(jnp.bfloat16)
        lanes = folded(rank_product(attended, left_ref[...]), meta[:, 64:65], spread_ref)
        for k in range(4):
            attended_ref[slots[k], :] = attended[k * pair : (k + 1) * pair]
            at = pl.ds(pl.multiple_of((4 * block + k) * pair, pair), pair)
            fold_ref[:, at] = swap_halves(info, lanes[:, k * pair : (k + 1) * pair])
        return 0

    lax.fori_loop(0, BLOCKS // 2, one, 0)
    out_ref[...] = (fold_ref[...] + hidden_rank_ref[...].astype(jnp.float32)).astype(out_ref.dtype)


def main_kernel(block, attended_ref, hidden_ref, output_ref, down_ref, kept_ref, sent_ref):
    rows = 256
    sent = sent_ref.shape[0]
    width = 512
    attended = attended_ref[block * rows : (block + 1) * rows, :]
    hidden = hidden_ref[block * rows : (block + 1) * rows, :]

    for step in range(output_ref.shape[1] // width):
        at = slice(step * width, (step + 1) * width)
        total = rank_product(attended, output_ref[:, at]) + rank_product(hidden, down_ref[:, at])
        if block:
            sent_ref[:, at] = total[:sent].astype(sent_ref.dtype)
            kept_ref[:, at] = total[sent:]
        else:
            kept_ref[:, at] = total[: rows - sent]
            sent_ref[:, at] = total[rows - sent :].astype(sent_ref.dtype)


def adapt_kernel(slot, first, info, rank_ref, meta_ref, spread_ref, right_ref, kept_ref, arrived_ref, *out_refs):
    pair = 128
    half = pair // 2
    columns = spread_ref.shape[1]
    count = columns // (4 * ADAPTER_RANK)
    column_id = lax.broadcasted_iota(jnp.int32, (pair, columns), 1) // (2 * ADAPTER_RANK)
    partner = info[MLP] + 1 - 2 * info[CORE]
    column_id = column_id + jnp.where(column_id < count, info[MLP] * count, (partner - 1) * count)
    own = column_id.astype(jnp.float32) == meta_ref[slot * pair : (slot + 1) * pair, 64:65]
    spread = rank_product(rank_rows(info, rank_ref, slot, 1), spread_ref[...])
    wide = jnp.where(own, spread, 0.0).astype(jnp.bfloat16)
    width = 512

    for step in range(right_ref.shape[1] // width):
        at = slice(step * width, (step + 1) * width)
        if len(out_refs) == 1:
            total = rank_product(wide[:half], right_ref[:, at]) + kept_ref[first : first + half, at]
            total = total + arrived_ref[:, at].astype(jnp.float32)
            out_refs[0][:, at] = total.astype(out_refs[0].dtype)
        else:
            total = rank_product(wide, right_ref[:, at]) + kept_ref[:, at]
            out_refs[0][:, at] = total[:half] + arrived_ref[half:, at].astype(jnp.float32)
            out_refs[1][:, at] = total[half:] + arrived_ref[:half, at].astype(jnp.float32)


def call(kernel, operands, outs, info=None, scratch=(), mib=24, flops=1000, space=pltpu.VMEM, in_hbm=0):
    vmem = pl.BlockSpec(memory_space=pltpu.VMEM)
    specs = [pl.BlockSpec(memory_space=space)] * (len(operands) - in_hbm)
    specs += [pl.BlockSpec(memory_space=pltpu.HBM)] * in_hbm
    if info is not None:
        operands, specs = [info] + operands, [pl.BlockSpec(memory_space=pltpu.SMEM)] + specs
    return pl.pallas_call(
        kernel,
        in_specs=specs,
        out_specs=[vmem] * len(outs),
        out_shape=outs,
        scratch_shapes=scratch,
        compiler_params=pltpu.CompilerParams(vmem_limit_bytes=mib * 1024 * 1024),
        cost_estimate=pl.CostEstimate(flops=flops, bytes_accessed=1000, transcendentals=0),
    )(*operands)


def shape(rows, width, dtype=jnp.bfloat16):
    return jax.ShapeDtypeStruct((rows, width), dtype)


def sum_over_mlp(value, bits):
    for bit in bits:
        value = value + lax.ppermute(value, "mlp", [(i, i ^ bit) for i in range(16)])
    return value


def narrow(value):
    return value.astype(jnp.bfloat16)


def wide(value):
    return value.astype(jnp.float32)


def per_device(
    tokens,
    layer_norm_gain,
    layer_norm_bias,
    query_key_weight,
    output_weight,
    up_weight,
    input_bias,
    down_weight,
    output_bias,
    input_adapter_left,
    query_key_value_right,
    up_adapter_right,
    output_adapter_left,
    down_adapter_left,
    output_adapter_right,
    lengths,
    request_adapter,
    slot_adapter,
):
    block = tokens.shape[0]
    model_width = tokens.shape[1]
    pair_rows = 2 * block
    group_rows = SLOTS * pair_rows
    req_count = lax.axis_size("req")
    group = lax.axis_index("req")
    me = lax.axis_index("mlp")
    block_rows = 2 * pair_rows
    table = np.zeros((req_count, 16, 2 + SLOTS * (2 + req_count)), np.int32)
    for g in range(req_count):
        for m in range(16):
            side = 2 * (m % 2) - 1
            steps = [0, 4] + [t for s in (1, 2, 3) for t in (side * s, -side * s)]
            pairs = [RING[(PLACE[m // 2] + t) % 8] for t in steps]
            firsts = [(g - d) * group_rows + p * pair_rows for d in range(req_count) for p in pairs]
            table[g, m] = [m % 2, m] + pairs + [pairs.index(p) for p in range(SLOTS)] + firsts
    info = lax.dynamic_slice(jnp.asarray(table), (group, me, 0), (1, 1, table.shape[2])).reshape(-1)

    norm_args = [tokens, layer_norm_gain.reshape(1, -1), layer_norm_bias.reshape(1, -1)]
    norm_args = [pltpu.with_memory_space_constraint(x, pltpu.HBM) for x in norm_args]
    own = call(
        norm_kernel,
        norm_args,
        [shape(block, model_width)],
        scratch=[pltpu.VMEM(x.shape, x.dtype) for x in norm_args] + [pltpu.SemaphoreType.DMA((3,))],
        space=pltpu.HBM,
    )[0]
    other = to_partner(own)
    ring_a, ring_b = along_ring(own), along_ring(other)
    near_left, far_left = input_adapter_left, to_partner(input_adapter_left)

    float_lengths = wide(lengths)
    lane = np.arange(128)
    turn_rows = np.zeros((8, 128), np.float32)
    turn_rows[0] = np.exp(lane % ROT // 2 * (-2.0 * math.log(10000.0) / ROT))
    turn_rows[1] = np.where(lane < ROT, 0.0, math.pi / 2)
    turn_rows[2] = np.where(lane < ROT, 1.0, np.where(lane % 2 == 0, -1.0, 1.0))
    token_rows = req_count * group_rows
    token_args = [
        float_lengths[:, None],
        float_lengths[None, :],
        wide(request_adapter)[None, :],
        jnp.asarray(turn_rows),
    ]
    weights = [query_key_weight.reshape(model_width, 3 * HEAD_SIZE), up_weight]
    weights = [pltpu.with_memory_space_constraint(x, pltpu.HBM) for x in weights]
    meta, turns, qkv_rows, up_rows = call(
        token_kernel,
        token_args + weights,
        [shape(token_rows, 128, jnp.float32)] * 2 + [shape(*x.shape) for x in weights],
        info,
        [pltpu.SemaphoreType.DMA((2,))],
        in_hbm=2,
    )

    adapter_columns = query_key_value_right.shape[0]
    qkv_right = query_key_value_right.reshape(adapter_columns, 3 * HEAD_SIZE)
    spread_first = spread_table(ADAPTER_RANK, 0, 128)
    spread_last = spread_table(ADAPTER_RANK, ADAPTER_RANK, 128)
    near_right = output_adapter_right
    slot_columns = wide(jnp.repeat(slot_adapter, 2 * ADAPTER_RANK))[None, :]
    slot_columns = jnp.concatenate([slot_columns, to_partner(slot_columns)], axis=1)
    own_columns = near_right.shape[0]
    spread_own = spread_table(2 * ADAPTER_RANK, 0, 2 * own_columns)
    hidden_width = up_weight.shape[1]

    def to_group(value, d):
        return lax.ppermute(value, "req", [(g, g + d) for g in range(req_count - d)])

    held = functools.partial(pltpu.VMEM, dtype=jnp.float32)

    def add_ranks(part, slots, so_far):
        return call(
            functools.partial(rank_kernel, len(part), slots),
            list(part) + [pair_left, meta, slot_columns, spread_own, so_far],
            [shape(32, group_rows)],
            info,
        )[0]

    def products_of(part, flops=1000):
        rows = len(part) * block
        return call(
            functools.partial(base_kernel, len(part)),
            list(part) + [qkv_rows, up_rows],
            [
                shape(rows, 3 * HEAD_SIZE, jnp.float32),
                shape(rows, hidden_width, jnp.float32),
                shape(rows, 2 * HEAD_SIZE),
            ],
            flops=flops,
        )

    def to_groups(value):
        return [to_group(value, d) for d in range(1, req_count)]

    def arrivals(a, b):
        return a, b, to_partner(b), to_partner(a)

    tie = lax.optimization_barrier
    own_part = (own, other)
    ring_a, meta, turns, qkv_rows, up_rows = tie((ring_a, meta, turns, qkv_rows, up_rows))
    ring_b, near_left, far_left = tie((ring_b, near_left, far_left))
    pair_left = jnp.concatenate([near_left, far_left], axis=1)
    part = arrivals(ring_a, ring_b)
    ring_a, ring_b = along_ring(ring_a), along_ring(ring_b)
    ranks = add_ranks(own_part + part, (0, 2, 3), jnp.zeros((32, group_rows), jnp.bfloat16))
    first = products_of(own_part + part)
    ring_b, ranks, first = tie((ring_b, ranks, first))
    part = arrivals(ring_a, ring_b)
    ring_a, ring_b = along_ring(ring_a), along_ring(ring_b)
    far_right = to_partner(near_right)
    far_early = to_groups(first[2])
    ranks = add_ranks(part, (4, 5), ranks)
    second = products_of(part)
    ring_b, ranks, second, far_right = tie((ring_b, ranks, second, far_right))
    part = arrivals(ring_a, ring_b)
    ring_a = along_ring(ring_a)
    held_rows = part[:2]
    third = products_of(held_rows, 2000000000)
    ranks = add_ranks(held_rows, (6,), ranks)
    ring_a, ranks, third, far_early = tie((ring_a, ranks, third, far_early))
    part = part[2:] + (ring_a, to_partner(ring_a))
    ranks = add_ranks(part, (7, 1), ranks)
    moved = lax.ppermute(ranks, "mlp", [(i, i ^ 2) for i in range(16)])
    fourth = products_of(part)
    ranks, fourth = tie((ranks + moved, fourth))
    far_late = to_groups(jnp.concatenate([second[2], third[2], fourth[2]], axis=0))
    rank_in = sum_over_mlp(ranks, (4, 8))
    products = (first, second, third, fourth)

    bias_row = input_bias.reshape(1, -1)
    far_rank = to_groups(rank_in)
    queries, own_keys, own_values, hidden, hidden_rank = call(
        inner_kernel,
        [part[0] for part in products]
        + [part[1] for part in products]
        + [rank_in, meta, turns, spread_first, spread_last]
        + [qkv_right, up_adapter_right, bias_row, down_adapter_left],
        [shape(group_rows, HEAD_SIZE)] * 3 + [shape(group_rows, hidden_width), shape(32, group_rows)],
        info,
    )
    keys, values = [own_keys], [own_values]
    for d in range(1, req_count):
        early, late = far_early[d - 1], far_late[d - 1]
        ends = (0, block_rows, block_rows + pair_rows, 2 * block_rows + pair_rows)
        shared = [early] + [late[ends[k] : ends[k + 1]] for k in range(3)]
        far_keys, far_values = call(
            functools.partial(far_kernel, d * group_rows),
            shared + [far_rank[d - 1], meta, turns, spread_first, qkv_right],
            [shape(group_rows, HEAD_SIZE)] * 2,
            info,
        )
        keys.append(far_keys)
        values.append(far_values)

    output_left = output_adapter_left.reshape(HEAD_SIZE, adapter_columns)
    attended, rank_out = call(
        functools.partial(attention_kernel, req_count),
        [queries] + keys + values + [meta, spread_first, output_left, hidden_rank],
        [shape(group_rows, HEAD_SIZE), shape(32, group_rows)],
        info,
        [
            pltpu.VMEM((req_count * group_rows, HEAD_SIZE), jnp.bfloat16),
            pltpu.VMEM((req_count * group_rows, HEAD_SIZE), jnp.bfloat16),
            held((2 * block_rows, req_count * group_rows)),
            held((2 * block_rows, 128)),
            held((2 * block_rows, 128)),
            held((2 * block_rows, HEAD_SIZE)),
            held((32, group_rows)),
        ],
        mib=24 + 3 * req_count,
    )
    output_rows = output_weight.reshape(HEAD_SIZE, model_width)

    def main(k, attended, hidden):
        sent = block if k == 0 else pair_rows
        return call(
            functools.partial(main_kernel, k),
            [attended, hidden, output_rows, down_weight],
            [shape(block_rows - sent, model_width, jnp.float32), shape(sent, model_width)],
        )

    kept, arrived, sent = {}, {}, {}
    for bit, k in zip((1, 2, 4, 8), (0, 3, 2, 1)):
        moved = lax.ppermute(rank_out, "mlp", [(i, i ^ bit) for i in range(16)])
        kept[k], sent[k] = main(k, attended, hidden)
        rank_out, attended, kept[k], sent[k] = tie((rank_out + moved, attended, kept[k], sent[k]))
        if k == 0:
            arrived[k] = to_partner(sent[k])
        if bit == 4:
            arrived[3] = to_partner(sent[3])
            rank_out, arrived[0] = tie((rank_out, arrived[0]))
    rank_out, arrived[3] = tie((rank_out, arrived[3]))
    pair_right = jnp.concatenate([near_right, far_right], axis=0)

    def adapt(slot, half, kept, first, arrived):
        if half:
            outs = [shape(block, model_width, jnp.bfloat16 if slot else jnp.float32)]
        else:
            outs = [shape(block, model_width, jnp.float32)] * 2
        return call(
            functools.partial(adapt_kernel, slot, first),
            [rank_out, meta, spread_own, pair_right, kept, arrived],
            outs,
            info,
        )

    chain_a = along_ring(adapt(1, True, kept[0], 2 * block, arrived[0])[0])
    chain_b = None
    for s in (3, 2, 1):
        add_a, add_b = adapt(2 * s + 1, False, kept[s], 0, arrived[s])
        if s > 1:
            arrived[s - 1] = to_partner(sent[s - 1])
        if chain_b is None:
            chain_b = along_ring(narrow(add_b))
            chain_a = along_ring(narrow(wide(chain_a) + add_a))
        else:
            chain_a = along_ring(narrow(wide(chain_a) + add_a))
            chain_b = along_ring(narrow(wide(chain_b) + add_b))
    own_sum = adapt(0, True, kept[0], 0, tokens)[0]
    chain_a, own_sum = tie((chain_a, own_sum))
    arrived_last = to_partner(narrow(wide(chain_b) + kept[0][block : 2 * block]))
    return narrow(wide(chain_a) + wide(arrived_last) + own_sum + output_bias)


def solution(mesh):
    in_specs = (
        P(("req", "mlp"), None),
        P(),
        P(),
        P(None, "mlp", None),
        P("mlp", None, None),
        P(None, "mlp"),
        P("mlp"),
        P("mlp", None),
        P(),
        P(None, "mlp"),
        P(None, "mlp", None),
        P(None, "mlp"),
        P("mlp", None, None),
        P("mlp", None),
        P("mlp", None),
        P(),
        P(),
        P("mlp"),
    )
    out_specs = P(("req", "mlp"), None)
    return jax.shard_map(
        per_device, mesh=mesh, in_specs=in_specs, out_specs=out_specs, check_vma=False
    )
```

```python
import functools
import math

import jax
import jax.numpy as jnp
import numpy as np
from jax import lax
from jax.experimental import pallas as pl
from jax.experimental.pallas import tpu as pltpu
from jax.sharding import PartitionSpec as P

HEAD_SIZE = 256
ROT = 64
ADAPTER_RANK = 16
EPSILON = 1e-05
NEGATIVE_FILL = -1e30
RING = (0, 2, 4, 6, 7, 5, 3, 1)
PLACE = tuple(RING.index(pair) for pair in range(8))
CORE_PERM = [(i, i ^ 1) for i in range(16)]
RING_PERM = [(RING[i] * 2, RING[(i + 1) % 8] * 2) for i in range(8)] + [
    (RING[i] * 2 + 1, RING[(i - 1) % 8] * 2 + 1) for i in range(8)
]
SLOTS = 8
BLOCKS = 4
CORE, MLP, PAIRS, PLACES, BASES = 0, 1, 2, 2 + SLOTS, 2 + 2 * SLOTS


def to_partner(value):
    return lax.ppermute(value, "mlp", CORE_PERM)


def along_ring(value):
    return lax.ppermute(value, "mlp", RING_PERM)


def rank_product(left_side, right_side):
    return jnp.dot(left_side, right_side, preferred_element_type=jnp.float32)


def across(left_side, right_side):
    return lax.dot_general(
        left_side, right_side, (((1,), (1,)), ((), ())), preferred_element_type=jnp.float32
    )


def spread_table(period, first, width):
    row = np.arange(32)[:, None]
    column = np.arange(width)[None, :]
    return jnp.asarray((row - first == column % period).astype(np.float32), jnp.bfloat16)


def swap_halves(info, lanes):
    half = lanes.shape[1] // 2
    return jnp.where(info[CORE] == 1, pltpu.roll(lanes, half, 1), lanes)


def lane_ids(shape, period):
    return (lax.broadcasted_iota(jnp.int32, shape, 1) // period).astype(jnp.float32)


def pair_at(info, slot, rows):
    return pl.ds(pl.multiple_of(info[PAIRS + slot] * rows, rows), rows)


def store_lanes(info, out_ref, lanes, slots):
    width = out_ref.shape[1] // SLOTS
    for k, slot in enumerate(slots):
        part = lanes[:, k * width : (k + 1) * width]
        out_ref[:, pair_at(info, slot, width)] = swap_halves(info, part).astype(out_ref.dtype)


def rank_rows(info, rank_ref, slot, count):
    width = rank_ref.shape[1] // SLOTS
    lanes = [
        swap_halves(info, rank_ref[:, pair_at(info, slot + k, width)].astype(jnp.float32))
        for k in range(count)
    ]
    lanes = lanes[0] if count == 1 else jnp.concatenate(lanes, axis=1)
    return jnp.transpose(lanes).astype(jnp.bfloat16)


def widened(rows, spread_ref, adapter, columns):
    tile = rank_product(rows, spread_ref[...]).astype(jnp.bfloat16)
    group = lax.broadcasted_iota(jnp.int32, tile.shape, 1) // ADAPTER_RANK
    apart = (adapter - group.astype(jnp.float32)).astype(jnp.bfloat16)
    step = tile.shape[1] // ADAPTER_RANK
    zero = jnp.zeros_like(tile)
    return jnp.concatenate(
        [jnp.where(apart == first, tile, zero) for first in range(0, columns // ADAPTER_RANK, step)], axis=1
    )


def folded(products, adapter, spread_ref):
    width = spread_ref.shape[1]
    group = lax.broadcasted_iota(jnp.int32, (products.shape[0], width), 1) // ADAPTER_RANK
    apart = adapter - group.astype(jnp.float32)
    total = None
    for first in range(0, products.shape[1], width):
        part = products[:, first : first + width]
        part = jnp.where(apart == float(first // ADAPTER_RANK), part, 0.0)
        total = part if total is None else total + part
    return across(spread_ref[...], total.astype(jnp.bfloat16))


def cosine(angle):
    turns = jnp.floor(angle * (1.0 / math.pi) + 0.5)
    rest = ((angle - turns * 3.140625) - turns * 9.67502593994140625e-4) - turns * 1.509957990978376e-7
    square = rest * rest
    value = jnp.full_like(square, 1.0 / 479001600.0)
    for factor in (-1.0 / 3628800.0, 1.0 / 40320.0, -1.0 / 720.0, 1.0 / 24.0, -0.5, 1.0):
        value = value * square + factor
    odd = turns - 2.0 * jnp.floor(turns * 0.5)
    return value * (1.0 - 2.0 * odd)


def norm_kernel(x_hbm, gain_hbm, bias_hbm, out_ref, x_ref, gain_ref, bias_ref, sems):
    pairs = ((x_hbm, x_ref), (gain_hbm, gain_ref), (bias_hbm, bias_ref))
    copies = [pltpu.make_async_copy(a, b, sems.at[k]) for k, (a, b) in enumerate(pairs)]
    for copy in copies:
        copy.start()
    copies[0].wait()
    values = x_ref[...].astype(jnp.float32)
    center = values - jnp.mean(values, axis=1, keepdims=True)
    spread = jnp.mean(center * center, axis=1, keepdims=True)
    scaled = center * lax.rsqrt(spread + EPSILON)
    copies[1].wait()
    copies[2].wait()
    out_ref[...] = (scaled * gain_ref[...] + bias_ref[...]).astype(out_ref.dtype)


def local_tokens(info, slot, shape, dim):
    rows = shape[dim] // 2
    at = lax.broadcasted_iota(jnp.int32, shape, dim)
    second = at >= rows
    at = jnp.where(second, at - rows, at) + info[CORE] * (rows // 2)
    at = jnp.where(at >= rows, at - rows, at)
    return (at + jnp.where(second, info[BASES + slot + 1], info[BASES + slot])).astype(jnp.float32)


def token_kernel(info, column_ref, row_ref, ids_ref, table_ref, *refs):
    count = (len(refs) - 3) // 2
    meta_ref, turn_ref = refs[count : count + 2]
    pairs = zip(refs[:count], refs[count + 2 : -1])
    copies = [pltpu.make_async_copy(a, b, refs[-1].at[k]) for k, (a, b) in enumerate(pairs)]
    for copy in copies:
        copy.start()
    rows = 2 * 128
    count = row_ref.shape[1]
    earlier = lax.broadcasted_iota(jnp.int32, (count, count), 0) < lax.broadcasted_iota(
        jnp.int32, (count, count), 1
    )
    anchors = jnp.sum(jnp.where(earlier, column_ref[...], 0.0), axis=0, keepdims=True)
    endings = anchors + row_ref[...]
    ids = ids_ref[...]
    lane = lax.broadcasted_iota(jnp.int32, (rows, 128), 1)

    def one(block, _):
        token = local_tokens(info, 2 * block, (rows, 1), 0)
        inside = jnp.logical_and(anchors <= token, token < endings)
        start = jnp.sum(jnp.where(inside, anchors, 0.0), axis=1, keepdims=True)
        adapter = jnp.sum(jnp.where(inside, ids, 0.0), axis=1, keepdims=True)
        at = pl.ds(pl.multiple_of(block * rows, rows), rows)
        meta_ref[at, :] = jnp.where(lane < 64, start, adapter)
        angle = (token - start) * table_ref[0:1, :] - table_ref[1:2, :]
        turn_ref[at, :] = cosine(angle) * table_ref[2:3, :]
        return 0

    lax.fori_loop(0, meta_ref.shape[0] // rows, one, 0)
    for copy in copies:
        copy.wait()


def rank_kernel(count, slots, info, *refs):
    x = jnp.concatenate([ref[...] for ref in refs[:count]], axis=0)
    left_ref, meta_ref, slot_ref, fold_ref, held_ref = refs[count : count + 5]
    out_ref = refs[-1]
    products = rank_product(x, left_ref[...])
    adapter = jnp.concatenate([meta_ref[k * 128 : (k + 1) * 128, 64:65] for k in slots], axis=0)
    chosen = jnp.where(slot_ref[...] == adapter, products, 0.0).astype(jnp.bfloat16)
    out_ref[...] = held_ref[...]
    store_lanes(info, out_ref, across(fold_ref[...], chosen), slots)


def base_kernel(count, *refs):
    x = jnp.concatenate([ref[...] for ref in refs[:count]], axis=0)
    qkv_ref, up_ref, base_ref, up_base_ref, shared_ref = refs[count:]
    first = rank_product(x, qkv_ref[...])
    base_ref[...] = first
    shared_ref[...] = first[:, HEAD_SIZE:].astype(shared_ref.dtype)
    up_base_ref[...] = rank_product(x, up_ref[...])


def turn(part, table):
    width = table.shape[1]
    lane = lax.broadcasted_iota(jnp.int32, table.shape, 1)
    cos = jnp.where(lane < ROT, table, 1.0)
    sin = jnp.where(lane < ROT, pltpu.roll(table, width - ROT, 1), 0.0)
    head = part[:, :width]
    swapped = jnp.where(
        lane % 2 == 0, pltpu.roll(head, width - 1, 1), pltpu.roll(head, 1, 1)
    )
    return jnp.concatenate([head * cos + swapped * sin, part[:, width:]], axis=1)


def block_rows_of(refs, block):
    if block == 0:
        return jnp.concatenate([refs[0][...], refs[4][128:]], axis=0)
    if block == 3:
        return jnp.concatenate([refs[3][...], refs[4][:128]], axis=0)
    return refs[block][...]


def two_blocks(refs, index):
    return jnp.concatenate([block_rows_of(refs, 2 * index + k) for k in (0, 1)], axis=0)


def inner_kernel(info, *refs):
    base_refs, up_refs, (rank_ref, meta_ref, turn_ref, first_ref, last_ref) = refs[:5], refs[5:10], refs[10:15]
    qkv_right_ref, up_right_ref, bias_ref, left_ref = refs[15:19]
    q_ref, k_ref, v_ref, hidden_ref, out_ref = refs[19:]
    rows = 512
    columns = qkv_right_ref.shape[0]
    for block in range(BLOCKS // 2):
        at = slice(block * rows, (block + 1) * rows)
        adapter = meta_ref[at, 64:65]
        ranks = rank_rows(info, rank_ref, 4 * block, 4)
        total = two_blocks(base_refs, block) + rank_product(
            widened(ranks, first_ref, adapter, columns), qkv_right_ref[...]
        )
        table = turn_ref[at, :]
        q_ref[at, :] = (turn(total[:, :HEAD_SIZE], table) * HEAD_SIZE ** (-0.5)).astype(jnp.bfloat16)
        k_ref[at, :] = turn(total[:, HEAD_SIZE : 2 * HEAD_SIZE], table).astype(jnp.bfloat16)
        v_ref[at, :] = total[:, 2 * HEAD_SIZE :].astype(jnp.bfloat16)
        wide = widened(ranks, last_ref, adapter, columns)
        x = two_blocks(up_refs, block) + rank_product(wide, up_right_ref[...]) + bias_ref[...]
        inner = math.sqrt(2.0 / math.pi) * (x + 0.044715 * (x * x * x))
        hidden = (0.5 * x * (1.0 + jnp.tanh(inner))).astype(jnp.bfloat16)
        hidden_ref[at, :] = hidden
        lanes = folded(rank_product(hidden, left_ref[...]), adapter, last_ref)
        store_lanes(info, out_ref, lanes, range(4 * block, 4 * block + 4))


def far_kernel(first_row, info, *refs):
    shared_refs, (rank_ref, meta_ref, turn_ref, spread_ref, right_ref, k_ref, v_ref) = refs[:5], refs[5:]
    rows = 512
    for block in range(BLOCKS // 2):
        at = slice(block * rows, (block + 1) * rows)
        far_at = slice(first_row + block * rows, first_row + (block + 1) * rows)
        ranks = rank_rows(info, rank_ref, 4 * block, 4)
        wide = widened(ranks, spread_ref, meta_ref[far_at, 64:65], right_ref.shape[0])
        total = two_blocks(shared_refs, block).astype(jnp.float32)
        total = total + rank_product(wide, right_ref[:, HEAD_SIZE:])
        k_ref[at, :] = turn(total[:, :HEAD_SIZE], turn_ref[far_at, :]).astype(jnp.bfloat16)
        v_ref[at, :] = total[:, HEAD_SIZE:].astype(jnp.bfloat16)


def attention_kernel(req_count, info, *refs):
    q_ref, refs = refs[0], refs[1:]
    key_refs, value_refs, refs = refs[:req_count], refs[req_count : 2 * req_count], refs[2 * req_count :]
    meta_ref, spread_ref, left_ref, hidden_rank_ref, attended_ref, out_ref = refs[:6]
    keys_ref, values_ref, scores_ref, top_ref, sum_ref, acc_ref, fold_ref = refs[6:]
    span = rows = 512
    pair = 128
    group_rows = q_ref.shape[0]

    def lane_parts(value):
        return [value[:, k * pair : (k + 1) * pair] for k in range(span // pair)]

    def slot_rows(slot):
        return pl.ds(pl.multiple_of(slot * pair, pair), pair)

    for d in range(req_count):
        for k in range(SLOTS):
            at = slice((req_count - 1 - d) * group_rows + k * pair, (req_count - 1 - d) * group_rows + (k + 1) * pair)
            slot = slot_rows(info[PLACES + k])
            keys_ref[at, :] = key_refs[d][slot, :]
            values_ref[at, :] = value_refs[d][slot, :]
    first_token = info[BASES + info[PLACES]] - (req_count - 1) * group_rows

    def places(shape, dim):
        at = lax.broadcasted_iota(jnp.int32, shape, dim)
        before = at // pair * pair
        at = at - before + info[CORE] * (pair // 2)
        return (before + jnp.where(at >= pair, at - pair, at)).astype(jnp.float32)

    key_place = places((1, span), 1)
    query_place = places((rows, 1), 0)

    def one(block, _):
        slots = [slot_rows(info[PLACES + 4 * block + k]) for k in range(4)]

        def both(ref):
            return jnp.concatenate([ref[at, :] for at in slots], axis=0)

        meta = both(meta_ref)
        start = meta[:, 0:1]
        number = (req_count - 1) * (group_rows // span) + block
        query = query_place + (first_token + number * span).astype(jnp.float32)
        q = both(q_ref)
        lowest = jnp.min(start).astype(jnp.int32) - first_token
        top_ref[...] = jnp.full_like(top_ref, NEGATIVE_FILL)
        sum_ref[...] = jnp.zeros_like(sum_ref)
        acc_ref[...] = jnp.zeros_like(acc_ref)

        def score(j, _):
            at = pl.ds(pl.multiple_of(j * span, span), span)
            scores = across(q, keys_ref[at, :])
            key = key_place + (first_token + j * span).astype(jnp.float32)
            allowed = jnp.logical_and(key <= query, key >= start)
            scores = jnp.where(allowed, scores, NEGATIVE_FILL)
            scores_ref[:, at] = scores
            top_ref[...] = functools.reduce(jnp.maximum, lane_parts(scores), top_ref[...])
            return 0

        lax.fori_loop(lowest // span, number + 1, score, 0)
        top = jnp.max(top_ref[...], axis=1, keepdims=True)

        def weigh(j, _):
            at = pl.ds(pl.multiple_of(j * span, span), span)
            weights = jnp.exp(scores_ref[:, at] - top)
            sum_ref[...] = functools.reduce(jnp.add, lane_parts(weights), sum_ref[...])
            acc_ref[...] = acc_ref[...] + rank_product(weights.astype(jnp.bfloat16), values_ref[at, :])
            return 0

        lax.fori_loop(lowest // span, number + 1, weigh, 0)
        total = jnp.sum(sum_ref[...], axis=1, keepdims=True)
        attended = (acc_ref[...] / total).astype(jnp.bfloat16)
        lanes = folded(rank_product(attended, left_ref[...]), meta[:, 64:65], spread_ref)
        for k in range(4):
            attended_ref[slots[k], :] = attended[k * pair : (k + 1) * pair]
            at = pl.ds(pl.multiple_of((4 * block + k) * pair, pair), pair)
            fold_ref[:, at] = swap_halves(info, lanes[:, k * pair : (k + 1) * pair])
        return 0

    lax.fori_loop(0, BLOCKS // 2, one, 0)
    out_ref[...] = (fold_ref[...] + hidden_rank_ref[...].astype(jnp.float32)).astype(out_ref.dtype)


def main_kernel(block, attended_ref, hidden_ref, output_ref, down_ref, kept_ref, sent_ref):
    rows = 256
    sent = sent_ref.shape[0]
    width = 512
    attended = attended_ref[block * rows : (block + 1) * rows, :]
    hidden = hidden_ref[block * rows : (block + 1) * rows, :]

    for step in range(output_ref.shape[1] // width):
        at = slice(step * width, (step + 1) * width)
        total = rank_product(attended, output_ref[:, at]) + rank_product(hidden, down_ref[:, at])
        if block:
            sent_ref[:, at] = total[:sent].astype(sent_ref.dtype)
            kept_ref[:, at] = total[sent:]
        else:
            kept_ref[:, at] = total[: rows - sent]
            sent_ref[:, at] = total[rows - sent :].astype(sent_ref.dtype)


def adapt_kernel(slot, first, info, rank_ref, meta_ref, spread_ref, right_ref, kept_ref, arrived_ref, *out_refs):
    pair = 128
    half = pair // 2
    columns = spread_ref.shape[1]
    count = columns // (4 * ADAPTER_RANK)
    column_id = lax.broadcasted_iota(jnp.int32, (pair, columns), 1) // (2 * ADAPTER_RANK)
    partner = info[MLP] + 1 - 2 * info[CORE]
    column_id = column_id + jnp.where(column_id < count, info[MLP] * count, (partner - 1) * count)
    own = column_id.astype(jnp.float32) == meta_ref[slot * pair : (slot + 1) * pair, 64:65]
    spread = rank_product(rank_rows(info, rank_ref, slot, 1), spread_ref[...])
    wide = jnp.where(own, spread, 0.0).astype(jnp.bfloat16)
    width = 512

    for step in range(right_ref.shape[1] // width):
        at = slice(step * width, (step + 1) * width)
        if len(out_refs) == 1:
            total = rank_product(wide[:half], right_ref[:, at]) + kept_ref[first : first + half, at]
            total = total + arrived_ref[:, at].astype(jnp.float32)
            out_refs[0][:, at] = total.astype(out_refs[0].dtype)
        else:
            total = rank_product(wide, right_ref[:, at]) + kept_ref[:, at]
            out_refs[0][:, at] = total[:half] + arrived_ref[half:, at].astype(jnp.float32)
            out_refs[1][:, at] = total[half:] + arrived_ref[:half, at].astype(jnp.float32)


def call(kernel, operands, outs, info=None, scratch=(), mib=24, flops=1000, space=pltpu.VMEM, in_hbm=0):
    vmem = pl.BlockSpec(memory_space=pltpu.VMEM)
    specs = [pl.BlockSpec(memory_space=space)] * (len(operands) - in_hbm)
    specs += [pl.BlockSpec(memory_space=pltpu.HBM)] * in_hbm
    if info is not None:
        operands, specs = [info] + operands, [pl.BlockSpec(memory_space=pltpu.SMEM)] + specs
    return pl.pallas_call(
        kernel,
        in_specs=specs,
        out_specs=[vmem] * len(outs),
        out_shape=outs,
        scratch_shapes=scratch,
        compiler_params=pltpu.CompilerParams(vmem_limit_bytes=mib * 1024 * 1024),
        cost_estimate=pl.CostEstimate(flops=flops, bytes_accessed=1000, transcendentals=0),
    )(*operands)


def shape(rows, width, dtype=jnp.bfloat16):
    return jax.ShapeDtypeStruct((rows, width), dtype)


def sum_over_mlp(value, bits):
    for bit in bits:
        value = value + lax.ppermute(value, "mlp", [(i, i ^ bit) for i in range(16)])
    return value


def narrow(value):
    return value.astype(jnp.bfloat16)


def wide(value):
    return value.astype(jnp.float32)


def per_device(
    tokens,
    layer_norm_gain,
    layer_norm_bias,
    query_key_weight,
    output_weight,
    up_weight,
    input_bias,
    down_weight,
    output_bias,
    input_adapter_left,
    query_key_value_right,
    up_adapter_right,
    output_adapter_left,
    down_adapter_left,
    output_adapter_right,
    lengths,
    request_adapter,
    slot_adapter,
):
    block = tokens.shape[0]
    model_width = tokens.shape[1]
    pair_rows = 2 * block
    group_rows = SLOTS * pair_rows
    req_count = lax.axis_size("req")
    group = lax.axis_index("req")
    me = lax.axis_index("mlp")
    block_rows = 2 * pair_rows
    table = np.zeros((req_count, 16, 2 + SLOTS * (2 + req_count)), np.int32)
    for g in range(req_count):
        for m in range(16):
            side = 2 * (m % 2) - 1
            steps = [0, 4] + [t for s in (1, 2, 3) for t in (side * s, -side * s)]
            pairs = [RING[(PLACE[m // 2] + t) % 8] for t in steps]
            firsts = [(g - d) * group_rows + p * pair_rows for d in range(req_count) for p in pairs]
            table[g, m] = [m % 2, m] + pairs + [pairs.index(p) for p in range(SLOTS)] + firsts
    info = lax.dynamic_slice(jnp.asarray(table), (group, me, 0), (1, 1, table.shape[2])).reshape(-1)

    norm_args = [tokens, layer_norm_gain.reshape(1, -1), layer_norm_bias.reshape(1, -1)]
    norm_args = [pltpu.with_memory_space_constraint(x, pltpu.HBM) for x in norm_args]
    own = call(
        norm_kernel,
        norm_args,
        [shape(block, model_width)],
        scratch=[pltpu.VMEM(x.shape, x.dtype) for x in norm_args] + [pltpu.SemaphoreType.DMA((3,))],
        space=pltpu.HBM,
    )[0]
    other = to_partner(own)
    ring_a, ring_b = along_ring(own), along_ring(other)
    near_left, far_left = input_adapter_left, to_partner(input_adapter_left)

    float_lengths = wide(lengths)
    lane = np.arange(128)
    turn_rows = np.zeros((8, 128), np.float32)
    turn_rows[0] = np.exp(lane % ROT // 2 * (-2.0 * math.log(10000.0) / ROT))
    turn_rows[1] = np.where(lane < ROT, 0.0, math.pi / 2)
    turn_rows[2] = np.where(lane < ROT, 1.0, np.where(lane % 2 == 0, -1.0, 1.0))
    token_rows = req_count * group_rows
    token_args = [
        float_lengths[:, None],
        float_lengths[None, :],
        wide(request_adapter)[None, :],
        jnp.asarray(turn_rows),
    ]
    weights = [query_key_weight.reshape(model_width, 3 * HEAD_SIZE), up_weight]
    weights = [pltpu.with_memory_space_constraint(x, pltpu.HBM) for x in weights]
    meta, turns, qkv_rows, up_rows = call(
        token_kernel,
        token_args + weights,
        [shape(token_rows, 128, jnp.float32)] * 2 + [shape(*x.shape) for x in weights],
        info,
        [pltpu.SemaphoreType.DMA((2,))],
        in_hbm=2,
    )

    adapter_columns = query_key_value_right.shape[0]
    qkv_right = query_key_value_right.reshape(adapter_columns, 3 * HEAD_SIZE)
    spread_first = spread_table(ADAPTER_RANK, 0, 128)
    spread_last = spread_table(ADAPTER_RANK, ADAPTER_RANK, 128)
    near_right = output_adapter_right
    slot_columns = wide(jnp.repeat(slot_adapter, 2 * ADAPTER_RANK))[None, :]
    slot_columns = jnp.concatenate([slot_columns, to_partner(slot_columns)], axis=1)
    own_columns = near_right.shape[0]
    spread_own = spread_table(2 * ADAPTER_RANK, 0, 2 * own_columns)
    hidden_width = up_weight.shape[1]

    def to_group(value, d):
        return lax.ppermute(value, "req", [(g, g + d) for g in range(req_count - d)])

    held = functools.partial(pltpu.VMEM, dtype=jnp.float32)

    def add_ranks(part, slots, so_far):
        return call(
            functools.partial(rank_kernel, len(part), slots),
            list(part) + [pair_left, meta, slot_columns, spread_own, so_far],
            [shape(32, group_rows)],
            info,
        )[0]

    def products_of(part, flops=1000):
        rows = len(part) * block
        return call(
            functools.partial(base_kernel, len(part)),
            list(part) + [qkv_rows, up_rows],
            [
                shape(rows, 3 * HEAD_SIZE, jnp.float32),
                shape(rows, hidden_width, jnp.float32),
                shape(rows, 2 * HEAD_SIZE),
            ],
            flops=flops,
        )

    def to_groups(value):
        return [to_group(value, d) for d in range(1, req_count)]

    def arrivals(a, b):
        return a, b, to_partner(b), to_partner(a)

    tie = lax.optimization_barrier
    own_part = (own, other)
    ring_a, meta, turns, qkv_rows, up_rows = tie((ring_a, meta, turns, qkv_rows, up_rows))
    ring_b, near_left, far_left = tie((ring_b, near_left, far_left))
    pair_left = jnp.concatenate([near_left, far_left], axis=1)
    part = arrivals(ring_a, ring_b)
    ring_a, ring_b = along_ring(ring_a), along_ring(ring_b)
    ranks = add_ranks(own_part + part, (0, 2, 3), jnp.zeros((32, group_rows), jnp.bfloat16))
    zeroth = products_of(own_part)
    ring_a, zeroth = tie((ring_a, zeroth))
    far_own = to_groups(zeroth[2])
    first = products_of(part)
    ring_b, ranks, first, far_own = tie((ring_b, ranks, first, far_own))
    part = arrivals(ring_a, ring_b)
    ring_a, ring_b = along_ring(ring_a), along_ring(ring_b)
    far_right = to_partner(near_right)
    far_early = to_groups(first[2])
    ranks = add_ranks(part, (4, 5), ranks)
    second = products_of(part)
    ring_b, ranks, second, far_right = tie((ring_b, ranks, second, far_right))
    part = arrivals(ring_a, ring_b)
    ring_a = along_ring(ring_a)
    held_rows = part[:2]
    third = products_of(held_rows, 2000000000)
    ranks = add_ranks(held_rows, (6,), ranks)
    ring_a, ranks, third, far_early = tie((ring_a, ranks, third, far_early))
    part = part[2:] + (ring_a, to_partner(ring_a))
    ranks = add_ranks(part, (7, 1), ranks)
    moved = lax.ppermute(ranks, "mlp", [(i, i ^ 2) for i in range(16)])
    fourth = products_of(part)
    ranks, fourth = tie((ranks + moved, fourth))
    far_late = to_groups(jnp.concatenate([second[2], third[2], fourth[2]], axis=0))
    rank_in = sum_over_mlp(ranks, (4, 8))
    products = (zeroth, first, second, third, fourth)

    bias_row = input_bias.reshape(1, -1)
    far_rank = to_groups(rank_in)
    queries, own_keys, own_values, hidden, hidden_rank = call(
        inner_kernel,
        [part[0] for part in products]
        + [part[1] for part in products]
        + [rank_in, meta, turns, spread_first, spread_last]
        + [qkv_right, up_adapter_right, bias_row, down_adapter_left],
        [shape(group_rows, HEAD_SIZE)] * 3 + [shape(group_rows, hidden_width), shape(32, group_rows)],
        info,
    )
    keys, values = [own_keys], [own_values]
    for d in range(1, req_count):
        early, late = far_early[d - 1], far_late[d - 1]
        ends = (0, block_rows, block_rows + pair_rows, 2 * block_rows + pair_rows)
        shared = [far_own[d - 1], early] + [late[ends[k] : ends[k + 1]] for k in range(3)]
        far_keys, far_values = call(
            functools.partial(far_kernel, d * group_rows),
            shared + [far_rank[d - 1], meta, turns, spread_first, qkv_right],
            [shape(group_rows, HEAD_SIZE)] * 2,
            info,
        )
        keys.append(far_keys)
        values.append(far_values)

    output_left = output_adapter_left.reshape(HEAD_SIZE, adapter_columns)
    attended, rank_out = call(
        functools.partial(attention_kernel, req_count),
        [queries] + keys + values + [meta, spread_first, output_left, hidden_rank],
        [shape(group_rows, HEAD_SIZE), shape(32, group_rows)],
        info,
        [
            pltpu.VMEM((req_count * group_rows, HEAD_SIZE), jnp.bfloat16),
            pltpu.VMEM((req_count * group_rows, HEAD_SIZE), jnp.bfloat16),
            held((2 * block_rows, req_count * group_rows)),
            held((2 * block_rows, 128)),
            held((2 * block_rows, 128)),
            held((2 * block_rows, HEAD_SIZE)),
            held((32, group_rows)),
        ],
        mib=24 + 3 * req_count,
    )
    output_rows = output_weight.reshape(HEAD_SIZE, model_width)

    def main(k, attended, hidden):
        sent = block if k == 0 else pair_rows
        return call(
            functools.partial(main_kernel, k),
            [attended, hidden, output_rows, down_weight],
            [shape(block_rows - sent, model_width, jnp.float32), shape(sent, model_width)],
        )

    kept, arrived, sent = {}, {}, {}
    for bit, k in zip((1, 2, 4, 8), (0, 3, 2, 1)):
        moved = lax.ppermute(rank_out, "mlp", [(i, i ^ bit) for i in range(16)])
        kept[k], sent[k] = main(k, attended, hidden)
        rank_out, attended, kept[k], sent[k] = tie((rank_out + moved, attended, kept[k], sent[k]))
        if k == 0:
            arrived[k] = to_partner(sent[k])
        if bit == 4:
            arrived[3] = to_partner(sent[3])
            rank_out, arrived[0] = tie((rank_out, arrived[0]))
    rank_out, arrived[3] = tie((rank_out, arrived[3]))
    pair_right = jnp.concatenate([near_right, far_right], axis=0)

    def adapt(slot, half, kept, first, arrived):
        if half:
            outs = [shape(block, model_width, jnp.bfloat16 if slot else jnp.float32)]
        else:
            outs = [shape(block, model_width, jnp.float32)] * 2
        return call(
            functools.partial(adapt_kernel, slot, first),
            [rank_out, meta, spread_own, pair_right, kept, arrived],
            outs,
            info,
        )

    chain_a = along_ring(adapt(1, True, kept[0], 2 * block, arrived[0])[0])
    chain_b = None
    for s in (3, 2, 1):
        add_a, add_b = adapt(2 * s + 1, False, kept[s], 0, arrived[s])
        if s > 1:
            arrived[s - 1] = to_partner(sent[s - 1])
        if chain_b is None:
            chain_b = along_ring(narrow(add_b))
            chain_a = along_ring(narrow(wide(chain_a) + add_a))
        else:
            chain_a = along_ring(narrow(wide(chain_a) + add_a))
            chain_b = along_ring(narrow(wide(chain_b) + add_b))
    own_sum = adapt(0, True, kept[0], 0, tokens)[0]
    chain_a, own_sum = tie((chain_a, own_sum))
    arrived_last = to_partner(narrow(wide(chain_b) + kept[0][block : 2 * block]))
    return narrow(wide(chain_a) + wide(arrived_last) + own_sum + output_bias)


def solution(mesh):
    in_specs = (
        P(("req", "mlp"), None),
        P(),
        P(),
        P(None, "mlp", None),
        P("mlp", None, None),
        P(None, "mlp"),
        P("mlp"),
        P("mlp", None),
        P(),
        P(None, "mlp"),
        P(None, "mlp", None),
        P(None, "mlp"),
        P("mlp", None, None),
        P("mlp", None),
        P("mlp", None),
        P(),
        P(),
        P("mlp"),
    )
    out_specs = P(("req", "mlp"), None)
    return jax.shard_map(
        per_device, mesh=mesh, in_specs=in_specs, out_specs=out_specs, check_vma=False
    )
```

```python
import functools
import math

import jax
import jax.numpy as jnp
import numpy as np
from jax import lax
from jax.experimental import pallas as pl
from jax.experimental.pallas import tpu as pltpu
from jax.sharding import PartitionSpec as P

HEAD_SIZE = 256
ROT = 64
ADAPTER_RANK = 16
EPSILON = 1e-05
NEGATIVE_FILL = -1e30
RING = (0, 2, 4, 6, 7, 5, 3, 1)
PLACE = tuple(RING.index(pair) for pair in range(8))
CORE_PERM = [(i, i ^ 1) for i in range(16)]
RING_PERM = [(RING[i] * 2, RING[(i + 1) % 8] * 2) for i in range(8)] + [
    (RING[i] * 2 + 1, RING[(i - 1) % 8] * 2 + 1) for i in range(8)
]
SLOTS = 8
BLOCKS = 4
CORE, MLP, PAIRS, PLACES, BASES = 0, 1, 2, 2 + SLOTS, 2 + 2 * SLOTS


def to_partner(value):
    return lax.ppermute(value, "mlp", CORE_PERM)


def along_ring(value):
    return lax.ppermute(value, "mlp", RING_PERM)


def rank_product(left_side, right_side):
    return jnp.dot(left_side, right_side, preferred_element_type=jnp.float32)


def across(left_side, right_side):
    return lax.dot_general(
        left_side, right_side, (((1,), (1,)), ((), ())), preferred_element_type=jnp.float32
    )


def spread_table(period, first, width):
    row = np.arange(32)[:, None]
    column = np.arange(width)[None, :]
    return jnp.asarray((row - first == column % period).astype(np.float32), jnp.bfloat16)


def swap_halves(info, lanes):
    half = lanes.shape[1] // 2
    return jnp.where(info[CORE] == 1, pltpu.roll(lanes, half, 1), lanes)


def lane_ids(shape, period):
    return (lax.broadcasted_iota(jnp.int32, shape, 1) // period).astype(jnp.float32)


def pair_at(info, slot, rows):
    return pl.ds(pl.multiple_of(info[PAIRS + slot] * rows, rows), rows)


def store_lanes(info, out_ref, lanes, slots):
    width = out_ref.shape[1] // SLOTS
    for k, slot in enumerate(slots):
        part = lanes[:, k * width : (k + 1) * width]
        out_ref[:, pair_at(info, slot, width)] = swap_halves(info, part).astype(out_ref.dtype)


def rank_rows(info, rank_ref, slot, count):
    width = rank_ref.shape[1] // SLOTS
    lanes = [
        swap_halves(info, rank_ref[:, pair_at(info, slot + k, width)].astype(jnp.float32))
        for k in range(count)
    ]
    lanes = lanes[0] if count == 1 else jnp.concatenate(lanes, axis=1)
    return jnp.transpose(lanes).astype(jnp.bfloat16)


def widened(rows, spread_ref, adapter, columns):
    tile = rank_product(rows, spread_ref[...]).astype(jnp.bfloat16)
    group = lax.broadcasted_iota(jnp.int32, tile.shape, 1) // ADAPTER_RANK
    apart = (adapter - group.astype(jnp.float32)).astype(jnp.bfloat16)
    step = tile.shape[1] // ADAPTER_RANK
    zero = jnp.zeros_like(tile)
    return jnp.concatenate(
        [jnp.where(apart == first, tile, zero) for first in range(0, columns // ADAPTER_RANK, step)], axis=1
    )


def folded(products, adapter, spread_ref):
    width = spread_ref.shape[1]
    group = lax.broadcasted_iota(jnp.int32, (products.shape[0], width), 1) // ADAPTER_RANK
    apart = adapter - group.astype(jnp.float32)
    total = None
    for first in range(0, products.shape[1], width):
        part = products[:, first : first + width]
        part = jnp.where(apart == float(first // ADAPTER_RANK), part, 0.0)
        total = part if total is None else total + part
    return across(spread_ref[...], total.astype(jnp.bfloat16))


def cosine(angle):
    turns = jnp.floor(angle * (1.0 / math.pi) + 0.5)
    rest = ((angle - turns * 3.140625) - turns * 9.67502593994140625e-4) - turns * 1.509957990978376e-7
    square = rest * rest
    value = jnp.full_like(square, 1.0 / 479001600.0)
    for factor in (-1.0 / 3628800.0, 1.0 / 40320.0, -1.0 / 720.0, 1.0 / 24.0, -0.5, 1.0):
        value = value * square + factor
    odd = turns - 2.0 * jnp.floor(turns * 0.5)
    return value * (1.0 - 2.0 * odd)


def norm_kernel(x_hbm, gain_hbm, bias_hbm, out_ref, x_ref, gain_ref, bias_ref, sems):
    pairs = ((x_hbm, x_ref), (gain_hbm, gain_ref), (bias_hbm, bias_ref))
    copies = [pltpu.make_async_copy(a, b, sems.at[k]) for k, (a, b) in enumerate(pairs)]
    for copy in copies:
        copy.start()
    copies[0].wait()
    values = x_ref[...].astype(jnp.float32)
    center = values - jnp.mean(values, axis=1, keepdims=True)
    spread = jnp.mean(center * center, axis=1, keepdims=True)
    scaled = center * lax.rsqrt(spread + EPSILON)
    copies[1].wait()
    copies[2].wait()
    out_ref[...] = (scaled * gain_ref[...] + bias_ref[...]).astype(out_ref.dtype)


def local_tokens(info, slot, shape, dim):
    rows = shape[dim] // 2
    at = lax.broadcasted_iota(jnp.int32, shape, dim)
    second = at >= rows
    at = jnp.where(second, at - rows, at) + info[CORE] * (rows // 2)
    at = jnp.where(at >= rows, at - rows, at)
    return (at + jnp.where(second, info[BASES + slot + 1], info[BASES + slot])).astype(jnp.float32)


def token_kernel(info, column_ref, row_ref, ids_ref, table_ref, *refs):
    count = (len(refs) - 3) // 2
    meta_ref, turn_ref = refs[count : count + 2]
    pairs = zip(refs[:count], refs[count + 2 : -1])
    copies = [pltpu.make_async_copy(a, b, refs[-1].at[k]) for k, (a, b) in enumerate(pairs)]
    for copy in copies:
        copy.start()
    rows = 2 * 128
    count = row_ref.shape[1]
    earlier = lax.broadcasted_iota(jnp.int32, (count, count), 0) < lax.broadcasted_iota(
        jnp.int32, (count, count), 1
    )
    anchors = jnp.sum(jnp.where(earlier, column_ref[...], 0.0), axis=0, keepdims=True)
    endings = anchors + row_ref[...]
    ids = ids_ref[...]
    lane = lax.broadcasted_iota(jnp.int32, (rows, 128), 1)

    def one(block, _):
        token = local_tokens(info, 2 * block, (rows, 1), 0)
        inside = jnp.logical_and(anchors <= token, token < endings)
        start = jnp.sum(jnp.where(inside, anchors, 0.0), axis=1, keepdims=True)
        adapter = jnp.sum(jnp.where(inside, ids, 0.0), axis=1, keepdims=True)
        at = pl.ds(pl.multiple_of(block * rows, rows), rows)
        meta_ref[at, :] = jnp.where(lane < 64, start, adapter)
        angle = (token - start) * table_ref[0:1, :] - table_ref[1:2, :]
        turn_ref[at, :] = cosine(angle) * table_ref[2:3, :]
        return 0

    lax.fori_loop(0, meta_ref.shape[0] // rows, one, 0)
    for copy in copies:
        copy.wait()


def rank_kernel(count, slots, info, *refs):
    x = jnp.concatenate([ref[...] for ref in refs[:count]], axis=0)
    left_ref, meta_ref, slot_ref, fold_ref, held_ref = refs[count : count + 5]
    out_ref = refs[-1]
    products = rank_product(x, left_ref[...])
    adapter = jnp.concatenate([meta_ref[k * 128 : (k + 1) * 128, 64:65] for k in slots], axis=0)
    chosen = jnp.where(slot_ref[...] == adapter, products, 0.0).astype(jnp.bfloat16)
    out_ref[...] = held_ref[...]
    store_lanes(info, out_ref, across(fold_ref[...], chosen), slots)


def base_kernel(count, *refs):
    x = jnp.concatenate([ref[...] for ref in refs[:count]], axis=0)
    qkv_ref, up_ref, base_ref, up_base_ref, shared_ref = refs[count:]
    first = rank_product(x, qkv_ref[...])
    base_ref[...] = first
    shared_ref[...] = first[:, HEAD_SIZE:].astype(shared_ref.dtype)
    up_base_ref[...] = rank_product(x, up_ref[...])


def turn(part, table):
    width = table.shape[1]
    lane = lax.broadcasted_iota(jnp.int32, table.shape, 1)
    cos = jnp.where(lane < ROT, table, 1.0)
    sin = jnp.where(lane < ROT, pltpu.roll(table, width - ROT, 1), 0.0)
    head = part[:, :width]
    swapped = jnp.where(
        lane % 2 == 0, pltpu.roll(head, width - 1, 1), pltpu.roll(head, 1, 1)
    )
    return jnp.concatenate([head * cos + swapped * sin, part[:, width:]], axis=1)


def block_rows_of(refs, block):
    if block == 0:
        return jnp.concatenate([refs[0][...], refs[4][128:]], axis=0)
    if block == 3:
        return jnp.concatenate([refs[3][...], refs[4][:128]], axis=0)
    return refs[block][...]


def four_blocks(refs, index):
    return jnp.concatenate([block_rows_of(refs, 4 * index + k) for k in range(4)], axis=0)


def inner_kernel(info, *refs):
    base_refs, up_refs, (rank_ref, meta_ref, turn_ref, first_ref, last_ref) = refs[:5], refs[5:10], refs[10:15]
    qkv_right_ref, up_right_ref, bias_ref, left_ref = refs[15:19]
    q_ref, k_ref, v_ref, hidden_ref, out_ref = refs[19:]
    rows = 1024
    columns = qkv_right_ref.shape[0]
    for block in range(BLOCKS // 4):
        at = slice(block * rows, (block + 1) * rows)
        adapter = meta_ref[at, 64:65]
        ranks = rank_rows(info, rank_ref, 8 * block, 8)
        total = four_blocks(base_refs, block) + rank_product(
            widened(ranks, first_ref, adapter, columns), qkv_right_ref[...]
        )
        table = turn_ref[at, :]
        q_ref[at, :] = (turn(total[:, :HEAD_SIZE], table) * HEAD_SIZE ** (-0.5)).astype(jnp.bfloat16)
        k_ref[at, :] = turn(total[:, HEAD_SIZE : 2 * HEAD_SIZE], table).astype(jnp.bfloat16)
        v_ref[at, :] = total[:, 2 * HEAD_SIZE :].astype(jnp.bfloat16)
        wide = widened(ranks, last_ref, adapter, columns)
        x = four_blocks(up_refs, block) + rank_product(wide, up_right_ref[...]) + bias_ref[...]
        inner = math.sqrt(2.0 / math.pi) * (x + 0.044715 * (x * x * x))
        hidden = (0.5 * x * (1.0 + jnp.tanh(inner))).astype(jnp.bfloat16)
        hidden_ref[at, :] = hidden
        lanes = folded(rank_product(hidden, left_ref[...]), adapter, last_ref)
        store_lanes(info, out_ref, lanes, range(8 * block, 8 * block + 8))


def far_kernel(first_row, info, *refs):
    shared_refs, (rank_ref, meta_ref, turn_ref, spread_ref, right_ref, k_ref, v_ref) = refs[:5], refs[5:]
    rows = 1024
    for block in range(BLOCKS // 4):
        at = slice(block * rows, (block + 1) * rows)
        far_at = slice(first_row + block * rows, first_row + (block + 1) * rows)
        ranks = rank_rows(info, rank_ref, 8 * block, 8)
        wide = widened(ranks, spread_ref, meta_ref[far_at, 64:65], right_ref.shape[0])
        total = four_blocks(shared_refs, block).astype(jnp.float32)
        total = total + rank_product(wide, right_ref[:, HEAD_SIZE:])
        k_ref[at, :] = turn(total[:, :HEAD_SIZE], turn_ref[far_at, :]).astype(jnp.bfloat16)
        v_ref[at, :] = total[:, HEAD_SIZE:].astype(jnp.bfloat16)


def attention_kernel(req_count, info, *refs):
    q_ref, refs = refs[0], refs[1:]
    key_refs, value_refs, refs = refs[:req_count], refs[req_count : 2 * req_count], refs[2 * req_count :]
    meta_ref, spread_ref, left_ref, hidden_rank_ref, attended_ref, out_ref = refs[:6]
    keys_ref, values_ref, scores_ref, top_ref, sum_ref, acc_ref, fold_ref = refs[6:]
    span = rows = 512
    pair = 128
    group_rows = q_ref.shape[0]

    def lane_parts(value):
        return [value[:, k * pair : (k + 1) * pair] for k in range(span // pair)]

    def slot_rows(slot):
        return pl.ds(pl.multiple_of(slot * pair, pair), pair)

    for d in range(req_count):
        for k in range(SLOTS):
            at = slice((req_count - 1 - d) * group_rows + k * pair, (req_count - 1 - d) * group_rows + (k + 1) * pair)
            slot = slot_rows(info[PLACES + k])
            keys_ref[at, :] = key_refs[d][slot, :]
            values_ref[at, :] = value_refs[d][slot, :]
    first_token = info[BASES + info[PLACES]] - (req_count - 1) * group_rows

    def places(shape, dim):
        at = lax.broadcasted_iota(jnp.int32, shape, dim)
        before = at // pair * pair
        at = at - before + info[CORE] * (pair // 2)
        return (before + jnp.where(at >= pair, at - pair, at)).astype(jnp.float32)

    key_place = places((1, span), 1)
    query_place = places((rows, 1), 0)

    def one(block, _):
        slots = [slot_rows(info[PLACES + 4 * block + k]) for k in range(4)]

        def both(ref):
            return jnp.concatenate([ref[at, :] for at in slots], axis=0)

        meta = both(meta_ref)
        start = meta[:, 0:1]
        number = (req_count - 1) * (group_rows // span) + block
        query = query_place + (first_token + number * span).astype(jnp.float32)
        q = both(q_ref)
        lowest = jnp.min(start).astype(jnp.int32) - first_token
        top_ref[...] = jnp.full_like(top_ref, NEGATIVE_FILL)
        sum_ref[...] = jnp.zeros_like(sum_ref)
        acc_ref[...] = jnp.zeros_like(acc_ref)

        def score(j, _):
            at = pl.ds(pl.multiple_of(j * span, span), span)
            scores = across(q, keys_ref[at, :])
            key = key_place + (first_token + j * span).astype(jnp.float32)
            allowed = jnp.logical_and(key <= query, key >= start)
            scores = jnp.where(allowed, scores, NEGATIVE_FILL)
            scores_ref[:, at] = scores
            top_ref[...] = functools.reduce(jnp.maximum, lane_parts(scores), top_ref[...])
            return 0

        lax.fori_loop(lowest // span, number + 1, score, 0)
        top = jnp.max(top_ref[...], axis=1, keepdims=True)

        def weigh(j, _):
            at = pl.ds(pl.multiple_of(j * span, span), span)
            weights = jnp.exp(scores_ref[:, at] - top)
            sum_ref[...] = functools.reduce(jnp.add, lane_parts(weights), sum_ref[...])
            acc_ref[...] = acc_ref[...] + rank_product(weights.astype(jnp.bfloat16), values_ref[at, :])
            return 0

        lax.fori_loop(lowest // span, number + 1, weigh, 0)
        total = jnp.sum(sum_ref[...], axis=1, keepdims=True)
        attended = (acc_ref[...] / total).astype(jnp.bfloat16)
        lanes = folded(rank_product(attended, left_ref[...]), meta[:, 64:65], spread_ref)
        for k in range(4):
            attended_ref[slots[k], :] = attended[k * pair : (k + 1) * pair]
            at = pl.ds(pl.multiple_of((4 * block + k) * pair, pair), pair)
            fold_ref[:, at] = swap_halves(info, lanes[:, k * pair : (k + 1) * pair])
        return 0

    lax.fori_loop(0, BLOCKS // 2, one, 0)
    out_ref[...] = (fold_ref[...] + hidden_rank_ref[...].astype(jnp.float32)).astype(out_ref.dtype)


def main_kernel(block, attended_ref, hidden_ref, output_ref, down_ref, kept_ref, sent_ref):
    rows = 256
    sent = sent_ref.shape[0]
    width = 512
    attended = attended_ref[block * rows : (block + 1) * rows, :]
    hidden = hidden_ref[block * rows : (block + 1) * rows, :]

    for step in range(output_ref.shape[1] // width):
        at = slice(step * width, (step + 1) * width)
        total = rank_product(attended, output_ref[:, at]) + rank_product(hidden, down_ref[:, at])
        if block:
            sent_ref[:, at] = total[:sent].astype(sent_ref.dtype)
            kept_ref[:, at] = total[sent:]
        else:
            kept_ref[:, at] = total[: rows - sent]
            sent_ref[:, at] = total[rows - sent :].astype(sent_ref.dtype)


def adapt_kernel(slot, first, info, rank_ref, meta_ref, spread_ref, right_ref, kept_ref, arrived_ref, *out_refs):
    pair = 128
    half = pair // 2
    columns = spread_ref.shape[1]
    count = columns // (4 * ADAPTER_RANK)
    column_id = lax.broadcasted_iota(jnp.int32, (pair, columns), 1) // (2 * ADAPTER_RANK)
    partner = info[MLP] + 1 - 2 * info[CORE]
    column_id = column_id + jnp.where(column_id < count, info[MLP] * count, (partner - 1) * count)
    own = column_id.astype(jnp.float32) == meta_ref[slot * pair : (slot + 1) * pair, 64:65]
    spread = rank_product(rank_rows(info, rank_ref, slot, 1), spread_ref[...])
    wide = jnp.where(own, spread, 0.0).astype(jnp.bfloat16)
    width = 512

    for step in range(right_ref.shape[1] // width):
        at = slice(step * width, (step + 1) * width)
        if len(out_refs) == 1:
            total = rank_product(wide[:half], right_ref[:, at]) + kept_ref[first : first + half, at]
            total = total + arrived_ref[:, at].astype(jnp.float32)
            out_refs[0][:, at] = total.astype(out_refs[0].dtype)
        else:
            total = rank_product(wide, right_ref[:, at]) + kept_ref[:, at]
            out_refs[0][:, at] = total[:half] + arrived_ref[half:, at].astype(jnp.float32)
            out_refs[1][:, at] = total[half:] + arrived_ref[:half, at].astype(jnp.float32)


def call(kernel, operands, outs, info=None, scratch=(), mib=24, flops=1000, space=pltpu.VMEM, in_hbm=0):
    vmem = pl.BlockSpec(memory_space=pltpu.VMEM)
    specs = [pl.BlockSpec(memory_space=space)] * (len(operands) - in_hbm)
    specs += [pl.BlockSpec(memory_space=pltpu.HBM)] * in_hbm
    if info is not None:
        operands, specs = [info] + operands, [pl.BlockSpec(memory_space=pltpu.SMEM)] + specs
    return pl.pallas_call(
        kernel,
        in_specs=specs,
        out_specs=[vmem] * len(outs),
        out_shape=outs,
        scratch_shapes=scratch,
        compiler_params=pltpu.CompilerParams(vmem_limit_bytes=mib * 1024 * 1024),
        cost_estimate=pl.CostEstimate(flops=flops, bytes_accessed=1000, transcendentals=0),
    )(*operands)


def shape(rows, width, dtype=jnp.bfloat16):
    return jax.ShapeDtypeStruct((rows, width), dtype)


def sum_over_mlp(value, bits):
    for bit in bits:
        value = value + lax.ppermute(value, "mlp", [(i, i ^ bit) for i in range(16)])
    return value


def narrow(value):
    return value.astype(jnp.bfloat16)


def wide(value):
    return value.astype(jnp.float32)


def per_device(
    tokens,
    layer_norm_gain,
    layer_norm_bias,
    query_key_weight,
    output_weight,
    up_weight,
    input_bias,
    down_weight,
    output_bias,
    input_adapter_left,
    query_key_value_right,
    up_adapter_right,
    output_adapter_left,
    down_adapter_left,
    output_adapter_right,
    lengths,
    request_adapter,
    slot_adapter,
):
    block = tokens.shape[0]
    model_width = tokens.shape[1]
    pair_rows = 2 * block
    group_rows = SLOTS * pair_rows
    req_count = lax.axis_size("req")
    group = lax.axis_index("req")
    me = lax.axis_index("mlp")
    block_rows = 2 * pair_rows
    table = np.zeros((req_count, 16, 2 + SLOTS * (2 + req_count)), np.int32)
    for g in range(req_count):
        for m in range(16):
            side = 2 * (m % 2) - 1
            steps = [0, 4] + [t for s in (1, 2, 3) for t in (side * s, -side * s)]
            pairs = [RING[(PLACE[m // 2] + t) % 8] for t in steps]
            firsts = [(g - d) * group_rows + p * pair_rows for d in range(req_count) for p in pairs]
            table[g, m] = [m % 2, m] + pairs + [pairs.index(p) for p in range(SLOTS)] + firsts
    info = lax.dynamic_slice(jnp.asarray(table), (group, me, 0), (1, 1, table.shape[2])).reshape(-1)

    norm_args = [tokens, layer_norm_gain.reshape(1, -1), layer_norm_bias.reshape(1, -1)]
    norm_args = [pltpu.with_memory_space_constraint(x, pltpu.HBM) for x in norm_args]
    own = call(
        norm_kernel,
        norm_args,
        [shape(block, model_width)],
        scratch=[pltpu.VMEM(x.shape, x.dtype) for x in norm_args] + [pltpu.SemaphoreType.DMA((3,))],
        space=pltpu.HBM,
    )[0]
    other = to_partner(own)
    ring_a, ring_b = along_ring(own), along_ring(other)
    near_left, far_left = input_adapter_left, to_partner(input_adapter_left)

    float_lengths = wide(lengths)
    lane = np.arange(128)
    turn_rows = np.zeros((8, 128), np.float32)
    turn_rows[0] = np.exp(lane % ROT // 2 * (-2.0 * math.log(10000.0) / ROT))
    turn_rows[1] = np.where(lane < ROT, 0.0, math.pi / 2)
    turn_rows[2] = np.where(lane < ROT, 1.0, np.where(lane % 2 == 0, -1.0, 1.0))
    token_rows = req_count * group_rows
    token_args = [
        float_lengths[:, None],
        float_lengths[None, :],
        wide(request_adapter)[None, :],
        jnp.asarray(turn_rows),
    ]
    weights = [query_key_weight.reshape(model_width, 3 * HEAD_SIZE), up_weight]
    weights = [pltpu.with_memory_space_constraint(x, pltpu.HBM) for x in weights]
    meta, turns, qkv_rows, up_rows = call(
        token_kernel,
        token_args + weights,
        [shape(token_rows, 128, jnp.float32)] * 2 + [shape(*x.shape) for x in weights],
        info,
        [pltpu.SemaphoreType.DMA((2,))],
        in_hbm=2,
    )

    adapter_columns = query_key_value_right.shape[0]
    qkv_right = query_key_value_right.reshape(adapter_columns, 3 * HEAD_SIZE)
    spread_first = spread_table(ADAPTER_RANK, 0, 128)
    spread_last = spread_table(ADAPTER_RANK, ADAPTER_RANK, 128)
    near_right = output_adapter_right
    slot_columns = wide(jnp.repeat(slot_adapter, 2 * ADAPTER_RANK))[None, :]
    slot_columns = jnp.concatenate([slot_columns, to_partner(slot_columns)], axis=1)
    own_columns = near_right.shape[0]
    spread_own = spread_table(2 * ADAPTER_RANK, 0, 2 * own_columns)
    hidden_width = up_weight.shape[1]

    def to_group(value, d):
        return lax.ppermute(value, "req", [(g, g + d) for g in range(req_count - d)])

    held = functools.partial(pltpu.VMEM, dtype=jnp.float32)

    def add_ranks(part, slots, so_far):
        return call(
            functools.partial(rank_kernel, len(part), slots),
            list(part) + [pair_left, meta, slot_columns, spread_own, so_far],
            [shape(32, group_rows)],
            info,
        )[0]

    def products_of(part, flops=1000):
        rows = len(part) * block
        return call(
            functools.partial(base_kernel, len(part)),
            list(part) + [qkv_rows, up_rows],
            [
                shape(rows, 3 * HEAD_SIZE, jnp.float32),
                shape(rows, hidden_width, jnp.float32),
                shape(rows, 2 * HEAD_SIZE),
            ],
            flops=flops,
        )

    def to_groups(value):
        return [to_group(value, d) for d in range(1, req_count)]

    def arrivals(a, b):
        return a, b, to_partner(b), to_partner(a)

    tie = lax.optimization_barrier
    own_part = (own, other)
    ring_a, meta, turns, qkv_rows, up_rows = tie((ring_a, meta, turns, qkv_rows, up_rows))
    ring_b, near_left, far_left = tie((ring_b, near_left, far_left))
    pair_left = jnp.concatenate([near_left, far_left], axis=1)
    part = arrivals(ring_a, ring_b)
    ring_a, ring_b = along_ring(ring_a), along_ring(ring_b)
    ranks = add_ranks(own_part + part, (0, 2, 3), jnp.zeros((32, group_rows), jnp.bfloat16))
    zeroth = products_of(own_part)
    ring_a, zeroth = tie((ring_a, zeroth))
    far_own = to_groups(zeroth[2])
    first = products_of(part)
    ring_b, ranks, first, far_own = tie((ring_b, ranks, first, far_own))
    part = arrivals(ring_a, ring_b)
    ring_a, ring_b = along_ring(ring_a), along_ring(ring_b)
    far_right = to_partner(near_right)
    far_early = to_groups(first[2])
    ranks = add_ranks(part, (4, 5), ranks)
    second = products_of(part)
    ring_b, ranks, second, far_right = tie((ring_b, ranks, second, far_right))
    part = arrivals(ring_a, ring_b)
    ring_a = along_ring(ring_a)
    held_rows = part[:2]
    third = products_of(held_rows, 2000000000)
    ranks = add_ranks(held_rows, (6,), ranks)
    ring_a, ranks, third, far_early = tie((ring_a, ranks, third, far_early))
    part = part[2:] + (ring_a, to_partner(ring_a))
    ranks = add_ranks(part, (7, 1), ranks)
    moved = lax.ppermute(ranks, "mlp", [(i, i ^ 2) for i in range(16)])
    fourth = products_of(part)
    ranks, fourth = tie((ranks + moved, fourth))
    far_late = to_groups(jnp.concatenate([second[2], third[2], fourth[2]], axis=0))
    rank_in = sum_over_mlp(ranks, (4, 8))
    products = (zeroth, first, second, third, fourth)

    bias_row = input_bias.reshape(1, -1)
    far_rank = to_groups(rank_in)
    queries, own_keys, own_values, hidden, hidden_rank = call(
        inner_kernel,
        [part[0] for part in products]
        + [part[1] for part in products]
        + [rank_in, meta, turns, spread_first, spread_last]
        + [qkv_right, up_adapter_right, bias_row, down_adapter_left],
        [shape(group_rows, HEAD_SIZE)] * 3 + [shape(group_rows, hidden_width), shape(32, group_rows)],
        info,
    )
    keys, values = [own_keys], [own_values]
    for d in range(1, req_count):
        early, late = far_early[d - 1], far_late[d - 1]
        ends = (0, block_rows, block_rows + pair_rows, 2 * block_rows + pair_rows)
        shared = [far_own[d - 1], early] + [late[ends[k] : ends[k + 1]] for k in range(3)]
        far_keys, far_values = call(
            functools.partial(far_kernel, d * group_rows),
            shared + [far_rank[d - 1], meta, turns, spread_first, qkv_right],
            [shape(group_rows, HEAD_SIZE)] * 2,
            info,
        )
        keys.append(far_keys)
        values.append(far_values)

    output_left = output_adapter_left.reshape(HEAD_SIZE, adapter_columns)
    attended, rank_out = call(
        functools.partial(attention_kernel, req_count),
        [queries] + keys + values + [meta, spread_first, output_left, hidden_rank],
        [shape(group_rows, HEAD_SIZE), shape(32, group_rows)],
        info,
        [
            pltpu.VMEM((req_count * group_rows, HEAD_SIZE), jnp.bfloat16),
            pltpu.VMEM((req_count * group_rows, HEAD_SIZE), jnp.bfloat16),
            held((2 * block_rows, req_count * group_rows)),
            held((2 * block_rows, 128)),
            held((2 * block_rows, 128)),
            held((2 * block_rows, HEAD_SIZE)),
            held((32, group_rows)),
        ],
        mib=24 + 3 * req_count,
    )
    output_rows = output_weight.reshape(HEAD_SIZE, model_width)

    def main(k, attended, hidden):
        sent = block if k == 0 else pair_rows
        return call(
            functools.partial(main_kernel, k),
            [attended, hidden, output_rows, down_weight],
            [shape(block_rows - sent, model_width, jnp.float32), shape(sent, model_width)],
        )

    kept, arrived, sent = {}, {}, {}
    for bit, k in zip((1, 2, 4, 8), (0, 3, 2, 1)):
        moved = lax.ppermute(rank_out, "mlp", [(i, i ^ bit) for i in range(16)])
        kept[k], sent[k] = main(k, attended, hidden)
        rank_out, attended, kept[k], sent[k] = tie((rank_out + moved, attended, kept[k], sent[k]))
        if k == 0:
            arrived[k] = to_partner(sent[k])
        if bit == 4:
            arrived[3] = to_partner(sent[3])
            rank_out, arrived[0] = tie((rank_out, arrived[0]))
    rank_out, arrived[3] = tie((rank_out, arrived[3]))
    pair_right = jnp.concatenate([near_right, far_right], axis=0)

    def adapt(slot, half, kept, first, arrived):
        if half:
            outs = [shape(block, model_width, jnp.bfloat16 if slot else jnp.float32)]
        else:
            outs = [shape(block, model_width, jnp.float32)] * 2
        return call(
            functools.partial(adapt_kernel, slot, first),
            [rank_out, meta, spread_own, pair_right, kept, arrived],
            outs,
            info,
        )

    chain_a = along_ring(adapt(1, True, kept[0], 2 * block, arrived[0])[0])
    chain_b = None
    for s in (3, 2, 1):
        add_a, add_b = adapt(2 * s + 1, False, kept[s], 0, arrived[s])
        if s > 1:
            arrived[s - 1] = to_partner(sent[s - 1])
        if chain_b is None:
            chain_b = along_ring(narrow(add_b))
            chain_a = along_ring(narrow(wide(chain_a) + add_a))
        else:
            chain_a = along_ring(narrow(wide(chain_a) + add_a))
            chain_b = along_ring(narrow(wide(chain_b) + add_b))
    own_sum = adapt(0, True, kept[0], 0, tokens)[0]
    chain_a, own_sum = tie((chain_a, own_sum))
    arrived_last = to_partner(narrow(wide(chain_b) + kept[0][block : 2 * block]))
    return narrow(wide(chain_a) + wide(arrived_last) + own_sum + output_bias)


def solution(mesh):
    in_specs = (
        P(("req", "mlp"), None),
        P(),
        P(),
        P(None, "mlp", None),
        P("mlp", None, None),
        P(None, "mlp"),
        P("mlp"),
        P("mlp", None),
        P(),
        P(None, "mlp"),
        P(None, "mlp", None),
        P(None, "mlp"),
        P("mlp", None, None),
        P("mlp", None),
        P("mlp", None),
        P(),
        P(),
        P("mlp"),
    )
    out_specs = P(("req", "mlp"), None)
    return jax.shard_map(
        per_device, mesh=mesh, in_specs=in_specs, out_specs=out_specs, check_vma=False
    )
```

```python
import functools
import math

import jax
import jax.numpy as jnp
import numpy as np
from jax import lax
from jax.experimental import pallas as pl
from jax.experimental.pallas import tpu as pltpu
from jax.sharding import PartitionSpec as P

HEAD_SIZE = 256
ROT = 64
ADAPTER_RANK = 16
EPSILON = 1e-05
NEGATIVE_FILL = -1e30
RING = (0, 2, 4, 6, 7, 5, 3, 1)
PLACE = tuple(RING.index(pair) for pair in range(8))
CORE_PERM = [(i, i ^ 1) for i in range(16)]
RING_PERM = [(RING[i] * 2, RING[(i + 1) % 8] * 2) for i in range(8)] + [
    (RING[i] * 2 + 1, RING[(i - 1) % 8] * 2 + 1) for i in range(8)
]
SLOTS = 8
BLOCKS = 4
CORE, MLP, PAIRS, PLACES, BASES = 0, 1, 2, 2 + SLOTS, 2 + 2 * SLOTS


def to_partner(value):
    return lax.ppermute(value, "mlp", CORE_PERM)


def along_ring(value):
    return lax.ppermute(value, "mlp", RING_PERM)


def rank_product(left_side, right_side):
    return jnp.dot(left_side, right_side, preferred_element_type=jnp.float32)


def across(left_side, right_side):
    return lax.dot_general(
        left_side, right_side, (((1,), (1,)), ((), ())), preferred_element_type=jnp.float32
    )


def spread_table(period, first, width):
    row = np.arange(32)[:, None]
    column = np.arange(width)[None, :]
    return jnp.asarray((row - first == column % period).astype(np.float32), jnp.bfloat16)


def swap_halves(info, lanes):
    half = lanes.shape[1] // 2
    return jnp.where(info[CORE] == 1, pltpu.roll(lanes, half, 1), lanes)


def lane_ids(shape, period):
    return (lax.broadcasted_iota(jnp.int32, shape, 1) // period).astype(jnp.float32)


def pair_at(info, slot, rows):
    return pl.ds(pl.multiple_of(info[PAIRS + slot] * rows, rows), rows)


def store_lanes(info, out_ref, lanes, slots):
    width = out_ref.shape[1] // SLOTS
    for k, slot in enumerate(slots):
        part = lanes[:, k * width : (k + 1) * width]
        out_ref[:, pair_at(info, slot, width)] = swap_halves(info, part).astype(out_ref.dtype)


def rank_rows(info, rank_ref, slot, count):
    width = rank_ref.shape[1] // SLOTS
    lanes = [
        swap_halves(info, rank_ref[:, pair_at(info, slot + k, width)].astype(jnp.float32))
        for k in range(count)
    ]
    lanes = lanes[0] if count == 1 else jnp.concatenate(lanes, axis=1)
    return jnp.transpose(lanes).astype(jnp.bfloat16)


def widened(rows, spread_ref, adapter, columns):
    tile = rank_product(rows, spread_ref[...]).astype(jnp.bfloat16)
    group = lax.broadcasted_iota(jnp.int32, tile.shape, 1) // ADAPTER_RANK
    apart = (adapter - group.astype(jnp.float32)).astype(jnp.bfloat16)
    step = tile.shape[1] // ADAPTER_RANK
    zero = jnp.zeros_like(tile)
    return jnp.concatenate(
        [jnp.where(apart == first, tile, zero) for first in range(0, columns // ADAPTER_RANK, step)], axis=1
    )


def folded(products, adapter, spread_ref):
    width = spread_ref.shape[1]
    group = lax.broadcasted_iota(jnp.int32, (products.shape[0], width), 1) // ADAPTER_RANK
    apart = adapter - group.astype(jnp.float32)
    total = None
    for first in range(0, products.shape[1], width):
        part = products[:, first : first + width]
        part = jnp.where(apart == float(first // ADAPTER_RANK), part, 0.0)
        total = part if total is None else total + part
    return across(spread_ref[...], total.astype(jnp.bfloat16))


def cosine(angle):
    turns = jnp.floor(angle * (1.0 / math.pi) + 0.5)
    rest = ((angle - turns * 3.140625) - turns * 9.67502593994140625e-4) - turns * 1.509957990978376e-7
    square = rest * rest
    value = jnp.full_like(square, 1.0 / 479001600.0)
    for factor in (-1.0 / 3628800.0, 1.0 / 40320.0, -1.0 / 720.0, 1.0 / 24.0, -0.5, 1.0):
        value = value * square + factor
    odd = turns - 2.0 * jnp.floor(turns * 0.5)
    return value * (1.0 - 2.0 * odd)


def norm_kernel(x_hbm, gain_hbm, bias_hbm, out_ref, x_ref, gain_ref, bias_ref, sems):
    pairs = ((x_hbm, x_ref), (gain_hbm, gain_ref), (bias_hbm, bias_ref))
    copies = [pltpu.make_async_copy(a, b, sems.at[k]) for k, (a, b) in enumerate(pairs)]
    for copy in copies:
        copy.start()
    copies[0].wait()
    values = x_ref[...].astype(jnp.float32)
    center = values - jnp.mean(values, axis=1, keepdims=True)
    spread = jnp.mean(center * center, axis=1, keepdims=True)
    scaled = center * lax.rsqrt(spread + EPSILON)
    copies[1].wait()
    copies[2].wait()
    out_ref[...] = (scaled * gain_ref[...] + bias_ref[...]).astype(out_ref.dtype)


def local_tokens(info, slot, shape, dim):
    rows = shape[dim] // 2
    at = lax.broadcasted_iota(jnp.int32, shape, dim)
    second = at >= rows
    at = jnp.where(second, at - rows, at) + info[CORE] * (rows // 2)
    at = jnp.where(at >= rows, at - rows, at)
    return (at + jnp.where(second, info[BASES + slot + 1], info[BASES + slot])).astype(jnp.float32)


def token_kernel(info, column_ref, row_ref, ids_ref, table_ref, *refs):
    count = (len(refs) - 3) // 2
    meta_ref, turn_ref = refs[count : count + 2]
    pieces = 4
    copies = []
    for k, (a, b) in enumerate(zip(refs[:count], refs[count + 2 : -1])):
        depth = a.shape[0] // pieces
        for piece in range(pieces):
            at = pl.ds(piece * depth, depth)
            copies.append(pltpu.make_async_copy(a.at[at, :], b.at[at, :], refs[-1].at[k * pieces + piece]))
    for copy in copies:
        copy.start()
    rows = 2 * 128
    count = row_ref.shape[1]
    earlier = lax.broadcasted_iota(jnp.int32, (count, count), 0) < lax.broadcasted_iota(
        jnp.int32, (count, count), 1
    )
    anchors = jnp.sum(jnp.where(earlier, column_ref[...], 0.0), axis=0, keepdims=True)
    endings = anchors + row_ref[...]
    ids = ids_ref[...]
    lane = lax.broadcasted_iota(jnp.int32, (rows, 128), 1)

    def one(block, _):
        token = local_tokens(info, 2 * block, (rows, 1), 0)
        inside = jnp.logical_and(anchors <= token, token < endings)
        start = jnp.sum(jnp.where(inside, anchors, 0.0), axis=1, keepdims=True)
        adapter = jnp.sum(jnp.where(inside, ids, 0.0), axis=1, keepdims=True)
        at = pl.ds(pl.multiple_of(block * rows, rows), rows)
        meta_ref[at, :] = jnp.where(lane < 64, start, adapter)
        angle = (token - start) * table_ref[0:1, :] - table_ref[1:2, :]
        turn_ref[at, :] = cosine(angle) * table_ref[2:3, :]
        return 0

    lax.fori_loop(0, meta_ref.shape[0] // rows, one, 0)
    for copy in copies:
        copy.wait()


def rank_kernel(count, slots, info, *refs):
    x = jnp.concatenate([ref[...] for ref in refs[:count]], axis=0)
    left_ref, meta_ref, slot_ref, fold_ref, held_ref = refs[count : count + 5]
    out_ref = refs[-1]
    products = rank_product(x, left_ref[...])
    adapter = jnp.concatenate([meta_ref[k * 128 : (k + 1) * 128, 64:65] for k in slots], axis=0)
    chosen = jnp.where(slot_ref[...] == adapter, products, 0.0).astype(jnp.bfloat16)
    out_ref[...] = held_ref[...]
    store_lanes(info, out_ref, across(fold_ref[...], chosen), slots)


def base_kernel(count, *refs):
    x = jnp.concatenate([ref[...] for ref in refs[:count]], axis=0)
    qkv_ref, up_ref, base_ref, up_base_ref, shared_ref = refs[count:]
    first = rank_product(x, qkv_ref[...])
    base_ref[...] = first
    shared_ref[...] = first[:, HEAD_SIZE:].astype(shared_ref.dtype)
    up_base_ref[...] = rank_product(x, up_ref[...])


def turn(part, table):
    width = table.shape[1]
    lane = lax.broadcasted_iota(jnp.int32, table.shape, 1)
    cos = jnp.where(lane < ROT, table, 1.0)
    sin = jnp.where(lane < ROT, pltpu.roll(table, width - ROT, 1), 0.0)
    head = part[:, :width]
    swapped = jnp.where(
        lane % 2 == 0, pltpu.roll(head, width - 1, 1), pltpu.roll(head, 1, 1)
    )
    return jnp.concatenate([head * cos + swapped * sin, part[:, width:]], axis=1)


def block_rows_of(refs, block):
    if block == 0:
        return jnp.concatenate([refs[0][...], refs[4][128:]], axis=0)
    if block == 3:
        return jnp.concatenate([refs[3][...], refs[4][:128]], axis=0)
    return refs[block][...]


def four_blocks(refs, index):
    return jnp.concatenate([block_rows_of(refs, 4 * index + k) for k in range(4)], axis=0)


def inner_kernel(info, *refs):
    base_refs, up_refs, (rank_ref, meta_ref, turn_ref, first_ref, last_ref) = refs[:5], refs[5:10], refs[10:15]
    qkv_right_ref, up_right_ref, bias_ref, left_ref = refs[15:19]
    q_ref, k_ref, v_ref, hidden_ref, out_ref = refs[19:]
    rows = 1024
    columns = qkv_right_ref.shape[0]
    for block in range(BLOCKS // 4):
        at = slice(block * rows, (block + 1) * rows)
        adapter = meta_ref[at, 64:65]
        ranks = rank_rows(info, rank_ref, 8 * block, 8)
        total = four_blocks(base_refs, block) + rank_product(
            widened(ranks, first_ref, adapter, columns), qkv_right_ref[...]
        )
        table = turn_ref[at, :]
        q_ref[at, :] = (turn(total[:, :HEAD_SIZE], table) * HEAD_SIZE ** (-0.5)).astype(jnp.bfloat16)
        k_ref[at, :] = turn(total[:, HEAD_SIZE : 2 * HEAD_SIZE], table).astype(jnp.bfloat16)
        v_ref[at, :] = total[:, 2 * HEAD_SIZE :].astype(jnp.bfloat16)
        wide = widened(ranks, last_ref, adapter, columns)
        x = four_blocks(up_refs, block) + rank_product(wide, up_right_ref[...]) + bias_ref[...]
        inner = math.sqrt(2.0 / math.pi) * (x + 0.044715 * (x * x * x))
        hidden = (0.5 * x * (1.0 + jnp.tanh(inner))).astype(jnp.bfloat16)
        hidden_ref[at, :] = hidden
        lanes = folded(rank_product(hidden, left_ref[...]), adapter, last_ref)
        store_lanes(info, out_ref, lanes, range(8 * block, 8 * block + 8))


def far_kernel(first_row, info, *refs):
    shared_refs, (rank_ref, meta_ref, turn_ref, spread_ref, right_ref, k_ref, v_ref) = refs[:5], refs[5:]
    rows = 1024
    for block in range(BLOCKS // 4):
        at = slice(block * rows, (block + 1) * rows)
        far_at = slice(first_row + block * rows, first_row + (block + 1) * rows)
        ranks = rank_rows(info, rank_ref, 8 * block, 8)
        wide = widened(ranks, spread_ref, meta_ref[far_at, 64:65], right_ref.shape[0])
        total = four_blocks(shared_refs, block).astype(jnp.float32)
        total = total + rank_product(wide, right_ref[:, HEAD_SIZE:])
        k_ref[at, :] = turn(total[:, :HEAD_SIZE], turn_ref[far_at, :]).astype(jnp.bfloat16)
        v_ref[at, :] = total[:, HEAD_SIZE:].astype(jnp.bfloat16)


def attention_kernel(req_count, info, *refs):
    q_ref, refs = refs[0], refs[1:]
    key_refs, value_refs, refs = refs[:req_count], refs[req_count : 2 * req_count], refs[2 * req_count :]
    meta_ref, spread_ref, left_ref, hidden_rank_ref, attended_ref, out_ref = refs[:6]
    keys_ref, values_ref, scores_ref, top_ref, sum_ref, acc_ref, fold_ref = refs[6:]
    span = rows = 512
    pair = 128
    group_rows = q_ref.shape[0]

    def lane_parts(value):
        return [value[:, k * pair : (k + 1) * pair] for k in range(span // pair)]

    def slot_rows(slot):
        return pl.ds(pl.multiple_of(slot * pair, pair), pair)

    for d in range(req_count):
        for k in range(SLOTS):
            at = slice((req_count - 1 - d) * group_rows + k * pair, (req_count - 1 - d) * group_rows + (k + 1) * pair)
            slot = slot_rows(info[PLACES + k])
            keys_ref[at, :] = key_refs[d][slot, :]
            values_ref[at, :] = value_refs[d][slot, :]
    first_token = info[BASES + info[PLACES]] - (req_count - 1) * group_rows

    def places(shape, dim):
        at = lax.broadcasted_iota(jnp.int32, shape, dim)
        before = at // pair * pair
        at = at - before + info[CORE] * (pair // 2)
        return (before + jnp.where(at >= pair, at - pair, at)).astype(jnp.float32)

    key_place = places((1, span), 1)
    query_place = places((rows, 1), 0)

    def one(block, _):
        slots = [slot_rows(info[PLACES + 4 * block + k]) for k in range(4)]

        def both(ref):
            return jnp.concatenate([ref[at, :] for at in slots], axis=0)

        meta = both(meta_ref)
        start = meta[:, 0:1]
        number = (req_count - 1) * (group_rows // span) + block
        query = query_place + (first_token + number * span).astype(jnp.float32)
        q = both(q_ref)
        lowest = jnp.min(start).astype(jnp.int32) - first_token
        top_ref[...] = jnp.full_like(top_ref, NEGATIVE_FILL)
        sum_ref[...] = jnp.zeros_like(sum_ref)
        acc_ref[...] = jnp.zeros_like(acc_ref)

        def score(j, _):
            at = pl.ds(pl.multiple_of(j * span, span), span)
            scores = across(q, keys_ref[at, :])
            key = key_place + (first_token + j * span).astype(jnp.float32)
            allowed = jnp.logical_and(key <= query, key >= start)
            scores = jnp.where(allowed, scores, NEGATIVE_FILL)
            scores_ref[:, at] = scores
            top_ref[...] = functools.reduce(jnp.maximum, lane_parts(scores), top_ref[...])
            return 0

        lax.fori_loop(lowest // span, number + 1, score, 0)
        top = jnp.max(top_ref[...], axis=1, keepdims=True)

        def weigh(j, _):
            at = pl.ds(pl.multiple_of(j * span, span), span)
            weights = jnp.exp(scores_ref[:, at] - top)
            sum_ref[...] = functools.reduce(jnp.add, lane_parts(weights), sum_ref[...])
            acc_ref[...] = acc_ref[...] + rank_product(weights.astype(jnp.bfloat16), values_ref[at, :])
            return 0

        lax.fori_loop(lowest // span, number + 1, weigh, 0)
        total = jnp.sum(sum_ref[...], axis=1, keepdims=True)
        attended = (acc_ref[...] / total).astype(jnp.bfloat16)
        lanes = folded(rank_product(attended, left_ref[...]), meta[:, 64:65], spread_ref)
        for k in range(4):
            attended_ref[slots[k], :] = attended[k * pair : (k + 1) * pair]
            at = pl.ds(pl.multiple_of((4 * block + k) * pair, pair), pair)
            fold_ref[:, at] = swap_halves(info, lanes[:, k * pair : (k + 1) * pair])
        return 0

    lax.fori_loop(0, BLOCKS // 2, one, 0)
    out_ref[...] = (fold_ref[...] + hidden_rank_ref[...].astype(jnp.float32)).astype(out_ref.dtype)


def main_kernel(block, attended_ref, hidden_ref, output_ref, down_ref, kept_ref, sent_ref):
    rows = 256
    sent = sent_ref.shape[0]
    width = 512
    attended = attended_ref[block * rows : (block + 1) * rows, :]
    hidden = hidden_ref[block * rows : (block + 1) * rows, :]

    for step in range(output_ref.shape[1] // width):
        at = slice(step * width, (step + 1) * width)
        total = rank_product(attended, output_ref[:, at]) + rank_product(hidden, down_ref[:, at])
        if block:
            sent_ref[:, at] = total[:sent].astype(sent_ref.dtype)
            kept_ref[:, at] = total[sent:]
        else:
            kept_ref[:, at] = total[: rows - sent]
            sent_ref[:, at] = total[rows - sent :].astype(sent_ref.dtype)


def adapt_kernel(slot, first, info, rank_ref, meta_ref, spread_ref, right_ref, kept_ref, arrived_ref, *out_refs):
    pair = 128
    half = pair // 2
    columns = spread_ref.shape[1]
    count = columns // (4 * ADAPTER_RANK)
    column_id = lax.broadcasted_iota(jnp.int32, (pair, columns), 1) // (2 * ADAPTER_RANK)
    partner = info[MLP] + 1 - 2 * info[CORE]
    column_id = column_id + jnp.where(column_id < count, info[MLP] * count, (partner - 1) * count)
    own = column_id.astype(jnp.float32) == meta_ref[slot * pair : (slot + 1) * pair, 64:65]
    spread = rank_product(rank_rows(info, rank_ref, slot, 1), spread_ref[...])
    wide = jnp.where(own, spread, 0.0).astype(jnp.bfloat16)
    width = 512

    for step in range(right_ref.shape[1] // width):
        at = slice(step * width, (step + 1) * width)
        if len(out_refs) == 1:
            total = rank_product(wide[:half], right_ref[:, at]) + kept_ref[first : first + half, at]
            total = total + arrived_ref[:, at].astype(jnp.float32)
            out_refs[0][:, at] = total.astype(out_refs[0].dtype)
        else:
            total = rank_product(wide, right_ref[:, at]) + kept_ref[:, at]
            out_refs[0][:, at] = total[:half] + arrived_ref[half:, at].astype(jnp.float32)
            out_refs[1][:, at] = total[half:] + arrived_ref[:half, at].astype(jnp.float32)


def call(kernel, operands, outs, info=None, scratch=(), mib=24, flops=1000, space=pltpu.VMEM, in_hbm=0):
    vmem = pl.BlockSpec(memory_space=pltpu.VMEM)
    specs = [pl.BlockSpec(memory_space=space)] * (len(operands) - in_hbm)
    specs += [pl.BlockSpec(memory_space=pltpu.HBM)] * in_hbm
    if info is not None:
        operands, specs = [info] + operands, [pl.BlockSpec(memory_space=pltpu.SMEM)] + specs
    return pl.pallas_call(
        kernel,
        in_specs=specs,
        out_specs=[vmem] * len(outs),
        out_shape=outs,
        scratch_shapes=scratch,
        compiler_params=pltpu.CompilerParams(vmem_limit_bytes=mib * 1024 * 1024),
        cost_estimate=pl.CostEstimate(flops=flops, bytes_accessed=1000, transcendentals=0),
    )(*operands)


def shape(rows, width, dtype=jnp.bfloat16):
    return jax.ShapeDtypeStruct((rows, width), dtype)


def sum_over_mlp(value, bits):
    for bit in bits:
        value = value + lax.ppermute(value, "mlp", [(i, i ^ bit) for i in range(16)])
    return value


def narrow(value):
    return value.astype(jnp.bfloat16)


def wide(value):
    return value.astype(jnp.float32)


def per_device(
    tokens,
    layer_norm_gain,
    layer_norm_bias,
    query_key_weight,
    output_weight,
    up_weight,
    input_bias,
    down_weight,
    output_bias,
    input_adapter_left,
    query_key_value_right,
    up_adapter_right,
    output_adapter_left,
    down_adapter_left,
    output_adapter_right,
    lengths,
    request_adapter,
    slot_adapter,
):
    block = tokens.shape[0]
    model_width = tokens.shape[1]
    pair_rows = 2 * block
    group_rows = SLOTS * pair_rows
    req_count = lax.axis_size("req")
    group = lax.axis_index("req")
    me = lax.axis_index("mlp")
    block_rows = 2 * pair_rows
    table = np.zeros((req_count, 16, 2 + SLOTS * (2 + req_count)), np.int32)
    for g in range(req_count):
        for m in range(16):
            side = 2 * (m % 2) - 1
            steps = [0, 4] + [t for s in (1, 2, 3) for t in (side * s, -side * s)]
            pairs = [RING[(PLACE[m // 2] + t) % 8] for t in steps]
            firsts = [(g - d) * group_rows + p * pair_rows for d in range(req_count) for p in pairs]
            table[g, m] = [m % 2, m] + pairs + [pairs.index(p) for p in range(SLOTS)] + firsts
    info = lax.dynamic_slice(jnp.asarray(table), (group, me, 0), (1, 1, table.shape[2])).reshape(-1)

    norm_args = [tokens, layer_norm_gain.reshape(1, -1), layer_norm_bias.reshape(1, -1)]
    norm_args = [pltpu.with_memory_space_constraint(x, pltpu.HBM) for x in norm_args]
    own = call(
        norm_kernel,
        norm_args,
        [shape(block, model_width)],
        scratch=[pltpu.VMEM(x.shape, x.dtype) for x in norm_args] + [pltpu.SemaphoreType.DMA((3,))],
        space=pltpu.HBM,
    )[0]
    other = to_partner(own)
    ring_a, ring_b = along_ring(own), along_ring(other)
    near_left, far_left = input_adapter_left, to_partner(input_adapter_left)

    float_lengths = wide(lengths)
    lane = np.arange(128)
    turn_rows = np.zeros((8, 128), np.float32)
    turn_rows[0] = np.exp(lane % ROT // 2 * (-2.0 * math.log(10000.0) / ROT))
    turn_rows[1] = np.where(lane < ROT, 0.0, math.pi / 2)
    turn_rows[2] = np.where(lane < ROT, 1.0, np.where(lane % 2 == 0, -1.0, 1.0))
    token_rows = req_count * group_rows
    token_args = [
        float_lengths[:, None],
        float_lengths[None, :],
        wide(request_adapter)[None, :],
        jnp.asarray(turn_rows),
    ]
    weights = [query_key_weight.reshape(model_width, 3 * HEAD_SIZE), up_weight]
    weights = [pltpu.with_memory_space_constraint(x, pltpu.HBM) for x in weights]
    meta, turns, qkv_rows, up_rows = call(
        token_kernel,
        token_args + weights,
        [shape(token_rows, 128, jnp.float32)] * 2 + [shape(*x.shape) for x in weights],
        info,
        [pltpu.SemaphoreType.DMA((8,))],
        in_hbm=2,
    )

    adapter_columns = query_key_value_right.shape[0]
    qkv_right = query_key_value_right.reshape(adapter_columns, 3 * HEAD_SIZE)
    spread_first = spread_table(ADAPTER_RANK, 0, 128)
    spread_last = spread_table(ADAPTER_RANK, ADAPTER_RANK, 128)
    near_right = output_adapter_right
    slot_columns = wide(jnp.repeat(slot_adapter, 2 * ADAPTER_RANK))[None, :]
    slot_columns = jnp.concatenate([slot_columns, to_partner(slot_columns)], axis=1)
    own_columns = near_right.shape[0]
    spread_own = spread_table(2 * ADAPTER_RANK, 0, 2 * own_columns)
    hidden_width = up_weight.shape[1]

    def to_group(value, d):
        return lax.ppermute(value, "req", [(g, g + d) for g in range(req_count - d)])

    held = functools.partial(pltpu.VMEM, dtype=jnp.float32)

    def add_ranks(part, slots, so_far):
        return call(
            functools.partial(rank_kernel, len(part), slots),
            list(part) + [pair_left, meta, slot_columns, spread_own, so_far],
            [shape(32, group_rows)],
            info,
        )[0]

    def products_of(part, flops=1000):
        rows = len(part) * block
        return call(
            functools.partial(base_kernel, len(part)),
            list(part) + [qkv_rows, up_rows],
            [
                shape(rows, 3 * HEAD_SIZE, jnp.float32),
                shape(rows, hidden_width, jnp.float32),
                shape(rows, 2 * HEAD_SIZE),
            ],
            flops=flops,
        )

    def to_groups(value):
        return [to_group(value, d) for d in range(1, req_count)]

    def arrivals(a, b):
        return a, b, to_partner(b), to_partner(a)

    tie = lax.optimization_barrier
    own_part = (own, other)
    ring_a, meta, turns, qkv_rows, up_rows = tie((ring_a, meta, turns, qkv_rows, up_rows))
    ring_b, near_left, far_left = tie((ring_b, near_left, far_left))
    pair_left = jnp.concatenate([near_left, far_left], axis=1)
    part = arrivals(ring_a, ring_b)
    ring_a, ring_b = along_ring(ring_a), along_ring(ring_b)
    ranks = add_ranks(own_part + part, (0, 2, 3), jnp.zeros((32, group_rows), jnp.bfloat16))
    zeroth = products_of(own_part)
    ring_a, zeroth = tie((ring_a, zeroth))
    far_own = to_groups(zeroth[2])
    first = products_of(part)
    ring_b, ranks, first, far_own = tie((ring_b, ranks, first, far_own))
    part = arrivals(ring_a, ring_b)
    ring_a, ring_b = along_ring(ring_a), along_ring(ring_b)
    far_right = to_partner(near_right)
    far_early = to_groups(first[2])
    ranks = add_ranks(part, (4, 5), ranks)
    second = products_of(part)
    ring_b, ranks, second, far_right = tie((ring_b, ranks, second, far_right))
    part = arrivals(ring_a, ring_b)
    ring_a = along_ring(ring_a)
    held_rows = part[:2]
    third = products_of(held_rows, 2000000000)
    ranks = add_ranks(held_rows, (6,), ranks)
    ring_a, ranks, third, far_early = tie((ring_a, ranks, third, far_early))
    part = part[2:] + (ring_a, to_partner(ring_a))
    ranks = add_ranks(part, (7, 1), ranks)
    moved = lax.ppermute(ranks, "mlp", [(i, i ^ 2) for i in range(16)])
    fourth = products_of(part)
    ranks, fourth = tie((ranks + moved, fourth))
    far_late = to_groups(jnp.concatenate([second[2], third[2], fourth[2]], axis=0))
    rank_in = sum_over_mlp(ranks, (4, 8))
    products = (zeroth, first, second, third, fourth)

    bias_row = input_bias.reshape(1, -1)
    far_rank = to_groups(rank_in)
    queries, own_keys, own_values, hidden, hidden_rank = call(
        inner_kernel,
        [part[0] for part in products]
        + [part[1] for part in products]
        + [rank_in, meta, turns, spread_first, spread_last]
        + [qkv_right, up_adapter_right, bias_row, down_adapter_left],
        [shape(group_rows, HEAD_SIZE)] * 3 + [shape(group_rows, hidden_width), shape(32, group_rows)],
        info,
    )
    keys, values = [own_keys], [own_values]
    for d in range(1, req_count):
        early, late = far_early[d - 1], far_late[d - 1]
        ends = (0, block_rows, block_rows + pair_rows, 2 * block_rows + pair_rows)
        shared = [far_own[d - 1], early] + [late[ends[k] : ends[k + 1]] for k in range(3)]
        far_keys, far_values = call(
            functools.partial(far_kernel, d * group_rows),
            shared + [far_rank[d - 1], meta, turns, spread_first, qkv_right],
            [shape(group_rows, HEAD_SIZE)] * 2,
            info,
        )
        keys.append(far_keys)
        values.append(far_values)

    output_left = output_adapter_left.reshape(HEAD_SIZE, adapter_columns)
    attended, rank_out = call(
        functools.partial(attention_kernel, req_count),
        [queries] + keys + values + [meta, spread_first, output_left, hidden_rank],
        [shape(group_rows, HEAD_SIZE), shape(32, group_rows)],
        info,
        [
            pltpu.VMEM((req_count * group_rows, HEAD_SIZE), jnp.bfloat16),
            pltpu.VMEM((req_count * group_rows, HEAD_SIZE), jnp.bfloat16),
            held((2 * block_rows, req_count * group_rows)),
            held((2 * block_rows, 128)),
            held((2 * block_rows, 128)),
            held((2 * block_rows, HEAD_SIZE)),
            held((32, group_rows)),
        ],
        mib=24 + 3 * req_count,
    )
    output_rows = output_weight.reshape(HEAD_SIZE, model_width)

    def main(k, attended, hidden):
        sent = block if k == 0 else pair_rows
        return call(
            functools.partial(main_kernel, k),
            [attended, hidden, output_rows, down_weight],
            [shape(block_rows - sent, model_width, jnp.float32), shape(sent, model_width)],
        )

    kept, arrived, sent = {}, {}, {}
    for bit, k in zip((1, 2, 4, 8), (0, 3, 2, 1)):
        moved = lax.ppermute(rank_out, "mlp", [(i, i ^ bit) for i in range(16)])
        kept[k], sent[k] = main(k, attended, hidden)
        rank_out, attended, kept[k], sent[k] = tie((rank_out + moved, attended, kept[k], sent[k]))
        if k == 0:
            arrived[k] = to_partner(sent[k])
        if bit == 4:
            arrived[3] = to_partner(sent[3])
            rank_out, arrived[0] = tie((rank_out, arrived[0]))
    rank_out, arrived[3] = tie((rank_out, arrived[3]))
    pair_right = jnp.concatenate([near_right, far_right], axis=0)

    def adapt(slot, half, kept, first, arrived):
        if half:
            outs = [shape(block, model_width, jnp.bfloat16 if slot else jnp.float32)]
        else:
            outs = [shape(block, model_width, jnp.float32)] * 2
        return call(
            functools.partial(adapt_kernel, slot, first),
            [rank_out, meta, spread_own, pair_right, kept, arrived],
            outs,
            info,
        )

    chain_a = along_ring(adapt(1, True, kept[0], 2 * block, arrived[0])[0])
    chain_b = None
    for s in (3, 2, 1):
        add_a, add_b = adapt(2 * s + 1, False, kept[s], 0, arrived[s])
        if s > 1:
            arrived[s - 1] = to_partner(sent[s - 1])
        if chain_b is None:
            chain_b = along_ring(narrow(add_b))
            chain_a = along_ring(narrow(wide(chain_a) + add_a))
        else:
            chain_a = along_ring(narrow(wide(chain_a) + add_a))
            chain_b = along_ring(narrow(wide(chain_b) + add_b))
    own_sum = adapt(0, True, kept[0], 0, tokens)[0]
    chain_a, own_sum = tie((chain_a, own_sum))
    arrived_last = to_partner(narrow(wide(chain_b) + kept[0][block : 2 * block]))
    return narrow(wide(chain_a) + wide(arrived_last) + own_sum + output_bias)


def solution(mesh):
    in_specs = (
        P(("req", "mlp"), None),
        P(),
        P(),
        P(None, "mlp", None),
        P("mlp", None, None),
        P(None, "mlp"),
        P("mlp"),
        P("mlp", None),
        P(),
        P(None, "mlp"),
        P(None, "mlp", None),
        P(None, "mlp"),
        P("mlp", None, None),
        P("mlp", None),
        P("mlp", None),
        P(),
        P(),
        P("mlp"),
    )
    out_specs = P(("req", "mlp"), None)
    return jax.shard_map(
        per_device, mesh=mesh, in_specs=in_specs, out_specs=out_specs, check_vma=False
    )
```

```python
import functools
import math

import jax
import jax.numpy as jnp
import numpy as np
from jax import lax
from jax.experimental import pallas as pl
from jax.experimental.pallas import tpu as pltpu
from jax.sharding import PartitionSpec as P

HEAD_SIZE = 256
ROT = 64
ADAPTER_RANK = 16
EPSILON = 1e-05
NEGATIVE_FILL = -1e30
RING = (0, 2, 4, 6, 7, 5, 3, 1)
PLACE = tuple(RING.index(pair) for pair in range(8))
CORE_PERM = [(i, i ^ 1) for i in range(16)]
RING_PERM = [(RING[i] * 2, RING[(i + 1) % 8] * 2) for i in range(8)] + [
    (RING[i] * 2 + 1, RING[(i - 1) % 8] * 2 + 1) for i in range(8)
]
SLOTS = 8
BLOCKS = 4
CORE, MLP, PAIRS, PLACES, BASES = 0, 1, 2, 2 + SLOTS, 2 + 2 * SLOTS


def to_partner(value):
    return lax.ppermute(value, "mlp", CORE_PERM)


def along_ring(value):
    return lax.ppermute(value, "mlp", RING_PERM)


def rank_product(left_side, right_side):
    return jnp.dot(left_side, right_side, preferred_element_type=jnp.float32)


def across(left_side, right_side):
    return lax.dot_general(
        left_side, right_side, (((1,), (1,)), ((), ())), preferred_element_type=jnp.float32
    )


def spread_table(period, first, width):
    row = np.arange(32)[:, None]
    column = np.arange(width)[None, :]
    return jnp.asarray((row - first == column % period).astype(np.float32), jnp.bfloat16)


def swap_halves(info, lanes):
    half = lanes.shape[1] // 2
    return jnp.where(info[CORE] == 1, pltpu.roll(lanes, half, 1), lanes)


def lane_ids(shape, period):
    return (lax.broadcasted_iota(jnp.int32, shape, 1) // period).astype(jnp.float32)


def pair_at(info, slot, rows):
    return pl.ds(pl.multiple_of(info[PAIRS + slot] * rows, rows), rows)


def store_lanes(info, out_ref, lanes, slots):
    width = out_ref.shape[1] // SLOTS
    for k, slot in enumerate(slots):
        part = lanes[:, k * width : (k + 1) * width]
        out_ref[:, pair_at(info, slot, width)] = swap_halves(info, part).astype(out_ref.dtype)


def rank_rows(info, rank_ref, slot, count):
    width = rank_ref.shape[1] // SLOTS
    lanes = [
        swap_halves(info, rank_ref[:, pair_at(info, slot + k, width)].astype(jnp.float32))
        for k in range(count)
    ]
    lanes = lanes[0] if count == 1 else jnp.concatenate(lanes, axis=1)
    return jnp.transpose(lanes).astype(jnp.bfloat16)


def widened(rows, spread_ref, adapter, columns):
    tile = rank_product(rows, spread_ref[...]).astype(jnp.bfloat16)
    group = lax.broadcasted_iota(jnp.int32, tile.shape, 1) // ADAPTER_RANK
    apart = (adapter - group.astype(jnp.float32)).astype(jnp.bfloat16)
    step = tile.shape[1] // ADAPTER_RANK
    zero = jnp.zeros_like(tile)
    return jnp.concatenate(
        [jnp.where(apart == first, tile, zero) for first in range(0, columns // ADAPTER_RANK, step)], axis=1
    )


def folded(products, adapter, spread_ref):
    width = spread_ref.shape[1]
    group = lax.broadcasted_iota(jnp.int32, (products.shape[0], width), 1) // ADAPTER_RANK
    apart = adapter - group.astype(jnp.float32)
    total = None
    for first in range(0, products.shape[1], width):
        part = products[:, first : first + width]
        part = jnp.where(apart == float(first // ADAPTER_RANK), part, 0.0)
        total = part if total is None else total + part
    return across(spread_ref[...], total.astype(jnp.bfloat16))


def cosine(angle):
    turns = jnp.floor(angle * (1.0 / math.pi) + 0.5)
    rest = ((angle - turns * 3.140625) - turns * 9.67502593994140625e-4) - turns * 1.509957990978376e-7
    square = rest * rest
    value = jnp.full_like(square, 1.0 / 479001600.0)
    for factor in (-1.0 / 3628800.0, 1.0 / 40320.0, -1.0 / 720.0, 1.0 / 24.0, -0.5, 1.0):
        value = value * square + factor
    odd = turns - 2.0 * jnp.floor(turns * 0.5)
    return value * (1.0 - 2.0 * odd)


def norm_kernel(x_hbm, gain_hbm, bias_hbm, out_ref, x_ref, gain_ref, bias_ref, sems):
    pairs = ((x_hbm, x_ref), (gain_hbm, gain_ref), (bias_hbm, bias_ref))
    copies = [pltpu.make_async_copy(a, b, sems.at[k]) for k, (a, b) in enumerate(pairs)]
    for copy in copies:
        copy.start()
    copies[0].wait()
    values = x_ref[...].astype(jnp.float32)
    center = values - jnp.mean(values, axis=1, keepdims=True)
    spread = jnp.mean(center * center, axis=1, keepdims=True)
    scaled = center * lax.rsqrt(spread + EPSILON)
    copies[1].wait()
    copies[2].wait()
    out_ref[...] = (scaled * gain_ref[...] + bias_ref[...]).astype(out_ref.dtype)


def local_tokens(info, slot, shape, dim):
    rows = shape[dim] // 2
    at = lax.broadcasted_iota(jnp.int32, shape, dim)
    second = at >= rows
    at = jnp.where(second, at - rows, at) + info[CORE] * (rows // 2)
    at = jnp.where(at >= rows, at - rows, at)
    return (at + jnp.where(second, info[BASES + slot + 1], info[BASES + slot])).astype(jnp.float32)


def token_kernel(info, column_ref, row_ref, ids_ref, table_ref, *refs):
    count = (len(refs) - 3) // 2
    meta_ref, turn_ref = refs[count : count + 2]
    pieces = 4
    copies = []
    for k, (a, b) in enumerate(zip(refs[:count], refs[count + 2 : -1])):
        depth = a.shape[0] // pieces
        for piece in range(pieces):
            at = pl.ds(piece * depth, depth)
            copies.append(pltpu.make_async_copy(a.at[at, :], b.at[at, :], refs[-1].at[k * pieces + piece]))
    for copy in copies:
        copy.start()
    rows = 2 * 128
    count = row_ref.shape[1]
    earlier = lax.broadcasted_iota(jnp.int32, (count, count), 0) < lax.broadcasted_iota(
        jnp.int32, (count, count), 1
    )
    anchors = jnp.sum(jnp.where(earlier, column_ref[...], 0.0), axis=0, keepdims=True)
    endings = anchors + row_ref[...]
    ids = ids_ref[...]
    lane = lax.broadcasted_iota(jnp.int32, (rows, 128), 1)

    def one(block, _):
        token = local_tokens(info, 2 * block, (rows, 1), 0)
        inside = jnp.logical_and(anchors <= token, token < endings)
        start = jnp.sum(jnp.where(inside, anchors, 0.0), axis=1, keepdims=True)
        adapter = jnp.sum(jnp.where(inside, ids, 0.0), axis=1, keepdims=True)
        at = pl.ds(pl.multiple_of(block * rows, rows), rows)
        meta_ref[at, :] = jnp.where(lane < 64, start, adapter)
        angle = (token - start) * table_ref[0:1, :] - table_ref[1:2, :]
        turn_ref[at, :] = cosine(angle) * table_ref[2:3, :]
        return 0

    lax.fori_loop(0, meta_ref.shape[0] // rows, one, 0)
    for copy in copies:
        copy.wait()


def rank_kernel(count, slots, info, *refs):
    x = jnp.concatenate([ref[...] for ref in refs[:count]], axis=0)
    left_ref, meta_ref, slot_ref, fold_ref, held_ref = refs[count : count + 5]
    out_ref = refs[-1]
    products = rank_product(x, left_ref[...])
    adapter = jnp.concatenate([meta_ref[k * 128 : (k + 1) * 128, 64:65] for k in slots], axis=0)
    chosen = jnp.where(slot_ref[...] == adapter, products, 0.0).astype(jnp.bfloat16)
    out_ref[...] = held_ref[...]
    store_lanes(info, out_ref, across(fold_ref[...], chosen), slots)


def base_kernel(count, *refs):
    x = jnp.concatenate([ref[...] for ref in refs[:count]], axis=0)
    qkv_ref, up_ref, base_ref, up_base_ref, shared_ref = refs[count:]
    first = rank_product(x, qkv_ref[...])
    base_ref[...] = first
    shared_ref[...] = first[:, HEAD_SIZE:].astype(shared_ref.dtype)
    up_base_ref[...] = rank_product(x, up_ref[...])


def turn(part, table):
    width = table.shape[1]
    lane = lax.broadcasted_iota(jnp.int32, table.shape, 1)
    cos = jnp.where(lane < ROT, table, 1.0)
    sin = jnp.where(lane < ROT, pltpu.roll(table, width - ROT, 1), 0.0)
    head = part[:, :width]
    swapped = jnp.where(
        lane % 2 == 0, pltpu.roll(head, width - 1, 1), pltpu.roll(head, 1, 1)
    )
    return jnp.concatenate([head * cos + swapped * sin, part[:, width:]], axis=1)


def block_rows_of(refs, block):
    if block == 0:
        return jnp.concatenate([refs[0][...], refs[5][...]], axis=0)
    if block == 3:
        return jnp.concatenate([refs[3][...], refs[4][...]], axis=0)
    return refs[block][...]


def four_blocks(refs, index):
    return jnp.concatenate([block_rows_of(refs, 4 * index + k) for k in range(4)], axis=0)


def inner_kernel(info, *refs):
    base_refs, up_refs, (rank_ref, meta_ref, turn_ref, first_ref, last_ref) = refs[:6], refs[6:12], refs[12:17]
    qkv_right_ref, up_right_ref, bias_ref, left_ref = refs[17:21]
    q_ref, k_ref, v_ref, hidden_ref, out_ref = refs[21:]
    rows = 1024
    columns = qkv_right_ref.shape[0]
    for block in range(BLOCKS // 4):
        at = slice(block * rows, (block + 1) * rows)
        adapter = meta_ref[at, 64:65]
        ranks = rank_rows(info, rank_ref, 8 * block, 8)
        total = four_blocks(base_refs, block) + rank_product(
            widened(ranks, first_ref, adapter, columns), qkv_right_ref[...]
        )
        table = turn_ref[at, :]
        q_ref[at, :] = (turn(total[:, :HEAD_SIZE], table) * HEAD_SIZE ** (-0.5)).astype(jnp.bfloat16)
        k_ref[at, :] = turn(total[:, HEAD_SIZE : 2 * HEAD_SIZE], table).astype(jnp.bfloat16)
        v_ref[at, :] = total[:, 2 * HEAD_SIZE :].astype(jnp.bfloat16)
        wide = widened(ranks, last_ref, adapter, columns)
        x = four_blocks(up_refs, block) + rank_product(wide, up_right_ref[...]) + bias_ref[...]
        inner = math.sqrt(2.0 / math.pi) * (x + 0.044715 * (x * x * x))
        hidden = (0.5 * x * (1.0 + jnp.tanh(inner))).astype(jnp.bfloat16)
        hidden_ref[at, :] = hidden
        lanes = folded(rank_product(hidden, left_ref[...]), adapter, last_ref)
        store_lanes(info, out_ref, lanes, range(8 * block, 8 * block + 8))


def far_kernel(first_row, info, *refs):
    shared_refs, (rank_ref, meta_ref, turn_ref, spread_ref, right_ref, k_ref, v_ref) = refs[:6], refs[6:]
    rows = 1024
    for block in range(BLOCKS // 4):
        at = slice(block * rows, (block + 1) * rows)
        far_at = slice(first_row + block * rows, first_row + (block + 1) * rows)
        ranks = rank_rows(info, rank_ref, 8 * block, 8)
        wide = widened(ranks, spread_ref, meta_ref[far_at, 64:65], right_ref.shape[0])
        total = four_blocks(shared_refs, block).astype(jnp.float32)
        total = total + rank_product(wide, right_ref[:, HEAD_SIZE:])
        k_ref[at, :] = turn(total[:, :HEAD_SIZE], turn_ref[far_at, :]).astype(jnp.bfloat16)
        v_ref[at, :] = total[:, HEAD_SIZE:].astype(jnp.bfloat16)


def attention_kernel(req_count, info, *refs):
    q_ref, refs = refs[0], refs[1:]
    key_refs, value_refs, refs = refs[:req_count], refs[req_count : 2 * req_count], refs[2 * req_count :]
    meta_ref, spread_ref, left_ref, hidden_rank_ref, attended_ref, out_ref = refs[:6]
    keys_ref, values_ref, scores_ref, top_ref, sum_ref, acc_ref, fold_ref = refs[6:]
    span = rows = 512
    pair = 128
    group_rows = q_ref.shape[0]

    def lane_parts(value):
        return [value[:, k * pair : (k + 1) * pair] for k in range(span // pair)]

    def slot_rows(slot):
        return pl.ds(pl.multiple_of(slot * pair, pair), pair)

    for d in range(req_count):
        for k in range(SLOTS):
            at = slice((req_count - 1 - d) * group_rows + k * pair, (req_count - 1 - d) * group_rows + (k + 1) * pair)
            slot = slot_rows(info[PLACES + k])
            keys_ref[at, :] = key_refs[d][slot, :]
            values_ref[at, :] = value_refs[d][slot, :]
    first_token = info[BASES + info[PLACES]] - (req_count - 1) * group_rows

    def places(shape, dim):
        at = lax.broadcasted_iota(jnp.int32, shape, dim)
        before = at // pair * pair
        at = at - before + info[CORE] * (pair // 2)
        return (before + jnp.where(at >= pair, at - pair, at)).astype(jnp.float32)

    key_place = places((1, span), 1)
    query_place = places((rows, 1), 0)

    def one(block, _):
        slots = [slot_rows(info[PLACES + 4 * block + k]) for k in range(4)]

        def both(ref):
            return jnp.concatenate([ref[at, :] for at in slots], axis=0)

        meta = both(meta_ref)
        start = meta[:, 0:1]
        number = (req_count - 1) * (group_rows // span) + block
        query = query_place + (first_token + number * span).astype(jnp.float32)
        q = both(q_ref)
        lowest = jnp.min(start).astype(jnp.int32) - first_token
        top_ref[...] = jnp.full_like(top_ref, NEGATIVE_FILL)
        sum_ref[...] = jnp.zeros_like(sum_ref)
        acc_ref[...] = jnp.zeros_like(acc_ref)

        def score(j, _):
            at = pl.ds(pl.multiple_of(j * span, span), span)
            scores = across(q, keys_ref[at, :])
            key = key_place + (first_token + j * span).astype(jnp.float32)
            allowed = jnp.logical_and(key <= query, key >= start)
            scores = jnp.where(allowed, scores, NEGATIVE_FILL)
            scores_ref[:, at] = scores
            top_ref[...] = functools.reduce(jnp.maximum, lane_parts(scores), top_ref[...])
            return 0

        lax.fori_loop(lowest // span, number + 1, score, 0)
        top = jnp.max(top_ref[...], axis=1, keepdims=True)

        def weigh(j, _):
            at = pl.ds(pl.multiple_of(j * span, span), span)
            weights = jnp.exp(scores_ref[:, at] - top)
            sum_ref[...] = functools.reduce(jnp.add, lane_parts(weights), sum_ref[...])
            acc_ref[...] = acc_ref[...] + rank_product(weights.astype(jnp.bfloat16), values_ref[at, :])
            return 0

        lax.fori_loop(lowest // span, number + 1, weigh, 0)
        total = jnp.sum(sum_ref[...], axis=1, keepdims=True)
        attended = (acc_ref[...] / total).astype(jnp.bfloat16)
        lanes = folded(rank_product(attended, left_ref[...]), meta[:, 64:65], spread_ref)
        for k in range(4):
            attended_ref[slots[k], :] = attended[k * pair : (k + 1) * pair]
            at = pl.ds(pl.multiple_of((4 * block + k) * pair, pair), pair)
            fold_ref[:, at] = swap_halves(info, lanes[:, k * pair : (k + 1) * pair])
        return 0

    lax.fori_loop(0, BLOCKS // 2, one, 0)
    out_ref[...] = (fold_ref[...] + hidden_rank_ref[...].astype(jnp.float32)).astype(out_ref.dtype)


def main_kernel(block, attended_ref, hidden_ref, output_ref, down_ref, kept_ref, sent_ref):
    rows = 256
    sent = sent_ref.shape[0]
    width = 512
    attended = attended_ref[block * rows : (block + 1) * rows, :]
    hidden = hidden_ref[block * rows : (block + 1) * rows, :]

    for step in range(output_ref.shape[1] // width):
        at = slice(step * width, (step + 1) * width)
        total = rank_product(attended, output_ref[:, at]) + rank_product(hidden, down_ref[:, at])
        if block:
            sent_ref[:, at] = total[:sent].astype(sent_ref.dtype)
            kept_ref[:, at] = total[sent:]
        else:
            kept_ref[:, at] = total[: rows - sent]
            sent_ref[:, at] = total[rows - sent :].astype(sent_ref.dtype)


def adapt_kernel(slot, first, info, rank_ref, meta_ref, spread_ref, right_ref, kept_ref, arrived_ref, *out_refs):
    pair = 128
    half = pair // 2
    columns = spread_ref.shape[1]
    count = columns // (4 * ADAPTER_RANK)
    column_id = lax.broadcasted_iota(jnp.int32, (pair, columns), 1) // (2 * ADAPTER_RANK)
    partner = info[MLP] + 1 - 2 * info[CORE]
    column_id = column_id + jnp.where(column_id < count, info[MLP] * count, (partner - 1) * count)
    own = column_id.astype(jnp.float32) == meta_ref[slot * pair : (slot + 1) * pair, 64:65]
    spread = rank_product(rank_rows(info, rank_ref, slot, 1), spread_ref[...])
    wide = jnp.where(own, spread, 0.0).astype(jnp.bfloat16)
    width = 512

    for step in range(right_ref.shape[1] // width):
        at = slice(step * width, (step + 1) * width)
        if len(out_refs) == 1:
            total = rank_product(wide[:half], right_ref[:, at]) + kept_ref[first : first + half, at]
            total = total + arrived_ref[:, at].astype(jnp.float32)
            out_refs[0][:, at] = total.astype(out_refs[0].dtype)
        else:
            total = rank_product(wide, right_ref[:, at]) + kept_ref[:, at]
            out_refs[0][:, at] = total[:half] + arrived_ref[half:, at].astype(jnp.float32)
            out_refs[1][:, at] = total[half:] + arrived_ref[:half, at].astype(jnp.float32)


def call(kernel, operands, outs, info=None, scratch=(), mib=24, flops=1000, space=pltpu.VMEM, in_hbm=0):
    vmem = pl.BlockSpec(memory_space=pltpu.VMEM)
    specs = [pl.BlockSpec(memory_space=space)] * (len(operands) - in_hbm)
    specs += [pl.BlockSpec(memory_space=pltpu.HBM)] * in_hbm
    if info is not None:
        operands, specs = [info] + operands, [pl.BlockSpec(memory_space=pltpu.SMEM)] + specs
    return pl.pallas_call(
        kernel,
        in_specs=specs,
        out_specs=[vmem] * len(outs),
        out_shape=outs,
        scratch_shapes=scratch,
        compiler_params=pltpu.CompilerParams(vmem_limit_bytes=mib * 1024 * 1024),
        cost_estimate=pl.CostEstimate(flops=flops, bytes_accessed=1000, transcendentals=0),
    )(*operands)


def shape(rows, width, dtype=jnp.bfloat16):
    return jax.ShapeDtypeStruct((rows, width), dtype)


def sum_over_mlp(value, bits):
    for bit in bits:
        value = value + lax.ppermute(value, "mlp", [(i, i ^ bit) for i in range(16)])
    return value


def narrow(value):
    return value.astype(jnp.bfloat16)


def wide(value):
    return value.astype(jnp.float32)


def per_device(
    tokens,
    layer_norm_gain,
    layer_norm_bias,
    query_key_weight,
    output_weight,
    up_weight,
    input_bias,
    down_weight,
    output_bias,
    input_adapter_left,
    query_key_value_right,
    up_adapter_right,
    output_adapter_left,
    down_adapter_left,
    output_adapter_right,
    lengths,
    request_adapter,
    slot_adapter,
):
    block = tokens.shape[0]
    model_width = tokens.shape[1]
    pair_rows = 2 * block
    group_rows = SLOTS * pair_rows
    req_count = lax.axis_size("req")
    group = lax.axis_index("req")
    me = lax.axis_index("mlp")
    block_rows = 2 * pair_rows
    table = np.zeros((req_count, 16, 2 + SLOTS * (2 + req_count)), np.int32)
    for g in range(req_count):
        for m in range(16):
            side = 2 * (m % 2) - 1
            steps = [0, 4] + [t for s in (1, 2, 3) for t in (side * s, -side * s)]
            pairs = [RING[(PLACE[m // 2] + t) % 8] for t in steps]
            firsts = [(g - d) * group_rows + p * pair_rows for d in range(req_count) for p in pairs]
            table[g, m] = [m % 2, m] + pairs + [pairs.index(p) for p in range(SLOTS)] + firsts
    info = lax.dynamic_slice(jnp.asarray(table), (group, me, 0), (1, 1, table.shape[2])).reshape(-1)

    norm_args = [tokens, layer_norm_gain.reshape(1, -1), layer_norm_bias.reshape(1, -1)]
    norm_args = [pltpu.with_memory_space_constraint(x, pltpu.HBM) for x in norm_args]
    own = call(
        norm_kernel,
        norm_args,
        [shape(block, model_width)],
        scratch=[pltpu.VMEM(x.shape, x.dtype) for x in norm_args] + [pltpu.SemaphoreType.DMA((3,))],
        space=pltpu.HBM,
    )[0]
    other = to_partner(own)
    ring_a, ring_b = along_ring(own), along_ring(other)
    near_left, far_left = input_adapter_left, to_partner(input_adapter_left)

    float_lengths = wide(lengths)
    lane = np.arange(128)
    turn_rows = np.zeros((8, 128), np.float32)
    turn_rows[0] = np.exp(lane % ROT // 2 * (-2.0 * math.log(10000.0) / ROT))
    turn_rows[1] = np.where(lane < ROT, 0.0, math.pi / 2)
    turn_rows[2] = np.where(lane < ROT, 1.0, np.where(lane % 2 == 0, -1.0, 1.0))
    token_rows = req_count * group_rows
    token_args = [
        float_lengths[:, None],
        float_lengths[None, :],
        wide(request_adapter)[None, :],
        jnp.asarray(turn_rows),
    ]
    weights = [query_key_weight.reshape(model_width, 3 * HEAD_SIZE), up_weight]
    weights = [pltpu.with_memory_space_constraint(x, pltpu.HBM) for x in weights]
    meta, turns, qkv_rows, up_rows = call(
        token_kernel,
        token_args + weights,
        [shape(token_rows, 128, jnp.float32)] * 2 + [shape(*x.shape) for x in weights],
        info,
        [pltpu.SemaphoreType.DMA((8,))],
        in_hbm=2,
    )

    adapter_columns = query_key_value_right.shape[0]
    qkv_right = query_key_value_right.reshape(adapter_columns, 3 * HEAD_SIZE)
    spread_first = spread_table(ADAPTER_RANK, 0, 128)
    spread_last = spread_table(ADAPTER_RANK, ADAPTER_RANK, 128)
    near_right = output_adapter_right
    slot_columns = wide(jnp.repeat(slot_adapter, 2 * ADAPTER_RANK))[None, :]
    slot_columns = jnp.concatenate([slot_columns, to_partner(slot_columns)], axis=1)
    own_columns = near_right.shape[0]
    spread_own = spread_table(2 * ADAPTER_RANK, 0, 2 * own_columns)
    hidden_width = up_weight.shape[1]

    def to_group(value, d):
        return lax.ppermute(value, "req", [(g, g + d) for g in range(req_count - d)])

    held = functools.partial(pltpu.VMEM, dtype=jnp.float32)

    def add_ranks(part, slots, so_far):
        return call(
            functools.partial(rank_kernel, len(part), slots),
            list(part) + [pair_left, meta, slot_columns, spread_own, so_far],
            [shape(32, group_rows)],
            info,
        )[0]

    def products_of(part, flops=1000):
        rows = len(part) * block
        return call(
            functools.partial(base_kernel, len(part)),
            list(part) + [qkv_rows, up_rows],
            [
                shape(rows, 3 * HEAD_SIZE, jnp.float32),
                shape(rows, hidden_width, jnp.float32),
                shape(rows, 2 * HEAD_SIZE),
            ],
            flops=flops,
        )

    def to_groups(value):
        return [to_group(value, d) for d in range(1, req_count)]

    def arrivals(a, b):
        return a, b, to_partner(b), to_partner(a)

    tie = lax.optimization_barrier
    own_part = (own, other)
    ring_a, meta, turns, qkv_rows, up_rows = tie((ring_a, meta, turns, qkv_rows, up_rows))
    ring_b, near_left, far_left = tie((ring_b, near_left, far_left))
    pair_left = jnp.concatenate([near_left, far_left], axis=1)
    part = arrivals(ring_a, ring_b)
    ring_a, ring_b = along_ring(ring_a), along_ring(ring_b)
    ranks = add_ranks(own_part + part, (0, 2, 3), jnp.zeros((32, group_rows), jnp.bfloat16))
    zeroth = products_of(own_part)
    ring_a, zeroth = tie((ring_a, zeroth))
    far_own = to_groups(zeroth[2])
    first = products_of(part)
    ring_b, ranks, first, far_own = tie((ring_b, ranks, first, far_own))
    part = arrivals(ring_a, ring_b)
    ring_a, ring_b = along_ring(ring_a), along_ring(ring_b)
    far_right = to_partner(near_right)
    far_early = to_groups(first[2])
    ranks = add_ranks(part, (4, 5), ranks)
    second = products_of(part)
    ring_b, ranks, second, far_right = tie((ring_b, ranks, second, far_right))
    part = arrivals(ring_a, ring_b)
    ring_a = along_ring(ring_a)
    held_rows = part[:2]
    third = products_of(held_rows, 2000000000)
    ranks = add_ranks(held_rows, (6,), ranks)
    ring_a, ranks, third, far_early = tie((ring_a, ranks, third, far_early))
    fourth = products_of(part[2:])
    swapped, fourth = tie((to_partner(ring_a), fourth))
    opposite = (ring_a, swapped)
    ranks = add_ranks(part[2:] + opposite, (7, 1), ranks)
    moved = lax.ppermute(ranks, "mlp", [(i, i ^ 2) for i in range(16)])
    fifth = products_of(opposite)
    ranks, fifth = tie((ranks + moved, fifth))
    far_late = to_groups(jnp.concatenate([second[2], third[2], fourth[2], fifth[2]], axis=0))
    rank_in = sum_over_mlp(ranks, (4, 8))
    products = (zeroth, first, second, third, fourth, fifth)

    bias_row = input_bias.reshape(1, -1)
    far_rank = to_groups(rank_in)
    queries, own_keys, own_values, hidden, hidden_rank = call(
        inner_kernel,
        [part[0] for part in products]
        + [part[1] for part in products]
        + [rank_in, meta, turns, spread_first, spread_last]
        + [qkv_right, up_adapter_right, bias_row, down_adapter_left],
        [shape(group_rows, HEAD_SIZE)] * 3 + [shape(group_rows, hidden_width), shape(32, group_rows)],
        info,
    )
    keys, values = [own_keys], [own_values]
    for d in range(1, req_count):
        early, late = far_early[d - 1], far_late[d - 1]
        ends = (0, block_rows, block_rows + pair_rows, 2 * block_rows, 2 * block_rows + pair_rows)
        shared = [far_own[d - 1], early] + [late[ends[k] : ends[k + 1]] for k in range(4)]
        far_keys, far_values = call(
            functools.partial(far_kernel, d * group_rows),
            shared + [far_rank[d - 1], meta, turns, spread_first, qkv_right],
            [shape(group_rows, HEAD_SIZE)] * 2,
            info,
        )
        keys.append(far_keys)
        values.append(far_values)

    output_left = output_adapter_left.reshape(HEAD_SIZE, adapter_columns)
    attended, rank_out = call(
        functools.partial(attention_kernel, req_count),
        [queries] + keys + values + [meta, spread_first, output_left, hidden_rank],
        [shape(group_rows, HEAD_SIZE), shape(32, group_rows)],
        info,
        [
            pltpu.VMEM((req_count * group_rows, HEAD_SIZE), jnp.bfloat16),
            pltpu.VMEM((req_count * group_rows, HEAD_SIZE), jnp.bfloat16),
            held((2 * block_rows, req_count * group_rows)),
            held((2 * block_rows, 128)),
            held((2 * block_rows, 128)),
            held((2 * block_rows, HEAD_SIZE)),
            held((32, group_rows)),
        ],
        mib=24 + 3 * req_count,
    )
    output_rows = output_weight.reshape(HEAD_SIZE, model_width)

    def main(k, attended, hidden):
        sent = block if k == 0 else pair_rows
        return call(
            functools.partial(main_kernel, k),
            [attended, hidden, output_rows, down_weight],
            [shape(block_rows - sent, model_width, jnp.float32), shape(sent, model_width)],
        )

    kept, arrived, sent = {}, {}, {}
    for bit, k in zip((1, 2, 4, 8), (0, 3, 2, 1)):
        moved = lax.ppermute(rank_out, "mlp", [(i, i ^ bit) for i in range(16)])
        kept[k], sent[k] = main(k, attended, hidden)
        rank_out, attended, kept[k], sent[k] = tie((rank_out + moved, attended, kept[k], sent[k]))
        if k == 0:
            arrived[k] = to_partner(sent[k])
        if bit == 4:
            arrived[3] = to_partner(sent[3])
            rank_out, arrived[0] = tie((rank_out, arrived[0]))
    rank_out, arrived[3] = tie((rank_out, arrived[3]))
    pair_right = jnp.concatenate([near_right, far_right], axis=0)

    def adapt(slot, half, kept, first, arrived):
        if half:
            outs = [shape(block, model_width, jnp.bfloat16 if slot else jnp.float32)]
        else:
            outs = [shape(block, model_width, jnp.float32)] * 2
        return call(
            functools.partial(adapt_kernel, slot, first),
            [rank_out, meta, spread_own, pair_right, kept, arrived],
            outs,
            info,
        )

    chain_a = along_ring(adapt(1, True, kept[0], 2 * block, arrived[0])[0])
    chain_b = None
    for s in (3, 2, 1):
        add_a, add_b = adapt(2 * s + 1, False, kept[s], 0, arrived[s])
        if s > 1:
            arrived[s - 1] = to_partner(sent[s - 1])
        if chain_b is None:
            chain_b = along_ring(narrow(add_b))
            chain_a = along_ring(narrow(wide(chain_a) + add_a))
        else:
            chain_a = along_ring(narrow(wide(chain_a) + add_a))
            chain_b = along_ring(narrow(wide(chain_b) + add_b))
    own_sum = adapt(0, True, kept[0], 0, tokens)[0]
    chain_a, own_sum = tie((chain_a, own_sum))
    arrived_last = to_partner(narrow(wide(chain_b) + kept[0][block : 2 * block]))
    return narrow(wide(chain_a) + wide(arrived_last) + own_sum + output_bias)


def solution(mesh):
    in_specs = (
        P(("req", "mlp"), None),
        P(),
        P(),
        P(None, "mlp", None),
        P("mlp", None, None),
        P(None, "mlp"),
        P("mlp"),
        P("mlp", None),
        P(),
        P(None, "mlp"),
        P(None, "mlp", None),
        P(None, "mlp"),
        P("mlp", None, None),
        P("mlp", None),
        P("mlp", None),
        P(),
        P(),
        P("mlp"),
    )
    out_specs = P(("req", "mlp"), None)
    return jax.shard_map(
        per_device, mesh=mesh, in_specs=in_specs, out_specs=out_specs, check_vma=False
    )
```
